256 devices in a mesh: ctx: 32 (over y, z), head: 8 (over x, core).
Axes of the slice: x: 4, y: 4, z: 8, core: 2. Of those that a mesh axis runs over, the one named last changes fastest.
Arguments:
- queries: bfloat16 [16384, 4096], P('ctx', 'head'), may hold values from -48 to 48
- key_rows: bfloat16 [16384, 1024], P('ctx', 'head'), may hold values from -48 to 48
- value_rows: bfloat16 [16384, 1024], P('ctx', 'head'), may hold values from -6 to 6
- kept_positions: int32 [8, 8192], P('head', 'ctx'), may hold values from 0 to 511, as said below
- anchor_length: int32 [8], P('head'), may hold values from 128 to 512
- output_weight: bfloat16 [4096, 4096], P('head'), may hold values from -0.125 to 0.125
Outputs:
- layer_output: bfloat16 [16384, 4096], P('ctx', 'head')
The draws below stay inside these ranges and needn't reach their ends.
Inputs may be any that keep to these rules, and one draw needn't show every extreme that they name: `kept_positions`: for each key-value head and block, 256 distinct positions of that block.
All inputs are finite; a program needn't handle non-finite values.
Results may differ from the reference program's by a relative error of at most 0.02.
Values may be sent and summed in bfloat16 or wider, within the bound.
No kernel may reach another device: no remote copies, remote signals or barrier semaphores. Data moves between devices by JAX's collectives and lax.ppermute only.
A program may use at most 192 MiB of HBM per device.

```python
import jax
import jax.numpy as jnp
from jax import lax

KVH = 8
HD = 128
GROUP = 4
BLOCK = 512
ANCHOR = 512
KEEP = 256
QH = 32
D = 4096
TOKENS = 16384
PASS = 8192
N_CTX = 32
N_HEAD = 8


def common_keys(key):
    return jax.random.normal(key, (TOKENS, KVH * HD), jnp.float32)


def draw_key_rows(key, part):
    base = common_keys(key)
    return base.astype(jnp.bfloat16)


def draw_queries(key, part):
    key = jax.random.fold_in(key, 5)
    fresh = jax.random.normal(key, (TOKENS, QH * HD), jnp.float32)
    return fresh.astype(jnp.bfloat16)


def draw_kept_positions(key, part):
    key = jax.random.fold_in(key, 11)
    blocks = TOKENS // BLOCK
    several = jax.random.split(key, KVH * blocks)
    chosen = jax.vmap(lambda single: jax.random.permutation(single, BLOCK)[:KEEP])(several)
    return chosen.reshape(KVH, blocks * KEEP).astype(jnp.int32)


def set_ends(values, stream_key, low, high):
    index_at = [jax.random.randint(jax.random.fold_in(stream_key, axis), (), 0, length) for axis, length in enumerate(values.shape)]
    main_axis = values.shape.index(max(values.shape))
    neighbour = index_at[:main_axis] + [(index_at[main_axis] + 1) % values.shape[main_axis]] + index_at[main_axis + 1:]
    return values.at[tuple(index_at)].set(low).at[tuple(neighbour)].set(high)


def raised(array, own_key, source, target, parts, factor):
    owner, partner = [(jnp.arange(array.shape[dim]) // (array.shape[dim] // parts)).reshape([-1 if axis == dim else 1 for axis in range(array.ndim)]) for dim in (source, target)]
    chosen = jax.random.permutation(own_key, parts)[partner]
    strong = (owner == chosen) | (owner == (partner + parts // 2) % parts)
    return jnp.where(strong, factor * array, array)


def shard_levels(stream_key, shape, shards, low, top_value):
    factor_of = 1.0
    for axis_at, blocks in shards:
        heights = jax.random.uniform(jax.random.fold_in(jax.random.fold_in(stream_key, 6), axis_at), (blocks,), jnp.float32, low / len(shards), top_value / len(shards))
        factor_of = factor_of * jnp.repeat(jnp.exp(heights), shape[axis_at] // blocks).reshape((-1,) + (1,) * (len(shape) - 1 - axis_at))
    return factor_of


def scatter_about(rng, dims, deviation, reach, cuts=(), kind=jnp.bfloat16):
    factor_of = shard_levels(rng, dims, cuts, -0.22, 0.18) if cuts else 1.0
    drawn = jax.random.normal(rng, dims, jnp.float32) * deviation * factor_of
    return jnp.minimum(jnp.maximum(drawn, -reach), reach).astype(kind)


def noise_with(rng, dims, spread, reach, shards, heavy, dtype=jnp.bfloat16):
    entries = spread * jax.random.normal(rng, dims, jnp.float32)
    if shards:
        entries = entries * shard_levels(rng, dims, shards, -0.22, 0.18)
    return jnp.clip(raised(entries, jax.random.fold_in(rng, 3), *heavy), -reach, reach).astype(dtype)


def setup_inputs(seed: int = 0) -> dict:
    splits = jax.random.split(jax.random.key(seed), 7)
    queries = draw_queries(jax.random.fold_in(splits[6], 71), 0)
    key_rows = draw_key_rows(jax.random.fold_in(splits[6], 71), 0)
    value_rows = scatter_about(splits[2], (TOKENS, KVH * HD), 1.0, 6.0, ((0, 32), (1, 8)))
    kept_positions = draw_kept_positions(jax.random.fold_in(splits[6], 71), 0)
    anchor_length = set_ends(jax.random.randint(splits[4], (KVH,), ANCHOR // 4, ANCHOR + 1), jax.random.fold_in(splits[4], 1), ANCHOR // 4, ANCHOR).astype(jnp.int32)
    output_weight = noise_with(splits[5], (D, D), D ** -0.5, 0.125, ((0, 8),), (0, 1, 8, 2.0))
    return dict(queries=queries, key_rows=key_rows, value_rows=value_rows, kept_positions=kept_positions, anchor_length=anchor_length, output_weight=output_weight)


NEGATIVE = -1e30


def reference(queries, key_rows, value_rows, kept_positions, anchor_length, output_weight):
    key_three = key_rows.reshape(TOKENS, KVH, HD)
    val_three = value_rows.reshape(TOKENS, KVH, HD)
    starts = (jnp.arange(PASS) // KEEP * BLOCK).astype(jnp.int32)
    picked = starts[None, :] + kept_positions
    selector = jnp.arange(KVH)[:, None]
    kept_keys = key_three[picked, selector]
    kept_vals = val_three[picked, selector]
    anchor_keys = key_three[:ANCHOR].transpose(1, 0, 2)
    anchor_vals = val_three[:ANCHOR].transpose(1, 0, 2)
    owner = jnp.arange(PASS) // KEEP
    scale = HD ** -0.5

    def per_block(block_id):
        first = (block_id * BLOCK).astype(jnp.int32)
        query_block = lax.dynamic_slice_in_dim(queries, first, BLOCK, 0).reshape(BLOCK, KVH, GROUP, HD)
        key_block = lax.dynamic_slice_in_dim(key_three, first, BLOCK, 0)
        val_block = lax.dynamic_slice_in_dim(val_three, first, BLOCK, 0)
        passing_ok = owner < block_id
        local_ok = jnp.arange(BLOCK)[None, :] <= jnp.arange(BLOCK)[:, None]

        def per_head(head_id):
            anchor_ok = (jnp.arange(ANCHOR) < anchor_length[head_id]) & (block_id > 0)
            allowed = jnp.concatenate([
                jnp.broadcast_to(anchor_ok[None, :], (BLOCK, ANCHOR)),
                jnp.broadcast_to(passing_ok[None, :], (BLOCK, PASS)),
                local_ok], axis=1)
            every_key = jnp.concatenate([anchor_keys[head_id], kept_keys[head_id], key_block[:, head_id]], axis=0)
            every_val = jnp.concatenate([anchor_vals[head_id], kept_vals[head_id], val_block[:, head_id]], axis=0)
            scores = jnp.einsum("qgd,kd->gqk", query_block[:, head_id].astype(jnp.float32), every_key.astype(jnp.float32)) * scale
            scores = jnp.where(allowed[None], scores, NEGATIVE)
            peak = jnp.max(scores, axis=-1)
            weights = jnp.where(allowed[None], jnp.exp(scores - peak[..., None]), 0.0)
            total = jnp.sum(weights, axis=-1)
            mixed = jnp.einsum("gqk,kd->gqd", weights.astype(jnp.bfloat16).astype(jnp.float32), every_val.astype(jnp.float32))
            return (mixed / total[..., None]).transpose(1, 0, 2)

        result = lax.map(per_head, jnp.arange(KVH))
        return result.transpose(1, 0, 2, 3).reshape(BLOCK, QH * HD)

    attention = lax.map(per_block, jnp.arange(N_CTX)).reshape(TOKENS, QH * HD).astype(jnp.bfloat16)
    columns = QH * HD // N_HEAD
    summed = jnp.zeros((TOKENS, D), jnp.float32)
    for group_id in range(N_HEAD):
        partial_value = jnp.dot(attention[:, group_id * columns:(group_id + 1) * columns],
                          output_weight[group_id * columns:(group_id + 1) * columns],
                          preferred_element_type=jnp.float32).astype(jnp.bfloat16)
        summed = summed + partial_value.astype(jnp.float32)
    return summed.astype(jnp.bfloat16)
```

```python
import jax
import jax.numpy as jnp
from jax import lax
from jax.experimental import pallas as pl
from jax.experimental.pallas import tpu as pltpu
from jax.sharding import PartitionSpec as P

HEAD = 128
LOG2E = 1.4426950408889634
LIMIT = 2.0**100
NEGATIVE = -1e30
NT = (((1,), (1,)), ((), ()))
TN = (((0,), (0,)), ((), ()))


def select_kernel(kept_ref, key_ref, value_ref, out_ref):
    length, keep = key_ref.shape[0], kept_ref.shape[1]
    rows = lax.broadcasted_iota(jnp.int32, (length, keep), 0)
    chosen = jnp.where(rows == kept_ref[...], 1.0, 0.0).astype(jnp.bfloat16)
    for at, ref in enumerate((key_ref, value_ref)):
        out_ref[:, at * HEAD : (at + 1) * HEAD] = lax.dot_general(
            chosen, ref[...], TN, preferred_element_type=jnp.float32
        ).astype(jnp.bfloat16)


def select(kept, keys, values):
    return pl.pallas_call(
        select_kernel,
        out_shape=jax.ShapeDtypeStruct((kept.shape[1], 2 * HEAD), jnp.bfloat16),
        name="select_kept",
    )(kept, keys, values)


def attend_kernel(
    place_ref, q_ref, k_ref, v_ref, anchor_ref, kept_ref, w_ref, out_ref, acc_ref, peak_ref, att_ref
):
    mine, used = place_ref[0], place_ref[1]
    length, heads = q_ref.shape[0], q_ref.shape[1] // HEAD
    keep = kept_ref.shape[1]
    factor = HEAD**-0.5 * LOG2E

    def query(h):
        return q_ref[:, pl.ds(pl.multiple_of(h * HEAD, HEAD), HEAD)]

    def scores(h, keys):
        return lax.dot_general(query(h), keys, NT, preferred_element_type=jnp.float32) * factor

    def widened(values):
        return jnp.concatenate([values, jnp.ones_like(values)], axis=1)

    def wide(column, width):
        return jnp.concatenate([column] * (width // HEAD), axis=1)

    def product(weights, values):
        return jnp.dot(weights, values, preferred_element_type=jnp.float32)

    def causal():
        shape = (length, length)
        return lax.broadcasted_iota(jnp.int32, shape, 1) <= lax.broadcasted_iota(jnp.int32, shape, 0)

    def in_use():
        return lax.broadcasted_iota(jnp.int32, (length, anchor_ref.shape[0]), 1) < used

    def first(h):
        raw = jnp.where(causal(), scores(h, k_ref[...]), NEGATIVE)
        peak = jnp.broadcast_to(jnp.max(raw, axis=1, keepdims=True), (length, HEAD))
        peak_ref[h] = peak
        weights = jnp.exp2(raw - wide(peak, length)).astype(jnp.bfloat16)
        acc_ref[h] = product(weights, widened(v_ref[...]))

    def fixed(h, keys, values, allowed=None):
        raw = scores(h, keys)
        weights = jnp.exp2(raw - wide(peak_ref[h], keys.shape[0]))
        if allowed is not None:
            weights = jnp.where(allowed, weights, 0.0)
        acc_ref[h] += product(weights.astype(jnp.bfloat16), values)

    def moving(h, keys, values, allowed=None):
        raw = scores(h, keys)
        if allowed is not None:
            raw = jnp.where(allowed, raw, NEGATIVE)
        old = peak_ref[h]
        peak = jnp.maximum(old, jnp.max(raw, axis=1, keepdims=True))
        weights = jnp.exp2(raw - wide(peak, keys.shape[0]))
        if allowed is not None:
            weights = jnp.where(allowed, weights, 0.0)
        peak_ref[h] = peak
        acc_ref[h] = acc_ref[h] * wide(jnp.exp2(old - peak), 2 * HEAD) + product(
            weights.astype(jnp.bfloat16), values
        )

    def group(start, blocks):
        both = kept_ref[pl.ds(start, blocks)].reshape(blocks * keep, 2 * HEAD)
        return both[:, :HEAD], widened(both[:, HEAD:])

    for h in range(heads):
        first(h)

    @pl.when(mine > 0)
    def _():
        values = widened(anchor_ref[:, HEAD:])
        for h in range(heads):
            fixed(h, anchor_ref[:, :HEAD], values, in_use())

    @pl.loop(0, mine // 2)
    def _(pair):
        keys, values = group(pair * 2, 2)
        for h in range(heads):
            fixed(h, keys, values)

    @pl.when(mine % 2 == 1)
    def _():
        keys, values = group(mine - 1, 1)
        for h in range(heads):
            fixed(h, keys, values)

    largest = jnp.max(acc_ref[:, :, HEAD:])

    @pl.when(jnp.logical_not(largest < LIMIT))
    def _():
        @pl.loop(0, heads)
        def _(h):
            first(h)

            @pl.when(mine > 0)
            def _():
                moving(h, anchor_ref[:, :HEAD], widened(anchor_ref[:, HEAD:]), in_use())

            @pl.loop(0, mine)
            def _(block):
                moving(h, *group(block, 1))

    for h in range(heads):
        att_ref[:, h * HEAD : (h + 1) * HEAD] = (
            acc_ref[h, :, :HEAD] / acc_ref[h, :, HEAD:]
        ).astype(jnp.bfloat16)

    @pl.loop(0, out_ref.shape[1] // 512)
    def _(tile):
        columns = pl.ds(pl.multiple_of(tile * 512, 512), 512)
        out_ref[:, columns] = product(att_ref[...], w_ref[:, columns]).astype(jnp.bfloat16)


def attend(place, queries, keys, values, anchor, kept, weight):
    length, width = queries.shape
    heads = width // HEAD
    vmem = pl.BlockSpec(memory_space=pltpu.VMEM)
    return pl.pallas_call(
        attend_kernel,
        out_shape=jax.ShapeDtypeStruct((length, weight.shape[1]), jnp.bfloat16),
        in_specs=[pl.BlockSpec(memory_space=pltpu.SMEM)] + [vmem] * 6,
        out_specs=vmem,
        scratch_shapes=[
            pltpu.VMEM((heads, length, 2 * HEAD), jnp.float32),
            pltpu.VMEM((heads, length, HEAD), jnp.float32),
            pltpu.VMEM((length, width), jnp.bfloat16),
        ],
        compiler_params=pltpu.CompilerParams(vmem_limit_bytes=48 * 2**20),
        name="attend",
    )(place, queries, keys, values, anchor, kept, weight)


def from_first(block, axis):
    me, count = lax.axis_index(axis), lax.axis_size(axis)
    block = jnp.where(me == 0, block, jnp.zeros_like(block))
    step = count // 2
    have = [0]
    while step:
        block = block + lax.ppermute(block, axis, [(i, i + step) for i in have])
        have += [i + step for i in have]
        step //= 2
    return block


def on_device(queries, key_rows, value_rows, kept_positions, anchor_length, output_weight):
    mine = lax.axis_index("ctx")
    kept = lax.all_gather(select(kept_positions, key_rows, value_rows), "ctx")
    anchor = from_first(jnp.concatenate([key_rows, value_rows], axis=1), "ctx")
    place = jnp.concatenate([mine.astype(jnp.int32)[None], anchor_length])
    partial_value = attend(place, queries, key_rows, value_rows, anchor, kept, output_weight)
    return lax.psum_scatter(partial_value, "head", scatter_dimension=1, tiled=True)


def solution(mesh):
    placed = (
        P("ctx", "head"),
        P("ctx", "head"),
        P("ctx", "head"),
        P("head", "ctx"),
        P("head"),
        P("head", None),
    )
    return jax.shard_map(
        on_device, mesh=mesh, in_specs=placed, out_specs=P("ctx", "head"), check_vma=False
    )
```

```python
import jax
import jax.numpy as jnp
from jax import lax
from jax.experimental import pallas as pl
from jax.experimental.pallas import tpu as pltpu
from jax.sharding import PartitionSpec as P

HEAD = 128
LOG2E = 1.4426950408889634
LIMIT = 2.0**100
NEGATIVE = -1e30
NT = (((1,), (1,)), ((), ()))
TN = (((0,), (0,)), ((), ()))


def select_kernel(kept_ref, key_ref, value_ref, out_ref):
    length, keep = key_ref.shape[0], kept_ref.shape[1]
    rows = lax.broadcasted_iota(jnp.int32, (length, keep), 0)
    chosen = jnp.where(rows == kept_ref[...], 1.0, 0.0).astype(jnp.bfloat16)
    for at, ref in enumerate((key_ref, value_ref)):
        out_ref[:, at * HEAD : (at + 1) * HEAD] = lax.dot_general(
            chosen, ref[...], TN, preferred_element_type=jnp.float32
        ).astype(jnp.bfloat16)


def select(kept, keys, values):
    return pl.pallas_call(
        select_kernel,
        out_shape=jax.ShapeDtypeStruct((kept.shape[1], 2 * HEAD), jnp.bfloat16),
        name="select_kept",
    )(kept, keys, values)


def attend_kernel(
    place_ref, q_ref, k_ref, v_ref, anchor_ref, *rest
):
    kept_refs, (out_ref, acc_ref, peak_ref) = rest[:4], rest[4:]
    mine, used = place_ref[0], place_ref[1]
    length, heads = q_ref.shape[0], q_ref.shape[1] // HEAD
    count = kept_refs[0].shape[0]
    factor = HEAD**-0.5 * LOG2E

    def query(h):
        return q_ref[:, pl.ds(pl.multiple_of(h * HEAD, HEAD), HEAD)]

    def scores(h, keys):
        return lax.dot_general(query(h), keys, NT, preferred_element_type=jnp.float32) * factor

    def widened(values):
        return jnp.concatenate([values, jnp.ones_like(values)], axis=1)

    def wide(column, width):
        return jnp.concatenate([column] * (width // HEAD), axis=1)

    def product(weights, values):
        return jnp.dot(weights, values, preferred_element_type=jnp.float32)

    def causal():
        shape = (length, length)
        return lax.broadcasted_iota(jnp.int32, shape, 1) <= lax.broadcasted_iota(jnp.int32, shape, 0)

    def in_use():
        return lax.broadcasted_iota(jnp.int32, (length, anchor_ref.shape[0]), 1) < used

    def first(h):
        raw = jnp.where(causal(), scores(h, k_ref[...]), NEGATIVE)
        peak = jnp.broadcast_to(jnp.max(raw, axis=1, keepdims=True), (length, HEAD))
        peak_ref[h] = peak
        weights = jnp.exp2(raw - wide(peak, length)).astype(jnp.bfloat16)
        acc_ref[h] = product(weights, widened(v_ref[...]))

    def fixed(h, keys, values, allowed=None):
        raw = scores(h, keys)
        weights = jnp.exp2(raw - wide(peak_ref[h], keys.shape[0]))
        if allowed is not None:
            weights = jnp.where(allowed, weights, 0.0)
        acc_ref[h] += product(weights.astype(jnp.bfloat16), values)

    def moving(h, keys, values, allowed=None):
        raw = scores(h, keys)
        if allowed is not None:
            raw = jnp.where(allowed, raw, NEGATIVE)
        old = peak_ref[h]
        peak = jnp.maximum(old, jnp.max(raw, axis=1, keepdims=True))
        weights = jnp.exp2(raw - wide(peak, keys.shape[0]))
        if allowed is not None:
            weights = jnp.where(allowed, weights, 0.0)
        peak_ref[h] = peak
        acc_ref[h] = acc_ref[h] * wide(jnp.exp2(old - peak), 2 * HEAD) + product(
            weights.astype(jnp.bfloat16), values
        )

    def group(start, blocks):
        both = []
        for block in range(blocks):
            for ref, at in zip(kept_refs, ring_places(start + block, count)):
                both.append(ref[at])
        both = jnp.concatenate(both, axis=0)
        return both[:, :HEAD], widened(both[:, HEAD:])

    for h in range(heads):
        first(h)

    @pl.when(mine > 0)
    def _():
        values = widened(anchor_ref[:, HEAD:])
        for h in range(heads):
            fixed(h, anchor_ref[:, :HEAD], values, in_use())

    @pl.loop(0, mine // 2)
    def _(pair):
        keys, values = group(pair * 2, 2)
        for h in range(heads):
            fixed(h, keys, values)

    @pl.when(mine % 2 == 1)
    def _():
        keys, values = group(mine - 1, 1)
        for h in range(heads):
            fixed(h, keys, values)

    largest = jnp.max(acc_ref[:, :, HEAD:])

    @pl.when(jnp.logical_not(largest < LIMIT))
    def _():
        @pl.loop(0, heads)
        def _(h):
            first(h)

            @pl.when(mine > 0)
            def _():
                moving(h, anchor_ref[:, :HEAD], widened(anchor_ref[:, HEAD:]), in_use())

            @pl.loop(0, mine)
            def _(block):
                moving(h, *group(block, 1))

    for h in range(heads):
        out_ref[:, h * HEAD : (h + 1) * HEAD] = (
            acc_ref[h, :, :HEAD] / acc_ref[h, :, HEAD:]
        ).astype(jnp.bfloat16)


def attend(place, queries, keys, values, anchor, kept):
    length, width = queries.shape
    heads = width // HEAD
    vmem = pl.BlockSpec(memory_space=pltpu.VMEM)
    return pl.pallas_call(
        attend_kernel,
        out_shape=jax.ShapeDtypeStruct((length, width), jnp.bfloat16),
        in_specs=[pl.BlockSpec(memory_space=pltpu.SMEM)] + [vmem] * 8,
        out_specs=vmem,
        scratch_shapes=[
            pltpu.VMEM((heads, length, 2 * HEAD), jnp.float32),
            pltpu.VMEM((heads, length, HEAD), jnp.float32),
        ],
        compiler_params=pltpu.CompilerParams(vmem_limit_bytes=48 * 2**20),
        name="attend",
    )(place, queries, keys, values, anchor, *kept)


def project_kernel(place_ref, own_ref, other_ref, own_w_ref, other_w_ref, out_ref):
    chips = out_ref.shape[0]
    for step in range(chips):
        at = lax.rem(place_ref[0] + step, chips)
        total = jnp.dot(own_ref[...], own_w_ref[at], preferred_element_type=jnp.float32)
        total += jnp.dot(other_ref[...], other_w_ref[at], preferred_element_type=jnp.float32)
        out_ref[step] = total.astype(jnp.bfloat16)


def project(place, own, other, own_w, other_w):
    chips, _, columns = own_w.shape
    vmem = pl.BlockSpec(memory_space=pltpu.VMEM)
    return pl.pallas_call(
        project_kernel,
        out_shape=jax.ShapeDtypeStruct((chips, own.shape[0], columns), jnp.bfloat16),
        in_specs=[pl.BlockSpec(memory_space=pltpu.SMEM)] + [vmem] * 4,
        out_specs=vmem,
        compiler_params=pltpu.CompilerParams(vmem_limit_bytes=48 * 2**20),
        name="project",
    )(place, own, other, own_w, other_w)


def ring_orders(count):
    across = [y * 8 + z for z in range(8) for y in range(count // 8)]
    along = list(range(count))
    return along, along[::-1], across, across[::-1]


def ring_places(block, count):
    across = block % 8 * (count // 8) + block // 8
    return block, count - 1 - block, across, count - 1 - across


def from_first(block, axis):
    me, count = lax.axis_index(axis), lax.axis_size(axis)
    block = jnp.where(me == 0, block, jnp.zeros_like(block))
    step = count // 2
    have = [0]
    while step:
        block = block + lax.ppermute(block, axis, [(i, i + step) for i in have])
        have += [i + step for i in have]
        step //= 2
    return block


def added(*terms):
    return sum(term.astype(jnp.float32) for term in terms).astype(jnp.bfloat16)


def on_device(queries, key_rows, value_rows, kept_positions, anchor_length, output_weight):
    mine, head = lax.axis_index("ctx"), lax.axis_index("head")
    length, devices = queries.shape[0], lax.axis_size("head")
    chips, chip, core = devices // 2, head // 2, head % 2
    swap = [(i, i ^ 1) for i in range(devices)]
    up = [(i, (i + 2) % devices) for i in range(devices)]
    down = [(i, (i - 2) % devices) for i in range(devices)]

    retained = select(kept_positions, key_rows, value_rows)
    orders = ring_orders(lax.axis_size("ctx"))
    rows = retained.shape[0] // len(orders)
    kept = [
        lax.all_gather(retained[at * rows : (at + 1) * rows], "ctx", axis_index_groups=[order])
        for at, order in enumerate(orders)
    ]
    anchor = from_first(jnp.concatenate([key_rows, value_rows], axis=1), "ctx")

    weight = output_weight.reshape(output_weight.shape[0], chips, 2, -1).transpose(2, 1, 0, 3)
    own_w = lax.dynamic_index_in_dim(weight, core, 0, keepdims=False)
    other_w = lax.ppermute(lax.dynamic_index_in_dim(weight, 1 - core, 0, keepdims=False), "head", swap)

    place = jnp.concatenate([mine.astype(jnp.int32)[None], anchor_length])
    own = attend(place, queries, key_rows, value_rows, anchor, kept)
    other = lax.ppermute(own, "head", swap)
    parts = project(chip.astype(jnp.int32)[None], own, other, own_w, other_w)

    half = length // 2
    from_below = lax.ppermute(parts[2, :half], "head", up)
    from_above = lax.ppermute(parts[2, half:], "head", down)
    upward = jnp.concatenate([added(parts[1, :half], from_below), parts[1, half:]])
    downward = jnp.concatenate([parts[3, :half], added(parts[3, half:], from_above)])
    return added(
        parts[0], lax.ppermute(upward, "head", up), lax.ppermute(downward, "head", down)
    )


def solution(mesh):
    placed = (
        P("ctx", "head"),
        P("ctx", "head"),
        P("ctx", "head"),
        P("head", "ctx"),
        P("head"),
        P("head", None),
    )
    return jax.shard_map(
        on_device, mesh=mesh, in_specs=placed, out_specs=P("ctx", "head"), check_vma=False
    )
```

```python
import functools

import jax
import jax.numpy as jnp
from jax import lax
from jax.experimental import pallas as pl
from jax.experimental.pallas import tpu as pltpu
from jax.sharding import PartitionSpec as P

HEAD = 128
WIDE = 8
NEAR = 160
INFO = 16
LOG2E = 1.4426950408889634
FACTOR = HEAD**-0.5 * LOG2E
LIMIT = 2.0**100
NEGATIVE = -1e30
NT = (((1,), (1,)), ((), ()))
VMEM = pl.BlockSpec(memory_space=pltpu.VMEM)
SMEM = pl.BlockSpec(memory_space=pltpu.SMEM)
PARAMS = pltpu.CompilerParams(vmem_limit_bytes=48 * 2**20)


def dot(a, b):
    return jnp.dot(a, b, preferred_element_type=jnp.float32)


def dot_nt(a, b):
    return lax.dot_general(a, b, NT, preferred_element_type=jnp.float32)


def count_along(shape, dim):
    return lax.broadcasted_iota(jnp.int32, shape, dim)


def ones_where(condition):
    return jnp.where(condition, 1.0, 0.0).astype(jnp.bfloat16)


def select_kernel(used_ref, kept_ref, key_ref, value_ref, near_ref, far_ref, rest_ref):
    length, keep = key_ref.shape[0], kept_ref.shape[1]
    near = near_ref.shape[0]
    hit = ones_where(count_along((length, keep), 0) == kept_ref[...])
    kept = dot_nt(jnp.ones((8, keep), jnp.bfloat16), hit)
    square = (length, length)
    before = ones_where(count_along(square, 0) < count_along(square, 1))
    rank = dot(kept.astype(jnp.bfloat16), before)
    column = count_along((8, length), 1)
    place = jnp.where(kept > 0.5, rank, column.astype(jnp.float32) + keep - rank)
    order = ones_where(count_along(square, 0).astype(jnp.float32) == place[:1])
    for at, ref in enumerate((key_ref, value_ref)):
        columns = slice(at * HEAD, (at + 1) * HEAD)
        rows = dot(order, ref[...]).astype(jnp.bfloat16)
        near_ref[:, columns] = rows[:near]
        far_ref[:, columns] = rows[near:keep]
        rest_ref[: length - keep, columns] = rows[keep:]
    in_both = jnp.where((kept > 0.5) & (column < used_ref[0]), 1.0, 0.0)[:1]
    number = jnp.sum(in_both, axis=1, keepdims=True)
    rest_ref[length - keep :] = jnp.broadcast_to(number, (INFO, 2 * HEAD)).astype(jnp.bfloat16)


def select(used, kept, keys, values):
    length, keep = keys.shape[0], kept.shape[1]
    rows = (NEAR, keep - NEAR, length - keep + INFO)
    return pl.pallas_call(
        select_kernel,
        out_shape=[jax.ShapeDtypeStruct((n, 2 * HEAD), jnp.bfloat16) for n in rows],
        in_specs=[SMEM, VMEM, VMEM, VMEM],
        out_specs=[VMEM] * 3,
        compiler_params=PARAMS,
        name="select_kept",
    )(used, kept, keys, values)


def wide(column, width):
    return jnp.concatenate([column] * (width // HEAD), axis=1)


def widened(values):
    return jnp.concatenate([values, jnp.ones_like(values)], axis=1)


def scores(q_ref, h, keys):
    query = q_ref[:, pl.ds(pl.multiple_of(h * HEAD, HEAD), HEAD)]
    return dot_nt(query, keys) * FACTOR


def local(q_ref, k_ref, v_ref, acc_ref, peak_ref, h):
    length = q_ref.shape[0]
    causal = count_along((length, length), 1) <= count_along((length, length), 0)
    raw = jnp.where(causal, scores(q_ref, h, k_ref[...]), NEGATIVE)
    peak = jnp.broadcast_to(jnp.max(raw, axis=1, keepdims=True), (length, HEAD))
    peak_ref[h] = peak
    weights = jnp.exp2(raw - wide(peak, length)).astype(jnp.bfloat16)
    acc_ref[h] = dot(weights, widened(v_ref[...]))


def fixed(q_ref, acc_ref, peak_ref, h, keys, values, allowed):
    weights = jnp.exp2(scores(q_ref, h, keys) - wide(peak_ref[h], keys.shape[0]))
    if allowed is not None:
        weights = jnp.where(allowed, weights, 0.0)
    acc_ref[h] += dot(weights.astype(jnp.bfloat16), values)


def moving(q_ref, acc_ref, peak_ref, h, keys, values, allowed):
    raw = scores(q_ref, h, keys)
    if allowed is not None:
        raw = jnp.where(allowed, raw, NEGATIVE)
    old = peak_ref[h]
    peak = jnp.maximum(old, jnp.max(raw, axis=1, keepdims=True))
    weights = jnp.exp2(raw - wide(peak, keys.shape[0]))
    if allowed is not None:
        weights = jnp.where(allowed, weights, 0.0)
    peak_ref[h] = peak
    acc_ref[h] = acc_ref[h] * wide(jnp.exp2(old - peak), 2 * HEAD) + dot(
        weights.astype(jnp.bfloat16), values
    )


def absorb(q_ref, acc_ref, peak_ref, start, tiles):
    heads = acc_ref.shape[0]
    for h in range(heads):
        start(h)
    for condition, read in tiles:

        @pl.when(condition)
        def _():
            keys, values, allowed = read()
            for h in range(heads):
                fixed(q_ref, acc_ref, peak_ref, h, keys, values, allowed)

    largest = jnp.max(acc_ref[:, :, HEAD:])

    @pl.when(jnp.logical_not(largest < LIMIT))
    def _():
        @pl.loop(0, heads)
        def _(h):
            start(h)
            for condition, read in tiles:

                @pl.when(condition)
                def _():
                    moving(q_ref, acc_ref, peak_ref, h, *read())


def split_rows(rows):
    return [(at, min(512, rows - at)) for at in range(0, rows, 512)]


def reader(ref, at, rows, allowed=None):
    def read():
        both = ref[at : at + rows]
        mask = None if allowed is None else allowed(count_along((1, rows), 1) + at)
        return both[:, :HEAD], widened(both[:, HEAD:]), mask

    return read


def whole_tiles(ref, condition, allowed=None):
    return [
        (condition, reader(ref, at, rows, allowed)) for at, rows in split_rows(ref.shape[0])
    ]


def own_row_kernel(place_ref, q_ref, k_ref, v_ref, row_ref, acc_ref, peak_ref):
    z = place_ref[0] % WIDE
    rows = row_ref.shape[0] // WIDE
    first, last = (WIDE - 1 - z) * rows, (WIDE - 1) * rows
    allowed = lambda at: (at >= first) & (at < last)
    start = functools.partial(local, q_ref, k_ref, v_ref, acc_ref, peak_ref)
    absorb(q_ref, acc_ref, peak_ref, start, whole_tiles(row_ref, z > 0, allowed))


def carried(acc_in, peak_in, acc_ref, peak_ref):
    def start(h):
        acc_ref[h] = acc_in[h]
        peak_ref[h] = peak_in[h]

    return start


def rows_kernel(place_ref, q_ref, below_ref, above_ref, acc_in, peak_in, acc_ref, peak_ref):
    y = place_ref[0] // WIDE
    top = place_ref[1] // WIDE - 1
    tiles = whole_tiles(below_ref, y > 0) + whole_tiles(above_ref, y == top)
    absorb(q_ref, acc_ref, peak_ref, carried(acc_in, peak_in, acc_ref, peak_ref), tiles)


def last_kernel(
    place_ref, q_ref, below_ref, above_ref, far_ref, first_ref, rest_ref, acc_in, peak_in,
    out_ref, acc_ref, peak_ref,
):
    mine, used = place_ref[0], place_ref[2]
    y, z = mine // WIDE, mine % WIDE
    tiles = whole_tiles(below_ref, y > 1) + whole_tiles(above_ref, y > 1)

    def far(row, width, allowed=None):
        def read():
            both = jnp.concatenate([far_ref[at, row] for at in range(WIDE)], axis=0)
            mask = None if allowed is None else allowed(count_along((1, both.shape[0]), 1))
            return both[:, :HEAD], widened(both[:, HEAD:]), mask

        return read

    each = far_ref.shape[2]
    for row in range(far_ref.shape[1]):
        tiles.append((y > row, far(row, each)))
        tiles.append(((y == row) & (z > 0), far(row, each, lambda at: at < z * each)))

    keep = rest_ref.shape[0] - INFO

    def anchor():
        both = jnp.concatenate([first_ref[...], far_ref[0, 0], rest_ref[:keep]], axis=0)
        number = rest_ref[keep : keep + 1, :HEAD].astype(jnp.int32)
        number = wide(number, both.shape[0])
        at = count_along((1, both.shape[0]), 1)
        split = first_ref.shape[0] + each
        allowed = at < jnp.where(at < split, number, split + used - number)
        return both[:, :HEAD], widened(both[:, HEAD:]), allowed

    tiles.append((mine > 0, anchor))
    absorb(q_ref, acc_ref, peak_ref, carried(acc_in, peak_in, acc_ref, peak_ref), tiles)
    for h in range(acc_ref.shape[0]):
        out_ref[:, h * HEAD : (h + 1) * HEAD] = (
            acc_ref[h, :, :HEAD] / acc_ref[h, :, HEAD:]
        ).astype(jnp.bfloat16)


def cost(rows, keys):
    return pl.CostEstimate(
        flops=rows * keys * HEAD * 8, bytes_accessed=8 * 2**20, transcendentals=rows * keys
    )


def state_of(length, heads):
    return [
        jax.ShapeDtypeStruct((heads, length, 2 * HEAD), jnp.float32),
        jax.ShapeDtypeStruct((heads, length, HEAD), jnp.float32),
    ]


def own_row(place, queries, keys, values, row):
    length, width = queries.shape
    return pl.pallas_call(
        own_row_kernel,
        out_shape=state_of(length, width // HEAD),
        in_specs=[SMEM] + [VMEM] * 4,
        out_specs=[VMEM] * 2,
        compiler_params=PARAMS,
        cost_estimate=cost(length * width // HEAD, length + row.shape[0]),
        name="own_row",
    )(place, queries, keys, values, row)


def more_rows(place, queries, below, above, state):
    length, width = queries.shape
    return pl.pallas_call(
        rows_kernel,
        out_shape=state_of(length, width // HEAD),
        in_specs=[SMEM] + [VMEM] * 5,
        out_specs=[VMEM] * 2,
        compiler_params=PARAMS,
        cost_estimate=cost(length * width // HEAD, 2 * below.shape[0]),
        name="more_rows",
    )(place, queries, below, above, *state)


def last_rows(place, queries, below, above, far, first, rest, state, part, parts):
    length, width = queries.shape
    rows, heads = length // parts, width // HEAD
    whole = lambda x: pl.BlockSpec(x.shape, lambda i: (0,) * x.ndim)
    slab = lambda columns: pl.BlockSpec((heads, rows, columns), lambda i: (0, part, 0))
    return pl.pallas_call(
        last_kernel,
        grid=(1,),
        out_shape=jax.ShapeDtypeStruct((rows, width), jnp.bfloat16),
        in_specs=[
            SMEM,
            pl.BlockSpec((rows, width), lambda i: (part, 0)),
            *[whole(x) for x in (below, above, far, first, rest)],
            slab(2 * HEAD),
            slab(HEAD),
        ],
        out_specs=pl.BlockSpec((rows, width), lambda i: (0, 0)),
        scratch_shapes=[
            pltpu.VMEM((heads, rows, 2 * HEAD), jnp.float32),
            pltpu.VMEM((heads, rows, HEAD), jnp.float32),
        ],
        compiler_params=PARAMS,
        cost_estimate=cost(rows * heads, 5000),
        name=f"last_rows_{part}",
    )(place, queries, below, above, far, first, rest, *state)


def project_kernel(place_ref, own_ref, other_ref, own_w_ref, other_w_ref, out_ref):
    chips = out_ref.shape[0]
    for step in range(chips):
        at = lax.rem(place_ref[0] + step, chips)
        total = dot(own_ref[...], own_w_ref[at]) + dot(other_ref[...], other_w_ref[at])
        out_ref[step] = total.astype(jnp.bfloat16)


def project(place, own, other, own_w, other_w):
    chips, _, columns = own_w.shape
    return pl.pallas_call(
        project_kernel,
        out_shape=jax.ShapeDtypeStruct((chips, own.shape[0], columns), jnp.bfloat16),
        in_specs=[SMEM] + [VMEM] * 4,
        out_specs=VMEM,
        compiler_params=PARAMS,
        cost_estimate=pl.CostEstimate(
            flops=4 * own.size * chips * columns, bytes_accessed=8 * 2**20, transcendentals=0
        ),
        name="project",
    )(place, own, other, own_w, other_w)


def weight_kernel(place_ref, weight_ref, own_ref, other_ref, sems):
    chips, _, columns = own_ref.shape
    core = place_ref[0]
    copies = []
    for chip in range(chips):
        for at, (ref, side) in enumerate(((own_ref, core), (other_ref, 1 - core))):
            start = pl.multiple_of((2 * chip + side) * columns, columns)
            copies.append(
                pltpu.make_async_copy(
                    weight_ref.at[:, pl.ds(start, columns)], ref.at[chip], sems.at[chip, at]
                )
            )
    for copy in copies:
        copy.start()
    for copy in copies:
        copy.wait()


def weight_halves(core, weight, chips):
    rows, columns = weight.shape
    half = jax.ShapeDtypeStruct((chips, rows, columns // chips // 2), weight.dtype)
    hbm = pl.BlockSpec(memory_space=pl.ANY)
    return pl.pallas_call(
        weight_kernel,
        out_shape=[half, half],
        in_specs=[SMEM, hbm],
        out_specs=[hbm, hbm],
        scratch_shapes=[pltpu.SemaphoreType.DMA((chips, 2))],
        cost_estimate=pl.CostEstimate(flops=0, bytes_accessed=8 * 2**20, transcendentals=0),
        name="weight_halves",
    )(core, weight)


def added(*terms):
    return sum(term.astype(jnp.float32) for term in terms).astype(jnp.bfloat16)


def on_device(queries, key_rows, value_rows, kept_positions, anchor_length, output_weight):
    mine, head = lax.axis_index("ctx"), lax.axis_index("head")
    length, devices, blocks = queries.shape[0], lax.axis_size("head"), lax.axis_size("ctx")
    chips, chip, core = devices // 2, head // 2, head % 2
    tall = blocks // WIDE
    y, z = mine // WIDE, mine % WIDE
    swap = [(i, i ^ 1) for i in range(devices)]
    up = [(i, (i + 2) % devices) for i in range(devices)]
    down = [(i, (i - 2) % devices) for i in range(devices)]
    along = lambda step: [
        (r * WIDE + c, r * WIDE + (c + step) % WIDE) for r in range(tall) for c in range(WIDE)
    ]
    across = lambda hops: [(a * WIDE + c, b * WIDE + c) for a, b in hops for c in range(WIDE)]
    permute = lambda x, pairs: lax.ppermute(x, "ctx", pairs)

    near, far, rest = select(anchor_length, kept_positions, key_rows, value_rows)

    columns = [[r * WIDE + c for r in range(tall)] for c in range(WIDE)]
    rows = [[r * WIDE + c for c in range(WIDE)] for r in range(tall)]
    far = lax.all_gather(far, "ctx", axis_index_groups=columns)
    far = lax.all_gather(far, "ctx", axis_index_groups=rows)

    plus, minus = along(1), along(-1)
    half = NEAR // 2
    left, right = [near], [near]
    for _ in range(WIDE // 2 - 1):
        left.append(permute(left[-1], plus))
        right.append(permute(right[-1], minus))
    opposite = [permute(left[-1][:half], plus), permute(right[-1][half:], minus)]
    row = jnp.concatenate(right[1:] + opposite + left[:0:-1] + [near])

    below = permute(row, across([(0, 1), (1, 2), (2, 3)]))
    above = permute(row, across([(0, 3), (1, 0)]))
    middle = row.shape[0] // 2
    below2 = permute(below[:middle], across([(1, 2), (2, 3)]))
    above2 = permute(above[middle:], across([(0, 3), (3, 2)]))

    rest = jnp.where(mine == 0, rest, jnp.zeros_like(rest))
    rest = rest + permute(rest, [(0, WIDE)])
    rest = rest + permute(rest, [(0, 3 * WIDE), (WIDE, 2 * WIDE)])
    rest, row = lax.optimization_barrier((rest, row))
    chain = lambda hops: [(r * WIDE + a, r * WIDE + b) for a, b in hops for r in range(tall)]
    rest = rest + permute(rest, chain([(0, 1)]))
    rest = rest + permute(rest, chain([(0, 7), (1, 2)]))
    rest = rest + permute(rest, chain([(7, 6), (2, 3)]))
    rest = rest + permute(rest, chain([(6, 5), (3, 4)]))

    own_w, other_w = weight_halves(core.astype(jnp.int32)[None], output_weight, chips)
    other_w = lax.ppermute(other_w, "head", swap)

    place = jnp.concatenate([jnp.stack([mine, blocks]).astype(jnp.int32), anchor_length])
    state = own_row(place, queries, key_rows, value_rows, row)
    state = more_rows(place, queries, below, above, state)
    at = (WIDE - 1 - z) * NEAR
    pick = lambda x: lax.dynamic_slice_in_dim(x, at, NEAR)
    twice = jnp.concatenate([below2, above2])
    first = jnp.where(
        y == 0, pick(row), jnp.where(y == 1, pick(below), jnp.where(y == 2, pick(twice), pick(above)))
    )

    outs, parts = [], 2
    rows_each = length // parts
    half = rows_each // 2
    spot = chip.astype(jnp.int32)[None]
    for part in range(parts):
        own = last_rows(place, queries, below2, above2, far, first, rest, state, part, parts)
        other = lax.ppermute(own, "head", swap)
        terms = project(spot, own, other, own_w, other_w)
        from_below = lax.ppermute(terms[2, :half], "head", up)
        from_above = lax.ppermute(terms[2, half:], "head", down)
        upward = jnp.concatenate([added(terms[1, :half], from_below), terms[1, half:]])
        downward = jnp.concatenate([terms[3, :half], added(terms[3, half:], from_above)])
        outs.append(
            added(terms[0], lax.ppermute(upward, "head", up), lax.ppermute(downward, "head", down))
        )
    return jnp.concatenate(outs)


def solution(mesh):
    placed = (
        P("ctx", "head"),
        P("ctx", "head"),
        P("ctx", "head"),
        P("head", "ctx"),
        P("head"),
        P("head", None),
    )
    return jax.shard_map(
        on_device, mesh=mesh, in_specs=placed, out_specs=P("ctx", "head"), check_vma=False
    )
```

```python
import functools

import jax
import jax.numpy as jnp
from jax import lax
from jax.experimental import pallas as pl
from jax.experimental.pallas import tpu as pltpu
from jax.sharding import PartitionSpec as P

HEAD = 128
WIDE = 8
NEAR = 192
INFO = 16
PER_BLOCK = 256
OWN, BELOW, ABOVE, BELOW2 = range(4)
LOG2E = 1.4426950408889634
FACTOR = HEAD**-0.5 * LOG2E
LIMIT = 2.0**100
NEGATIVE = -1e30
NT = (((1,), (1,)), ((), ()))
VMEM = pl.BlockSpec(memory_space=pltpu.VMEM)
SMEM = pl.BlockSpec(memory_space=pltpu.SMEM)
PARAMS = pltpu.CompilerParams(vmem_limit_bytes=28 * 2**20)


def dot(a, b):
    return jnp.dot(a, b, preferred_element_type=jnp.float32)


def dot_nt(a, b):
    return lax.dot_general(a, b, NT, preferred_element_type=jnp.float32)


def count_along(shape, dim):
    return lax.broadcasted_iota(jnp.int32, shape, dim)


def ones_where(condition):
    return jnp.where(condition, 1.0, 0.0).astype(jnp.bfloat16)


def select_kernel(used_ref, kept_ref, key_ref, value_ref, near_ref, far_ref):
    length, keep = key_ref.shape[0], kept_ref.shape[1]
    near = near_ref.shape[0]
    hit = ones_where(count_along((length, keep), 0) == kept_ref[...])
    kept = dot_nt(jnp.ones((8, keep), jnp.bfloat16), hit)
    square = (length, length)
    before = ones_where(count_along(square, 0) < count_along(square, 1))
    rank = dot(kept.astype(jnp.bfloat16), before)
    column = count_along((8, length), 1)
    place = jnp.where(kept > 0.5, rank, column.astype(jnp.float32) + keep - rank)
    order = ones_where(count_along(square, 0).astype(jnp.float32) == place[:1])
    for at, ref in enumerate((key_ref, value_ref)):
        columns = slice(at * HEAD, (at + 1) * HEAD)
        rows = dot(order, ref[...]).astype(jnp.bfloat16)
        near_ref[:, columns] = rows[:near]
        far_ref[: length - near, columns] = rows[near:]
    in_both = jnp.where((kept > 0.5) & (column < used_ref[0]), 1.0, 0.0)[:1]
    number = jnp.sum(in_both, axis=1, keepdims=True)
    far_ref[length - near :] = jnp.broadcast_to(number, (INFO, 2 * HEAD)).astype(jnp.bfloat16)


def select(used, kept, keys, values):
    length = keys.shape[0]
    rows = (NEAR, length - NEAR + INFO)
    whole = lambda x: pl.BlockSpec(x.shape, lambda i: (0, 0))
    return pl.pallas_call(
        select_kernel,
        out_shape=[jax.ShapeDtypeStruct((n, 2 * HEAD), jnp.bfloat16) for n in rows],
        grid=(1,),
        in_specs=[SMEM, whole(kept), whole(keys), whole(values)],
        out_specs=[pl.BlockSpec((n, 2 * HEAD), lambda i: (0, 0)) for n in rows],
        compiler_params=PARAMS,
        name="select_kept",
    )(used, kept, keys, values)


def wide(column, width):
    return jnp.concatenate([column] * (width // HEAD), axis=1)


def widened(values):
    return jnp.concatenate([values, jnp.ones_like(values)], axis=1)


def scores(q_ref, h, keys):
    query = q_ref[:, pl.ds(pl.multiple_of(h * HEAD, HEAD), HEAD)]
    return dot_nt(query, keys) * FACTOR


def local(q_ref, k_ref, v_ref, acc_ref, peak_ref, h):
    length = q_ref.shape[0]
    causal = count_along((length, length), 1) <= count_along((length, length), 0)
    raw = jnp.where(causal, scores(q_ref, h, k_ref[...]), NEGATIVE)
    peak = jnp.broadcast_to(jnp.max(raw, axis=1, keepdims=True), (length, HEAD))
    peak_ref[h] = peak
    weights = jnp.exp2(raw - wide(peak, length)).astype(jnp.bfloat16)
    acc_ref[h] = dot(weights, widened(v_ref[...]))


def fixed(q_ref, acc_ref, peak_ref, h, keys, values, allowed):
    weights = jnp.exp2(scores(q_ref, h, keys) - wide(peak_ref[h], keys.shape[0]))
    if allowed is not None:
        weights = jnp.where(allowed, weights, 0.0)
    acc_ref[h] += dot(weights.astype(jnp.bfloat16), values)


def moving(q_ref, acc_ref, peak_ref, h, keys, values, allowed):
    raw = scores(q_ref, h, keys)
    if allowed is not None:
        raw = jnp.where(allowed, raw, NEGATIVE)
    old = peak_ref[h]
    peak = jnp.maximum(old, jnp.max(raw, axis=1, keepdims=True))
    weights = jnp.exp2(raw - wide(peak, keys.shape[0]))
    if allowed is not None:
        weights = jnp.where(allowed, weights, 0.0)
    peak_ref[h] = peak
    acc_ref[h] = acc_ref[h] * wide(jnp.exp2(old - peak), 2 * HEAD) + dot(
        weights.astype(jnp.bfloat16), values
    )


def absorb(q_ref, acc_ref, peak_ref, start, tiles):
    heads = acc_ref.shape[0]
    for h in range(heads):
        start(h)
    for condition, read in tiles:

        @pl.when(condition)
        def _():
            keys, values, allowed = read()
            for h in range(heads):
                fixed(q_ref, acc_ref, peak_ref, h, keys, values, allowed)

    largest = jnp.max(acc_ref[:, :, HEAD:])

    @pl.when(jnp.logical_not(largest < LIMIT))
    def _():
        @pl.loop(0, heads)
        def _(h):
            start(h)
            for condition, read in tiles:

                @pl.when(condition)
                def _():
                    moving(q_ref, acc_ref, peak_ref, h, *read())


def split_rows(rows):
    return [(at, min(512, rows - at)) for at in range(0, rows, 512)]


def reader(ref, at, rows, allowed=None):
    def read():
        both = ref[at : at + rows]
        mask = None if allowed is None else allowed(count_along((1, rows), 1) + at)
        return both[:, :HEAD], widened(both[:, HEAD:]), mask

    return read


def whole_tiles(ref, condition, allowed=None):
    return [
        (condition, reader(ref, at, rows, allowed)) for at, rows in split_rows(ref.shape[0])
    ]


def own_row_kernel(place_ref, q_ref, k_ref, v_ref, row_ref, acc_ref, peak_ref):
    z = place_ref[0] % WIDE
    rows = row_ref.shape[0] // WIDE
    first, last = (WIDE - 1 - z) * rows, (WIDE - 1) * rows
    allowed = lambda at: (at >= first) & (at < last)
    start = functools.partial(local, q_ref, k_ref, v_ref, acc_ref, peak_ref)
    absorb(q_ref, acc_ref, peak_ref, start, whole_tiles(row_ref, z > 0, allowed))


def carried(acc_in, peak_in, acc_ref, peak_ref):
    def start(h):
        acc_ref[h] = acc_in[h]
        peak_ref[h] = peak_in[h]

    return start


def rows_kernel(place_ref, q_ref, below_ref, above_ref, far_ref, acc_in, peak_in, acc_ref, peak_ref):
    y, z = place_ref[0] // WIDE, place_ref[0] % WIDE
    each = far_ref.shape[2]

    def far(at, allowed=None):
        def read():
            both = jnp.concatenate([far_ref[c, at] for c in range(WIDE)], axis=0)
            mask = None if allowed is None else allowed(count_along((1, both.shape[0]), 1))
            return both[:, :HEAD], widened(both[:, HEAD:]), mask

        return read

    tiles = whole_tiles(below_ref, y > 0) + whole_tiles(above_ref, y == 3)
    tiles += [
        (z > 0, far(OWN, lambda at: at < z * each)),
        (y > 0, far(BELOW)),
        (y == 3, far(ABOVE)),
        (y > 1, far(BELOW2)),
    ]
    absorb(q_ref, acc_ref, peak_ref, carried(acc_in, peak_in, acc_ref, peak_ref), tiles)


def last_kernel(
    place_ref, q_ref, below2_ref, above2_ref, far_ref, rest_ref, row_ref, below_ref, above_ref,
    acc_in, peak_in, out_ref, acc_ref, peak_ref, first_ref, sem,
):
    mine, used = place_ref[0], place_ref[1]
    y, z = mine // WIDE, mine % WIDE
    near, each, keep = first_ref.shape[0], far_ref.shape[0], rest_ref.shape[0] - INFO
    column = WIDE - 1 - z
    for condition, ref in ((y == 0, row_ref), (y == 1, below_ref), (y == 3, above_ref)):

        @pl.when(condition)
        def _():
            rows = pl.ds(pl.multiple_of(column * near, near), near)
            copy = pltpu.make_async_copy(ref.at[rows], first_ref, sem)
            copy.start()
            copy.wait()

    for condition, ref, start in (
        (column < WIDE // 2, below2_ref, column),
        (column >= WIDE // 2, above2_ref, column - WIDE // 2),
    ):

        @pl.when((y == 2) & condition)
        def _():
            first_ref[...] = ref[pl.ds(pl.multiple_of(start * near, near), near)]

    def anchor():
        both = jnp.concatenate([first_ref[...], far_ref[...], rest_ref[:keep]], axis=0)
        number = wide(rest_ref[keep : keep + 1, :HEAD].astype(jnp.int32), both.shape[0])
        at = count_along((1, both.shape[0]), 1)
        split = near + each
        allowed = at < jnp.where(at < split, number, split + used - number)
        return both[:, :HEAD], widened(both[:, HEAD:]), allowed

    tiles = whole_tiles(below2_ref, y > 1) + whole_tiles(above2_ref, y > 1)
    tiles.append((mine > 0, anchor))
    absorb(q_ref, acc_ref, peak_ref, carried(acc_in, peak_in, acc_ref, peak_ref), tiles)
    for h in range(acc_ref.shape[0]):
        out_ref[:, h * HEAD : (h + 1) * HEAD] = (
            acc_ref[h, :, :HEAD] / acc_ref[h, :, HEAD:]
        ).astype(jnp.bfloat16)


def pack_row_kernel(*refs):
    out_ref = refs[-1]
    at = 0
    for ref in refs[:-1]:
        out_ref[at : at + ref.shape[0]] = ref[...]
        at += ref.shape[0]


def pack_row(pieces):
    rows = sum(piece.shape[0] for piece in pieces)
    return pl.pallas_call(
        pack_row_kernel,
        out_shape=jax.ShapeDtypeStruct((rows, 2 * HEAD), jnp.bfloat16),
        in_specs=[VMEM] * len(pieces),
        out_specs=VMEM,
        compiler_params=PARAMS,
        name="pack_row",
    )(*pieces)


def pack_far_kernel(place_ref, own_ref, below_ref, above_ref, below2_ref, far_ref, rest_ref):
    y, z = place_ref[0] // WIDE, place_ref[0] % WIDE
    each = far_ref.shape[1]
    for at, ref in ((OWN, own_ref), (BELOW, below_ref), (ABOVE, above_ref), (BELOW2, below2_ref)):
        far_ref[at] = ref[:each]
    for row, ref in enumerate((own_ref, below_ref, below2_ref, above_ref)):

        @pl.when((y == row) & (z == 0))
        def _():
            rest_ref[...] = ref[each:]

    @pl.when(z > 0)
    def _():
        rest_ref[...] = jnp.zeros_like(rest_ref)


def pack_far(place, *pieces):
    rows, keep = pieces[0].shape[0], PER_BLOCK - NEAR
    return pl.pallas_call(
        pack_far_kernel,
        out_shape=[
            jax.ShapeDtypeStruct((len(pieces), keep, 2 * HEAD), jnp.bfloat16),
            jax.ShapeDtypeStruct((rows - keep, 2 * HEAD), jnp.bfloat16),
        ],
        in_specs=[SMEM] + [VMEM] * len(pieces),
        out_specs=[VMEM] * 2,
        compiler_params=PARAMS,
        name="pack_far",
    )(place, *pieces)


def cost(rows, keys):
    return pl.CostEstimate(
        flops=rows * keys * HEAD * 8, bytes_accessed=8 * 2**20, transcendentals=rows * keys
    )


def state_of(length, heads):
    return [
        jax.ShapeDtypeStruct((heads, length, 2 * HEAD), jnp.float32),
        jax.ShapeDtypeStruct((heads, length, HEAD), jnp.float32),
    ]


def own_row(place, queries, keys, values, row):
    length, width = queries.shape
    return pl.pallas_call(
        own_row_kernel,
        out_shape=state_of(length, width // HEAD),
        in_specs=[SMEM] + [VMEM] * 4,
        out_specs=[VMEM] * 2,
        compiler_params=PARAMS,
        cost_estimate=cost(length * width // HEAD, length + row.shape[0]),
        name="own_row",
    )(place, queries, keys, values, row)


def more_rows(place, queries, below, above, far, state):
    length, width = queries.shape
    return pl.pallas_call(
        rows_kernel,
        out_shape=state_of(length, width // HEAD),
        in_specs=[SMEM] + [VMEM] * 6,
        out_specs=[VMEM] * 2,
        compiler_params=PARAMS,
        cost_estimate=cost(length * width // HEAD, 2 * below.shape[0] + 3 * 512),
        name="more_rows",
    )(place, queries, below, above, far, *state)


def last_rows(place, queries, below2, above2, far, rest, row, below, above, state, part, parts):
    length, width = queries.shape
    rows, heads = length // parts, width // HEAD
    whole = lambda x: pl.BlockSpec(x.shape, lambda i: (0,) * x.ndim)
    slab = lambda columns: pl.BlockSpec((heads, rows, columns), lambda i: (0, part, 0))
    each = far.shape[2]

    def place_of(i, place):
        y = place[0] // WIDE
        return 0, jnp.where(y == 1, BELOW, jnp.where(y == 2, BELOW2, jnp.where(y == 3, ABOVE, OWN))), 0, 0

    return pl.pallas_call(
        last_kernel,
        grid_spec=pltpu.PrefetchScalarGridSpec(
            num_scalar_prefetch=1,
            grid=(1,),
            in_specs=[
                pl.BlockSpec((rows, width), lambda i, place: (part, 0)),
                *[pl.BlockSpec(x.shape, lambda i, place: (0, 0)) for x in (below2, above2)],
                pl.BlockSpec((None, None, each, 2 * HEAD), place_of),
                pl.BlockSpec(rest.shape, lambda i, place: (0, 0)),
                *[pl.BlockSpec(memory_space=pl.ANY)] * 3,
                pl.BlockSpec((heads, rows, 2 * HEAD), lambda i, place: (0, part, 0)),
                pl.BlockSpec((heads, rows, HEAD), lambda i, place: (0, part, 0)),
            ],
            out_specs=pl.BlockSpec((rows, width), lambda i, place: (0, 0)),
            scratch_shapes=[
                pltpu.VMEM((heads, rows, 2 * HEAD), jnp.float32),
                pltpu.VMEM((heads, rows, HEAD), jnp.float32),
                pltpu.VMEM((NEAR, 2 * HEAD), jnp.bfloat16),
                pltpu.SemaphoreType.DMA,
            ],
        ),
        out_shape=jax.ShapeDtypeStruct((rows, width), jnp.bfloat16),
        compiler_params=PARAMS,
        cost_estimate=cost(rows * heads, 2048),
        name=f"last_rows_{part}",
    )(place, queries, below2, above2, far, rest, row, below, above, *state)


def project_kernel(place_ref, own_ref, other_ref, weight_ref, other_w_ref, out_ref):
    chips, _, columns = out_ref.shape
    for step in range(chips):
        at = lax.rem(place_ref[0] + step, chips)
        mine = pl.ds(pl.multiple_of((2 * at + place_ref[1]) * columns, columns), columns)
        total = dot(own_ref[...], weight_ref[:, mine]) + dot(other_ref[...], other_w_ref[at])
        out_ref[step] = total.astype(jnp.bfloat16)


def project(place, own, other, weight, other_w):
    chips, _, columns = other_w.shape
    return pl.pallas_call(
        project_kernel,
        out_shape=jax.ShapeDtypeStruct((chips, own.shape[0], columns), jnp.bfloat16),
        in_specs=[SMEM] + [VMEM] * 4,
        out_specs=VMEM,
        compiler_params=PARAMS,
        cost_estimate=pl.CostEstimate(
            flops=4 * own.size * chips * columns, bytes_accessed=8 * 2**20, transcendentals=0
        ),
        name="project",
    )(place, own, other, weight, other_w)


def weight_kernel(place_ref, weight_ref, out_ref):
    columns = out_ref.shape[2]
    start = pl.multiple_of((1 - place_ref[1]) * columns, columns)
    out_ref[0] = weight_ref[:, pl.ds(start, columns)]


def weight_half(place, weight, chips):
    rows, columns = weight.shape[0], weight.shape[1] // chips // 2
    return pl.pallas_call(
        weight_kernel,
        grid=(chips,),
        out_shape=jax.ShapeDtypeStruct((chips, rows, columns), weight.dtype),
        in_specs=[SMEM, pl.BlockSpec((rows, 2 * columns), lambda i: (0, i))],
        out_specs=pl.BlockSpec((1, rows, columns), lambda i: (i, 0, 0)),
        compiler_params=PARAMS,
        cost_estimate=pl.CostEstimate(flops=0, bytes_accessed=6 * 2**20, transcendentals=0),
        name="weight_half",
    )(place, weight)


def added(*terms):
    return sum(term.astype(jnp.float32) for term in terms).astype(jnp.bfloat16)


def on_device(queries, key_rows, value_rows, kept_positions, anchor_length, output_weight):
    mine, head = lax.axis_index("ctx"), lax.axis_index("head")
    length, devices, blocks = queries.shape[0], lax.axis_size("head"), lax.axis_size("ctx")
    chips, chip, core = devices // 2, head // 2, head % 2
    tall = blocks // WIDE
    swap = [(i, i ^ 1) for i in range(devices)]
    up = [(i, (i + 2) % devices) for i in range(devices)]
    down = [(i, (i - 2) % devices) for i in range(devices)]
    along = lambda step: [
        (r * WIDE + c, r * WIDE + (c + step) % WIDE) for r in range(tall) for c in range(WIDE)
    ]
    across = lambda hops: [(a * WIDE + c, b * WIDE + c) for a, b in hops for c in range(WIDE)]
    permute = lambda x, pairs: lax.ppermute(x, "ctx", pairs)

    place = jnp.concatenate([mine.astype(jnp.int32)[None], anchor_length])
    spot = jnp.stack([chip, core]).astype(jnp.int32)
    near, far = select(anchor_length, kept_positions, key_rows, value_rows)

    below = permute(far, across([(0, 1), (1, 2), (2, 3)]))
    above = permute(far, across([(0, 3)]))
    below2 = permute(below, across([(1, 2), (2, 3)]))
    far, rest = pack_far(place, far, below, above, below2)
    rows = [[r * WIDE + c for c in range(WIDE)] for r in range(tall)]
    far = lax.all_gather(far, "ctx", axis_index_groups=rows)

    plus, minus = along(1), along(-1)
    half = NEAR // 2
    left, right = [near], [near]
    for _ in range(WIDE // 2 - 1):
        left.append(permute(left[-1], plus))
        right.append(permute(right[-1], minus))
    opposite = [permute(left[-1][:half], plus), permute(right[-1][half:], minus)]
    row = pack_row(right[1:] + opposite + left[:0:-1] + [near])

    below = permute(row, across([(0, 1), (1, 2), (2, 3)]))
    above = permute(row, across([(0, 3), (1, 0)]))
    middle = row.shape[0] // 2
    below2 = permute(below[:middle], across([(1, 2), (2, 3)]))
    above2 = permute(above[middle:], across([(0, 3), (3, 2)]))

    rest, row = lax.optimization_barrier((rest, row))
    chain = lambda hops: [(r * WIDE + a, r * WIDE + b) for a, b in hops for r in range(tall)]
    for hops in ([(0, 1)], [(0, 7), (1, 2)], [(7, 6), (2, 3)], [(6, 5), (3, 4)]):
        rest = rest + permute(rest, chain(hops))

    other_w = lax.ppermute(weight_half(spot, output_weight, chips), "head", swap)

    state = own_row(place, queries, key_rows, value_rows, row)
    state = more_rows(place, queries, below, above, far, state)

    outs, parts = [], 2
    rows_each = length // parts
    half = rows_each // 2
    for part in range(parts):
        own = last_rows(
            place, queries, below2, above2, far, rest, row, below, above, state, part, parts
        )
        other = lax.ppermute(own, "head", swap)
        terms = project(spot, own, other, output_weight, other_w)
        from_below = lax.ppermute(terms[2, :half], "head", up)
        from_above = lax.ppermute(terms[2, half:], "head", down)
        upward = jnp.concatenate([added(terms[1, :half], from_below), terms[1, half:]])
        downward = jnp.concatenate([terms[3, :half], added(terms[3, half:], from_above)])
        outs.append(
            added(terms[0], lax.ppermute(upward, "head", up), lax.ppermute(downward, "head", down))
        )
    return jnp.concatenate(outs)


def solution(mesh):
    placed = (
        P("ctx", "head"),
        P("ctx", "head"),
        P("ctx", "head"),
        P("head", "ctx"),
        P("head"),
        P("head", None),
    )
    return jax.shard_map(
        on_device, mesh=mesh, in_specs=placed, out_specs=P("ctx", "head"), check_vma=False
    )
```

```python
import functools

import jax
import jax.numpy as jnp
from jax import lax
from jax.experimental import pallas as pl
from jax.experimental.pallas import tpu as pltpu
from jax.sharding import PartitionSpec as P

HEAD = 128
WIDE = 8
NEAR = 192
INFO = 16
PER_BLOCK = 256
OWN, BELOW, ABOVE, BELOW2 = range(4)
LOG2E = 1.4426950408889634
FACTOR = HEAD**-0.5 * LOG2E
LIMIT = 2.0**100
NEGATIVE = -1e30
NT = (((1,), (1,)), ((), ()))
VMEM = pl.BlockSpec(memory_space=pltpu.VMEM)
SMEM = pl.BlockSpec(memory_space=pltpu.SMEM)
HBM = pl.BlockSpec(memory_space=pltpu.HBM)
ANY = pl.BlockSpec(memory_space=pl.ANY)
TILE = 512
EACH = 64
PARAMS = pltpu.CompilerParams(vmem_limit_bytes=28 * 2**20)


def dot(a, b):
    return jnp.dot(a, b, preferred_element_type=jnp.float32)


def dot_nt(a, b):
    return lax.dot_general(a, b, NT, preferred_element_type=jnp.float32)


def count_along(shape, dim):
    return lax.broadcasted_iota(jnp.int32, shape, dim)


def ones_where(condition):
    return jnp.where(condition, 1.0, 0.0).astype(jnp.bfloat16)


def select_kernel(used_ref, *refs):
    sources, (near_ref, far_ref), targets, sems = refs[:3], refs[3:5], refs[5:8], refs[8]
    copies = [
        pltpu.make_async_copy(source, target, sems.at[at])
        for at, (source, target) in enumerate(zip(sources, targets))
    ]
    for copy in copies:
        copy.start()
    for copy in copies:
        copy.wait()
    kept_ref, key_ref, value_ref = targets
    length, keep = key_ref.shape[0], kept_ref.shape[1]
    near = near_ref.shape[0]
    hit = ones_where(count_along((length, keep), 0) == kept_ref[...])
    kept = dot_nt(jnp.ones((8, keep), jnp.bfloat16), hit)
    square = (length, length)
    before = ones_where(count_along(square, 0) < count_along(square, 1))
    rank = dot(kept.astype(jnp.bfloat16), before)
    column = count_along((8, length), 1)
    place = jnp.where(kept > 0.5, rank, column.astype(jnp.float32) + keep - rank)
    order = ones_where(count_along(square, 0).astype(jnp.float32) == place[:1])
    for at, ref in enumerate((key_ref, value_ref)):
        columns = slice(at * HEAD, (at + 1) * HEAD)
        rows = dot(order, ref[...]).astype(jnp.bfloat16)
        near_ref[:, columns] = rows[:near]
        far_ref[: length - near, columns] = rows[near:]
    in_both = jnp.where((kept > 0.5) & (column < used_ref[0]), 1.0, 0.0)[:1]
    number = jnp.sum(in_both, axis=1, keepdims=True)
    far_ref[length - near :] = jnp.broadcast_to(number, (INFO, 2 * HEAD)).astype(jnp.bfloat16)


def select(used, kept, keys, values):
    length = keys.shape[0]
    rows = (NEAR, length - NEAR + INFO)
    return pl.pallas_call(
        select_kernel,
        out_shape=[jax.ShapeDtypeStruct((n, 2 * HEAD), jnp.bfloat16) for n in rows],
        in_specs=[SMEM, HBM, HBM, HBM],
        out_specs=[VMEM] * 2,
        scratch_shapes=[
            *[pltpu.VMEM(x.shape, x.dtype) for x in (kept, keys, values)],
            pltpu.SemaphoreType.DMA((3,)),
        ],
        compiler_params=PARAMS,
        name="select_kept",
    )(used, kept, keys, values)


def wide(column, width):
    return jnp.concatenate([column] * (width // HEAD), axis=1)


def widened(values):
    return jnp.concatenate([values, jnp.ones_like(values)], axis=1)


def scores(query, keys):
    return dot_nt(query, keys) * FACTOR


def local(k_ref, v_ref, acc_ref, peak_ref, h, query):
    shape = (query.shape[0], k_ref.shape[0])
    causal = count_along(shape, 1) <= count_along(shape, 0) + pl.program_id(0) * shape[0]
    raw = jnp.where(causal, scores(query, k_ref[...]), NEGATIVE)
    peak = jnp.broadcast_to(jnp.max(raw, axis=1, keepdims=True), (shape[0], HEAD))
    peak_ref[h] = peak
    weights = jnp.exp2(raw - wide(peak, shape[1])).astype(jnp.bfloat16)
    acc_ref[h] = dot(weights, widened(v_ref[...]))


def biased(raw, bias):
    return (raw.reshape(-1, *bias.shape) + bias).reshape(raw.shape)


def fixed(acc_ref, peak_ref, h, query, keys, values, bias):
    raw = biased(scores(query, keys), bias)
    weights = jnp.exp2(raw - wide(peak_ref[h], keys.shape[0])).astype(jnp.bfloat16)
    acc_ref[h] += dot(weights, values)


def moving(acc_ref, peak_ref, h, query, keys, values, bias):
    raw = biased(scores(query, keys), bias)
    old = peak_ref[h]
    peak = jnp.maximum(old, jnp.max(raw, axis=1, keepdims=True))
    weights = jnp.exp2(raw - wide(peak, keys.shape[0])).astype(jnp.bfloat16)
    peak_ref[h] = peak
    acc_ref[h] = acc_ref[h] * wide(jnp.exp2(old - peak), 2 * HEAD) + dot(weights, values)


def absorb(q_ref, acc_ref, peak_ref, start, tiles, read):
    heads = acc_ref.shape[0]

    def each_head(act):
        for h in range(heads):
            act(h, q_ref[:, h * HEAD : (h + 1) * HEAD])

    each_head(start)

    @pl.loop(0, tiles)
    def _(tile):
        keys = read(tile)
        each_head(lambda h, query: fixed(acc_ref, peak_ref, h, query, *keys))

    largest = jnp.max(acc_ref[:, :, HEAD:])

    @pl.when(jnp.logical_not(largest < LIMIT))
    def _():
        @pl.loop(0, heads)
        def _(h):
            query = q_ref[:, pl.ds(pl.multiple_of(h * HEAD, HEAD), HEAD)]
            start(h, query)

            @pl.loop(0, tiles)
            def _(tile):
                moving(acc_ref, peak_ref, h, query, *read(tile))


def tile_of(ref, at):
    rows = pl.ds(pl.multiple_of(at * TILE, TILE), TILE)
    return ref[rows, :HEAD], widened(ref[rows, HEAD:])


def bias_where(allowed):
    return jnp.where(allowed, 0.0, NEGATIVE)


def own_row_kernel(place_ref, q_ref, k_ref, v_ref, row_ref, acc_ref, peak_ref, bias_ref):
    keys = place_ref[0] % WIDE * NEAR
    start = functools.partial(local, k_ref, v_ref, acc_ref, peak_ref)

    def read(tile):
        bias_ref[...] = bias_where(count_along(bias_ref.shape, 1) + tile * TILE < keys)
        return *tile_of(row_ref, tile), bias_ref[...]

    absorb(q_ref, acc_ref, peak_ref, start, (keys + TILE - 1) // TILE, read)


def rest_kernel(
    place_ref, q_ref, row_ref, below_ref, above_ref, below2_ref, above2_ref, far_ref, rest_ref,
    acc_in, peak_in, out_ref, bank_ref, bias_ref, acc_ref, peak_ref, sems,
):
    mine, used = place_ref[0], place_ref[1]
    y, z = mine // WIDE, mine % WIDE
    span, far_rows = WIDE * NEAR, far_ref.shape[0]
    half = TILE // 2
    copies = []

    def copy(source, at, rows, condition=None):
        target = bank_ref.at[pl.ds(at, rows)]
        copies.append((pltpu.make_async_copy(source, target, sems.at[len(copies)]), condition))

    for row, ref in enumerate((row_ref, below_ref, below2_ref, above_ref)):
        copy(ref.at[pl.ds(0, NEAR)], 0, NEAR, y == row)
    at_row = jnp.where(y == 1, BELOW, jnp.where(y == 2, BELOW2, jnp.where(y == 3, ABOVE, OWN)))
    copy(far_ref.at[pl.ds(pl.multiple_of(at_row * EACH, EACH), EACH)], NEAR, EACH)
    copy(far_ref, TILE, far_rows)
    at = TILE + far_rows
    copy(below_ref, at, span, y > 0)
    copy(below2_ref, at + span, span // 2, y > 1)
    copy(above2_ref, at + span + span // 2, span // 2, y > 1)
    copy(above_ref, at + 2 * span, span, y == 3)

    def under(condition, act):
        if condition is None:
            act()
        else:
            pl.when(condition)(act)

    for one, condition in copies:
        under(condition, one.start)
    bank_ref[half:TILE] = rest_ref[:half]
    number = wide(rest_ref[half : half + 1, :HEAD].astype(jnp.int32), TILE)
    at = count_along((1, TILE), 1)
    limit = jnp.where(at < half, number, half + used - number)
    bias_ref[0] = jnp.broadcast_to(bias_where(at < limit), bias_ref.shape[1:])
    piece = count_along(bias_ref.shape[1:], 1) // EACH
    row = piece % 4
    for tile in range(far_rows // TILE):
        column = piece // 4 + tile * (TILE // EACH // 4)
        reach = jnp.where(
            row == OWN, z, jnp.where(row == BELOW, y, jnp.where(row == BELOW2, y - 1, y - 2)) * WIDE
        )
        bias_ref[1 + tile] = bias_where(column < reach)
    bias_ref[1 + far_rows // TILE] = jnp.zeros(bias_ref.shape[1:], jnp.float32)

    def start(h, query):
        acc_ref[h] = acc_in[h]
        peak_ref[h] = peak_in[h]

    for one, condition in copies:
        under(condition, one.wait)

    def read(tile):
        return *tile_of(bank_ref, tile), bias_ref[jnp.minimum(tile, bias_ref.shape[0] - 1)]

    tiles = jnp.where(mine > 0, 1 + far_rows // TILE + span // TILE * y, 0)
    absorb(q_ref, acc_ref, peak_ref, start, tiles, read)
    for h in range(acc_ref.shape[0]):
        out_ref[:, h * HEAD : (h + 1) * HEAD] = (
            acc_ref[h, :, :HEAD] / acc_ref[h, :, HEAD:]
        ).astype(jnp.bfloat16)


def pack_far_kernel(place_ref, own_ref, below_ref, above_ref, below2_ref, far_ref, rest_ref):
    y, z = place_ref[0] // WIDE, place_ref[0] % WIDE
    each = far_ref.shape[1]
    for at, ref in ((OWN, own_ref), (BELOW, below_ref), (ABOVE, above_ref), (BELOW2, below2_ref)):
        far_ref[at] = ref[:each]
    for row, ref in enumerate((own_ref, below_ref, below2_ref, above_ref)):

        @pl.when((y == row) & (z == 0))
        def _():
            rest_ref[...] = ref[each:]

    @pl.when(z > 0)
    def _():
        rest_ref[...] = jnp.zeros_like(rest_ref)


def pack_far(place, *pieces):
    rows, keep = pieces[0].shape[0], PER_BLOCK - NEAR
    return pl.pallas_call(
        pack_far_kernel,
        out_shape=[
            jax.ShapeDtypeStruct((len(pieces), keep, 2 * HEAD), jnp.bfloat16),
            jax.ShapeDtypeStruct((rows - keep, 2 * HEAD), jnp.bfloat16),
        ],
        in_specs=[SMEM] + [VMEM] * len(pieces),
        out_specs=[VMEM] * 2,
        compiler_params=PARAMS,
        name="pack_far",
    )(place, *pieces)


def cost(rows, keys):
    return pl.CostEstimate(
        flops=rows * keys * HEAD * 8, bytes_accessed=8 * 2**20, transcendentals=rows * keys
    )


def state_of(length, heads):
    return [
        jax.ShapeDtypeStruct((heads, length, 2 * HEAD), jnp.float32),
        jax.ShapeDtypeStruct((heads, length, HEAD), jnp.float32),
    ]


def own_row(place, queries, keys, values, row, parts):
    length, width = queries.shape
    rows, heads = length // parts, width // HEAD
    whole = lambda x: pl.BlockSpec(x.shape, lambda i: (0,) * x.ndim)
    slab = lambda columns: pl.BlockSpec((heads, rows, columns), lambda i: (0, i, 0))
    return pl.pallas_call(
        own_row_kernel,
        grid=(parts,),
        out_shape=state_of(length, heads),
        in_specs=[
            SMEM,
            pl.BlockSpec((rows, width), lambda i: (i, 0)),
            *[whole(x) for x in (keys, values, row)],
        ],
        out_specs=[slab(2 * HEAD), slab(HEAD)],
        scratch_shapes=[pltpu.VMEM((8, TILE), jnp.float32)],
        compiler_params=PARAMS,
        cost_estimate=cost(length * heads, length + WIDE * NEAR),
        name="own_row",
    )(place, queries, keys, values, row)


def rest_rows(place, queries, banks, rest, state, part, parts):
    length, width = queries.shape
    rows, heads = length // parts, width // HEAD
    tiles = 14
    slab = lambda columns: pl.BlockSpec((heads, rows, columns), lambda i: (0, part, 0))
    return pl.pallas_call(
        rest_kernel,
        grid=(1,),
        out_shape=jax.ShapeDtypeStruct((rows, width), jnp.bfloat16),
        in_specs=[
            SMEM,
            pl.BlockSpec((rows, width), lambda i: (part, 0)),
            *[HBM, ANY, ANY, ANY, ANY, HBM],
            pl.BlockSpec(rest.shape, lambda i: (0, 0)),
            slab(2 * HEAD),
            slab(HEAD),
        ],
        out_specs=pl.BlockSpec((rows, width), lambda i: (0, 0)),
        scratch_shapes=[
            pltpu.VMEM((tiles * TILE, 2 * HEAD), jnp.bfloat16),
            pltpu.VMEM((6, 8, TILE), jnp.float32),
            pltpu.VMEM((heads, rows, 2 * HEAD), jnp.float32),
            pltpu.VMEM((heads, rows, HEAD), jnp.float32),
            pltpu.SemaphoreType.DMA((10,)),
        ],
        compiler_params=PARAMS,
        cost_estimate=cost(rows * heads, tiles * TILE),
        name=f"rest_rows_{part}",
    )(place, queries, *banks, rest, *state)


def project_kernel(place_ref, own_ref, other_ref, weight_ref, other_w_ref, out_ref):
    chips, _, columns = out_ref.shape
    for step in range(chips):
        at = lax.rem(place_ref[0] + step, chips)
        mine = pl.ds(pl.multiple_of((2 * at + place_ref[1]) * columns, columns), columns)
        total = dot(own_ref[...], weight_ref[:, mine]) + dot(other_ref[...], other_w_ref[at])
        out_ref[step] = total.astype(jnp.bfloat16)


def project(place, own, other, weight, other_w):
    chips, _, columns = other_w.shape
    return pl.pallas_call(
        project_kernel,
        out_shape=jax.ShapeDtypeStruct((chips, own.shape[0], columns), jnp.bfloat16),
        in_specs=[SMEM] + [VMEM] * 4,
        out_specs=VMEM,
        compiler_params=PARAMS,
        cost_estimate=pl.CostEstimate(
            flops=4 * own.size * chips * columns, bytes_accessed=8 * 2**20, transcendentals=0
        ),
        name="project",
    )(place, own, other, weight, other_w)


def weight_kernel(place_ref, weight_ref, out_ref):
    columns = out_ref.shape[2]
    start = pl.multiple_of((1 - place_ref[1]) * columns, columns)
    out_ref[0] = weight_ref[:, pl.ds(start, columns)]


def weight_half(place, weight, chips):
    rows, columns = weight.shape[0], weight.shape[1] // chips // 2
    return pl.pallas_call(
        weight_kernel,
        grid=(chips,),
        out_shape=jax.ShapeDtypeStruct((chips, rows, columns), weight.dtype),
        in_specs=[SMEM, pl.BlockSpec((rows, 2 * columns), lambda i: (0, i))],
        out_specs=pl.BlockSpec((1, rows, columns), lambda i: (i, 0, 0)),
        compiler_params=PARAMS,
        cost_estimate=pl.CostEstimate(flops=0, bytes_accessed=6 * 2**20, transcendentals=0),
        name="weight_half",
    )(place, weight)


def added(*terms):
    return sum(term.astype(jnp.float32) for term in terms).astype(jnp.bfloat16)


def on_device(queries, key_rows, value_rows, kept_positions, anchor_length, output_weight):
    mine, head = lax.axis_index("ctx"), lax.axis_index("head")
    length, devices, blocks = queries.shape[0], lax.axis_size("head"), lax.axis_size("ctx")
    chips, chip, core = devices // 2, head // 2, head % 2
    tall = blocks // WIDE
    swap = [(i, i ^ 1) for i in range(devices)]
    up = [(i, (i + 2) % devices) for i in range(devices)]
    down = [(i, (i - 2) % devices) for i in range(devices)]
    across = lambda hops: [(a * WIDE + c, b * WIDE + c) for a, b in hops for c in range(WIDE)]
    permute = lambda x, pairs: lax.ppermute(x, "ctx", pairs)

    place = jnp.concatenate([mine.astype(jnp.int32)[None], anchor_length])
    spot = jnp.stack([chip, core]).astype(jnp.int32)
    near, far = select(anchor_length, kept_positions, key_rows, value_rows)

    below = permute(far, across([(0, 1), (1, 2), (2, 3)]))
    above = permute(far, across([(0, 3)]))
    below2 = permute(below, across([(1, 2), (2, 3)]))
    far, rest = pack_far(place, far, below, above, below2)
    half_w = weight_half(spot, output_weight, chips)
    rows = [[r * WIDE + c for c in range(WIDE)] for r in range(tall)]

    row = lax.all_gather(near, "ctx", axis_index_groups=rows).reshape(-1, 2 * HEAD)
    row, far, rest, half_w = lax.optimization_barrier((row, far, rest, half_w))
    far = lax.all_gather(far, "ctx", axis_index_groups=rows).reshape(-1, 2 * HEAD)
    below = permute(row, across([(0, 1), (1, 2), (2, 3)]))
    above = permute(row, across([(0, 3), (1, 0)]))
    middle = row.shape[0] // 2
    below2 = permute(below[:middle], across([(1, 2), (2, 3)]))
    above2 = permute(above[middle:], across([(0, 3), (3, 2)]))

    chain = lambda hops: [(r * WIDE + a, r * WIDE + b) for a, b in hops for r in range(tall)]
    for hops in ([(0, 1)], [(0, 7), (1, 2)], [(7, 6), (2, 3)], [(6, 5), (3, 4)]):
        rest = rest + permute(rest, chain(hops))

    other_w = lax.ppermute(half_w, "head", swap)

    parts = 2
    state = own_row(place, queries, key_rows, value_rows, row, parts)
    banks = (row, below, above, below2, above2, far)

    outs = []
    rows_each = length // parts
    half = rows_each // 2
    for part in range(parts):
        own = rest_rows(place, queries, banks, rest, state, part, parts)
        other = lax.ppermute(own, "head", swap)
        terms = project(spot, own, other, output_weight, other_w)
        from_below = lax.ppermute(terms[2, :half], "head", up)
        from_above = lax.ppermute(terms[2, half:], "head", down)
        upward = jnp.concatenate([added(terms[1, :half], from_below), terms[1, half:]])
        downward = jnp.concatenate([terms[3, :half], added(terms[3, half:], from_above)])
        outs.append(
            added(terms[0], lax.ppermute(upward, "head", up), lax.ppermute(downward, "head", down))
        )
    return jnp.concatenate(outs)


def solution(mesh):
    placed = (
        P("ctx", "head"),
        P("ctx", "head"),
        P("ctx", "head"),
        P("head", "ctx"),
        P("head"),
        P("head", None),
    )
    return jax.shard_map(
        on_device, mesh=mesh, in_specs=placed, out_specs=P("ctx", "head"), check_vma=False
    )
```

```python
import functools

import jax
import jax.numpy as jnp
from jax import lax
from jax.experimental import pallas as pl
from jax.experimental.pallas import tpu as pltpu
from jax.sharding import PartitionSpec as P

HEAD = 128
WIDE = 8
INFO = 16
KEEP = 256
LOG2E = 1.4426950408889634
FACTOR = HEAD**-0.5 * LOG2E
LIMIT = 2.0**100
NEGATIVE = -1e30
NT = (((1,), (1,)), ((), ()))
VMEM = pl.BlockSpec(memory_space=pltpu.VMEM)
SMEM = pl.BlockSpec(memory_space=pltpu.SMEM)
HBM = pl.BlockSpec(memory_space=pltpu.HBM)
ANY = pl.BlockSpec(memory_space=pl.ANY)
TILE = 512
PARAMS = pltpu.CompilerParams(vmem_limit_bytes=60 * 2**20)


def dot(a, b):
    return jnp.dot(a, b, preferred_element_type=jnp.float32)


def dot_nt(a, b):
    return lax.dot_general(a, b, NT, preferred_element_type=jnp.float32)


def count_along(shape, dim):
    return lax.broadcasted_iota(jnp.int32, shape, dim)


def ones_where(condition):
    return jnp.where(condition, 1.0, 0.0).astype(jnp.bfloat16)


def select_kernel(used_ref, *refs):
    sources, (kept_rows_ref, rest_ref), targets, sems = refs[:3], refs[3:5], refs[5:8], refs[8]
    copies = [
        pltpu.make_async_copy(source, target, sems.at[at])
        for at, (source, target) in enumerate(zip(sources, targets))
    ]
    for copy in copies:
        copy.start()
    for copy in copies:
        copy.wait()
    kept_ref, key_ref, value_ref = targets
    length, keep = key_ref.shape[0], kept_ref.shape[1]
    hit = ones_where(count_along((length, keep), 0) == kept_ref[...])
    kept = dot_nt(jnp.ones((8, keep), jnp.bfloat16), hit)
    square = (length, length)
    before = ones_where(count_along(square, 0) < count_along(square, 1))
    rank = dot(kept.astype(jnp.bfloat16), before)
    column = count_along((8, length), 1)
    place = jnp.where(kept > 0.5, rank, column.astype(jnp.float32) + keep - rank)
    order = ones_where(count_along(square, 0).astype(jnp.float32) == place[:1])
    for at, ref in enumerate((key_ref, value_ref)):
        columns = slice(at * HEAD, (at + 1) * HEAD)
        rows = dot(order, ref[...]).astype(jnp.bfloat16)
        kept_rows_ref[:, columns] = rows[:keep]
        rest_ref[: length - keep, columns] = rows[keep:]
    in_both = jnp.where((kept > 0.5) & (column < used_ref[0]), 1.0, 0.0)[:1]
    number = jnp.sum(in_both, axis=1, keepdims=True)
    rest_ref[length - keep :] = jnp.broadcast_to(number, (INFO, 2 * HEAD)).astype(jnp.bfloat16)


def select(used, kept, keys, values):
    length = keys.shape[0]
    rows = (KEEP, length - KEEP + INFO)
    return pl.pallas_call(
        select_kernel,
        out_shape=[jax.ShapeDtypeStruct((n, 2 * HEAD), jnp.bfloat16) for n in rows],
        in_specs=[SMEM, HBM, HBM, HBM],
        out_specs=[VMEM] * 2,
        scratch_shapes=[
            *[pltpu.VMEM(x.shape, x.dtype) for x in (kept, keys, values)],
            pltpu.SemaphoreType.DMA((3,)),
        ],
        compiler_params=PARAMS,
        name="select_kept",
    )(used, kept, keys, values)


def wide(column, width):
    return jnp.concatenate([column] * (width // HEAD), axis=1)


def widened(values):
    return jnp.concatenate([values, jnp.ones_like(values)], axis=1)


def scores(query, keys):
    return dot_nt(query, keys) * FACTOR


def local(k_ref, v_ref, acc_ref, peak_ref, h, query):
    shape = (query.shape[0], k_ref.shape[0])
    causal = count_along(shape, 1) <= count_along(shape, 0) + pl.program_id(0) * shape[0]
    raw = jnp.where(causal, scores(query, k_ref[...]), NEGATIVE)
    peak = jnp.broadcast_to(jnp.max(raw, axis=1, keepdims=True), (shape[0], HEAD))
    peak_ref[h] = peak
    weights = jnp.exp2(raw - wide(peak, shape[1])).astype(jnp.bfloat16)
    acc_ref[h] = dot(weights, widened(v_ref[...]))


def biased(raw, bias):
    if bias is None:
        return raw
    return (raw.reshape(-1, *bias.shape) + bias).reshape(raw.shape)


def moving(acc_ref, peak_ref, h, query, keys, values, bias):
    raw = biased(scores(query, keys), bias)
    old = peak_ref[h]
    peak = jnp.maximum(old, jnp.max(raw, axis=1, keepdims=True))
    weights = jnp.exp2(raw - wide(peak, keys.shape[0])).astype(jnp.bfloat16)
    peak_ref[h] = peak
    acc_ref[h] = acc_ref[h] * wide(jnp.exp2(old - peak), 2 * HEAD) + dot(weights, values)


def absorb(q_ref, acc_ref, peak_ref, start, masked, tiles, read):
    heads = acc_ref.shape[0]

    def query(h):
        return q_ref[:, h * HEAD : (h + 1) * HEAD]

    def fixed(keys, values, bias):
        raw = scores(query(0), keys)
        for h in range(heads):
            ahead = scores(query(h + 1), keys) if h + 1 < heads else None
            weights = jnp.exp2(biased(raw, bias) - wide(peak_ref[h], keys.shape[0]))
            acc_ref[h] += dot(weights.astype(jnp.bfloat16), values)
            raw = ahead

    for h in range(heads):
        start(h, query(h))

    @pl.loop(0, masked)
    def _(tile):
        fixed(*read(tile, True, True))

    if tiles is not None:

        @pl.loop(masked, tiles)
        def _(tile):
            fixed(*read(tile, False, True))

    largest = jnp.max(acc_ref[:, :, HEAD:])

    @pl.when(jnp.logical_not(largest < LIMIT))
    def _():
        @pl.loop(0, heads)
        def _(h):
            query = q_ref[:, pl.ds(pl.multiple_of(h * HEAD, HEAD), HEAD)]
            start(h, query)

            @pl.loop(0, masked if tiles is None else tiles)
            def _(tile):
                moving(acc_ref, peak_ref, h, query, *read(tile, True, False))


def tile_of(ref, at):
    rows = pl.ds(pl.multiple_of(at * TILE, TILE), TILE)
    return ref[rows, :HEAD], widened(ref[rows, HEAD:])


def bias_where(allowed):
    return jnp.where(allowed, 0.0, NEGATIVE)


def own_row_kernel(place_ref, q_ref, k_ref, v_ref, row_ref, acc_ref, peak_ref, bias_ref):
    keys = place_ref[0] % WIDE * KEEP
    start = functools.partial(local, k_ref, v_ref, acc_ref, peak_ref)

    def read(tile, masked, first_time):
        bias_ref[...] = bias_where(count_along(bias_ref.shape, 1) + tile * TILE < keys)
        return *tile_of(row_ref, tile), bias_ref[...]

    absorb(q_ref, acc_ref, peak_ref, start, (keys + TILE - 1) // TILE, None, read)


def rest_kernel(
    place_ref, q_ref, row_ref, below_ref, above_ref, below2_ref, above2_ref, rest_ref,
    acc_in, peak_in, out_ref, bank_ref, bias_ref, acc_ref, peak_ref, sems,
):
    mine, used = place_ref[0], place_ref[1]
    y = mine // WIDE
    span = WIDE * KEEP
    row_tiles = span // TILE
    copies = []

    def copy(source, at, rows, condition, tile):
        target = bank_ref.at[pl.ds(at, rows)]
        one = pltpu.make_async_copy(source, target, sems.at[len(copies)])
        copies.append((one, condition, tile))

    for row, ref in enumerate((row_ref, below_ref, below2_ref, above_ref)):
        copy(ref.at[pl.ds(0, KEEP)], 0, KEEP, (mine > 0) & (y == row), 0)
    copy(below_ref, TILE, span, y > 0, 1)
    copy(below2_ref, TILE + span, span // 2, y > 1, 1 + row_tiles)
    copy(above2_ref, TILE + span + span // 2, span // 2, y > 1, 1 + row_tiles)
    copy(above_ref, TILE + 2 * span, span, y == 3, 1 + 2 * row_tiles)
    for one, condition, _ in copies:
        pl.when(condition)(one.start)
    bank_ref[KEEP:TILE] = rest_ref[: TILE - KEEP]
    number = wide(rest_ref[TILE - KEEP : TILE - KEEP + 1, :HEAD].astype(jnp.int32), TILE)
    at = count_along((1, TILE), 1)
    limit = jnp.where(at < KEEP, number, KEEP + used - number)
    bias_ref[0] = jnp.broadcast_to(bias_where(at < limit), bias_ref.shape[1:])
    bias_ref[1] = jnp.zeros(bias_ref.shape[1:], jnp.float32)

    def start(h, query):
        acc_ref[h] = acc_in[h]
        peak_ref[h] = peak_in[h]

    def read(tile, masked, first_time):
        if first_time:
            for one, condition, when in copies:
                if masked == (when == 0):
                    pl.when(condition & (tile == when))(one.wait)
        bias = bias_ref[jnp.minimum(tile, 1)] if masked else None
        return *tile_of(bank_ref, tile), bias

    masked = jnp.where(mine > 0, 1, 0)
    absorb(q_ref, acc_ref, peak_ref, start, masked, masked + row_tiles * y, read)
    for h in range(acc_ref.shape[0]):
        out_ref[:, h * HEAD : (h + 1) * HEAD] = (
            acc_ref[h, :, :HEAD] / acc_ref[h, :, HEAD:]
        ).astype(jnp.bfloat16)


def pack_row_kernel(place_ref, *refs):
    out_ref = refs[-1]
    z = place_ref[0] % WIDE
    at = KEEP
    for ref in refs[:-1]:
        rows = ref.shape[0]
        start = pl.multiple_of(lax.rem(z * KEEP + at, WIDE * KEEP), KEEP // 2)
        out_ref[pl.ds(start, rows)] = ref[...]
        at += rows


def pack_row(place, pieces):
    return pl.pallas_call(
        pack_row_kernel,
        out_shape=jax.ShapeDtypeStruct((WIDE * KEEP, 2 * HEAD), jnp.bfloat16),
        in_specs=[SMEM] + [VMEM] * len(pieces),
        out_specs=VMEM,
        compiler_params=pltpu.CompilerParams(vmem_limit_bytes=8 * 2**20),
        name="pack_row",
    )(place, *pieces)


def cost(rows, keys):
    return pl.CostEstimate(
        flops=rows * keys * HEAD * 8, bytes_accessed=8 * 2**20, transcendentals=rows * keys
    )


def state_of(length, heads):
    return [
        jax.ShapeDtypeStruct((heads, length, 2 * HEAD), jnp.float32),
        jax.ShapeDtypeStruct((heads, length, HEAD), jnp.float32),
    ]


def own_row(place, queries, keys, values, row, parts):
    length, width = queries.shape
    rows, heads = length // parts, width // HEAD
    whole = lambda x: pl.BlockSpec(x.shape, lambda i: (0,) * x.ndim)
    slab = lambda columns: pl.BlockSpec((heads, rows, columns), lambda i: (0, i, 0))
    return pl.pallas_call(
        own_row_kernel,
        grid=(parts,),
        out_shape=state_of(length, heads),
        in_specs=[
            SMEM,
            pl.BlockSpec((rows, width), lambda i: (i, 0)),
            *[whole(x) for x in (keys, values, row)],
        ],
        out_specs=[slab(2 * HEAD), slab(HEAD)],
        scratch_shapes=[pltpu.VMEM((8, TILE), jnp.float32)],
        compiler_params=PARAMS,
        cost_estimate=cost(length * heads, length + WIDE * KEEP),
        name="own_row",
    )(place, queries, keys, values, row)


def rest_rows(place, queries, banks, rest, state, part, parts):
    length, width = queries.shape
    rows, heads = length // parts, width // HEAD
    tiles = 13
    slab = lambda columns: pl.BlockSpec((heads, rows, columns), lambda i: (0, part, 0))
    return pl.pallas_call(
        rest_kernel,
        grid=(1,),
        out_shape=jax.ShapeDtypeStruct((rows, width), jnp.bfloat16),
        in_specs=[
            SMEM,
            pl.BlockSpec((rows, width), lambda i: (part, 0)),
            *[ANY] * len(banks),
            pl.BlockSpec(rest.shape, lambda i: (0, 0)),
            slab(2 * HEAD),
            slab(HEAD),
        ],
        out_specs=pl.BlockSpec((rows, width), lambda i: (0, 0)),
        scratch_shapes=[
            pltpu.VMEM((tiles * TILE, 2 * HEAD), jnp.bfloat16),
            pltpu.VMEM((2, 8, TILE), jnp.float32),
            pltpu.VMEM((heads, rows, 2 * HEAD), jnp.float32),
            pltpu.VMEM((heads, rows, HEAD), jnp.float32),
            pltpu.SemaphoreType.DMA((8,)),
        ],
        compiler_params=PARAMS,
        cost_estimate=cost(rows * heads, tiles * TILE),
        name=f"rest_rows_{part}",
    )(place, queries, *banks, rest, *state)


def project_kernel(place_ref, own_ref, other_ref, weight_ref, other_w_ref, out_ref):
    total = dot(own_ref[...], weight_ref[...]) + dot(other_ref[...], other_w_ref[...])
    out_ref[...] = total.astype(jnp.bfloat16)


def project(place, own, other, weight, other_w):
    chips, rows, columns = other_w.shape
    chip = lambda i, place: lax.rem(place[0] + i, chips)
    whole = pl.BlockSpec(own.shape, lambda i, place: (0, 0))
    return pl.pallas_call(
        project_kernel,
        grid_spec=pltpu.PrefetchScalarGridSpec(
            num_scalar_prefetch=1,
            grid=(chips,),
            in_specs=[
                whole,
                whole,
                pl.BlockSpec((rows, columns), lambda i, place: (0, 2 * chip(i, place) + place[1])),
                pl.BlockSpec((None, rows, columns), lambda i, place: (chip(i, place), 0, 0)),
            ],
            out_specs=pl.BlockSpec((None, own.shape[0], columns), lambda i, place: (i, 0, 0)),
        ),
        out_shape=jax.ShapeDtypeStruct((chips, own.shape[0], columns), jnp.bfloat16),
        compiler_params=PARAMS,
        cost_estimate=pl.CostEstimate(
            flops=4 * own.size * chips * columns, bytes_accessed=8 * 2**20, transcendentals=0
        ),
        name="project",
    )(place, own, other, weight, other_w)


def weight_kernel(place_ref, weight_ref, out_ref):
    columns = out_ref.shape[2]
    start = pl.multiple_of((1 - place_ref[1]) * columns, columns)
    out_ref[0] = weight_ref[:, pl.ds(start, columns)]


def weight_half(place, weight, chips):
    rows, columns = weight.shape[0], weight.shape[1] // chips // 2
    return pl.pallas_call(
        weight_kernel,
        grid=(chips,),
        out_shape=jax.ShapeDtypeStruct((chips, rows, columns), weight.dtype),
        in_specs=[SMEM, pl.BlockSpec((rows, 2 * columns), lambda i: (0, i))],
        out_specs=pl.BlockSpec((1, rows, columns), lambda i: (i, 0, 0)),
        compiler_params=PARAMS,
        cost_estimate=pl.CostEstimate(flops=0, bytes_accessed=6 * 2**20, transcendentals=0),
        name="weight_half",
    )(place, weight)


def added(*terms):
    return sum(term.astype(jnp.float32) for term in terms).astype(jnp.bfloat16)


def on_device(queries, key_rows, value_rows, kept_positions, anchor_length, output_weight):
    mine, head = lax.axis_index("ctx"), lax.axis_index("head")
    length, devices, blocks = queries.shape[0], lax.axis_size("head"), lax.axis_size("ctx")
    chips, chip, core = devices // 2, head // 2, head % 2
    tall = blocks // WIDE
    swap = [(i, i ^ 1) for i in range(devices)]
    up = [(i, (i + 2) % devices) for i in range(devices)]
    down = [(i, (i - 2) % devices) for i in range(devices)]
    along = lambda step: [
        (r * WIDE + c, r * WIDE + (c + step) % WIDE) for r in range(tall) for c in range(WIDE)
    ]
    across = lambda hops: [(a * WIDE + c, b * WIDE + c) for a, b in hops for c in range(WIDE)]
    permute = lambda x, pairs: lax.ppermute(x, "ctx", pairs)

    place = jnp.concatenate([mine.astype(jnp.int32)[None], anchor_length])
    spot = jnp.stack([chip, core]).astype(jnp.int32)
    kept, rest = select(anchor_length, kept_positions, key_rows, value_rows)

    plus, minus = along(1), along(-1)
    half = KEEP // 2
    left, right = [kept], [kept]
    rest = jnp.where(mine == 0, rest, jnp.zeros_like(rest))
    upward = [[(0, WIDE)], [(0, 3 * WIDE), (WIDE, 2 * WIDE)]]
    for step in range(WIDE // 2 - 1):
        left.append(permute(left[-1], plus))
        right.append(permute(right[-1], minus))
        if step < len(upward):
            rest = rest + permute(rest, upward[step])
            left[-1], right[-1], rest = lax.optimization_barrier((left[-1], right[-1], rest))
    opposite = [permute(left[-1][:half], plus), permute(right[-1][half:], minus)]
    row = pack_row(place, right[1:] + opposite + left[:0:-1] + [kept])

    below = permute(row, across([(0, 1), (1, 2), (2, 3)]))
    above = permute(row, across([(0, 3), (1, 0)]))
    half_w = weight_half(spot, output_weight, chips)
    below, half_w = lax.optimization_barrier((below, half_w))
    middle = row.shape[0] // 2
    below2 = permute(below[:middle], across([(1, 2), (2, 3)]))
    above2 = permute(above[middle:], across([(0, 3), (3, 2)]))

    rest, row = lax.optimization_barrier((rest, row))
    chain = lambda hops: [(r * WIDE + a, r * WIDE + b) for a, b in hops for r in range(tall)]
    for hops in ([(0, 1)], [(0, 7), (1, 2)], [(7, 6), (2, 3)], [(6, 5), (3, 4)]):
        rest = rest + permute(rest, chain(hops))

    other_w = lax.ppermute(half_w, "head", swap)

    parts = 2
    state = own_row(place, queries, key_rows, value_rows, row, parts)
    banks = (row, below, above, below2, above2)

    outs = []
    rows_each = length // parts
    half = rows_each // 2
    for part in range(parts):
        own = rest_rows(place, queries, banks, rest, state, part, parts)
        other = lax.ppermute(own, "head", swap)
        terms = project(spot, own, other, output_weight, other_w)
        from_below = lax.ppermute(terms[2, :half], "head", up)
        from_above = lax.ppermute(terms[2, half:], "head", down)
        upward = jnp.concatenate([added(terms[1, :half], from_below), terms[1, half:]])
        downward = jnp.concatenate([terms[3, :half], added(terms[3, half:], from_above)])
        outs.append(
            added(terms[0], lax.ppermute(upward, "head", up), lax.ppermute(downward, "head", down))
        )
    return jnp.concatenate(outs)


def solution(mesh):
    placed = (
        P("ctx", "head"),
        P("ctx", "head"),
        P("ctx", "head"),
        P("head", "ctx"),
        P("head"),
        P("head", None),
    )
    return jax.shard_map(
        on_device, mesh=mesh, in_specs=placed, out_specs=P("ctx", "head"), check_vma=False
    )
```

```python
import functools

import jax
import jax.numpy as jnp
from jax import lax
from jax.experimental import pallas as pl
from jax.experimental.pallas import tpu as pltpu
from jax.sharding import PartitionSpec as P

HEAD = 128
WIDE = 8
INFO = 16
KEEP = 256
LOG2E = 1.4426950408889634
FACTOR = HEAD**-0.5 * LOG2E
LIMIT = 2.0**100
NEGATIVE = -1e30
NT = (((1,), (1,)), ((), ()))
VMEM = pl.BlockSpec(memory_space=pltpu.VMEM)
SMEM = pl.BlockSpec(memory_space=pltpu.SMEM)
HBM = pl.BlockSpec(memory_space=pltpu.HBM)
ANY = pl.BlockSpec(memory_space=pl.ANY)
TILE = 512
CHUNK = 512
PARAMS = pltpu.CompilerParams(vmem_limit_bytes=60 * 2**20)


def dot(a, b):
    return jnp.dot(a, b, preferred_element_type=jnp.float32)


def dot_nt(a, b):
    return lax.dot_general(a, b, NT, preferred_element_type=jnp.float32)


def count_along(shape, dim):
    return lax.broadcasted_iota(jnp.int32, shape, dim)


def ones_where(condition):
    return jnp.where(condition, 1.0, 0.0).astype(jnp.bfloat16)


def select_kernel(used_ref, *refs):
    sources, (kept_rows_ref, rest_ref), targets, sems = refs[:3], refs[3:5], refs[5:8], refs[8]
    copies = [
        pltpu.make_async_copy(source, target, sems.at[at])
        for at, (source, target) in enumerate(zip(sources, targets))
    ]
    for copy in copies:
        copy.start()
    for copy in copies:
        copy.wait()
    kept_ref, key_ref, value_ref = targets
    length, keep = key_ref.shape[0], kept_ref.shape[1]
    hit = ones_where(count_along((length, keep), 0) == kept_ref[...])
    kept = dot_nt(jnp.ones((8, keep), jnp.bfloat16), hit)
    square = (length, length)
    before = ones_where(count_along(square, 0) < count_along(square, 1))
    rank = dot(kept.astype(jnp.bfloat16), before)
    column = count_along((8, length), 1)
    place = jnp.where(kept > 0.5, rank, column.astype(jnp.float32) + keep - rank)
    order = ones_where(count_along(square, 0).astype(jnp.float32) == place[:1])
    for at, ref in enumerate((key_ref, value_ref)):
        columns = slice(at * HEAD, (at + 1) * HEAD)
        rows = dot(order, ref[...]).astype(jnp.bfloat16)
        kept_rows_ref[:, columns] = rows[:keep]
        rest_ref[: length - keep, columns] = rows[keep:]
    in_both = jnp.where((kept > 0.5) & (column < used_ref[0]), 1.0, 0.0)[:1]
    number = jnp.sum(in_both, axis=1, keepdims=True)
    rest_ref[length - keep :] = jnp.broadcast_to(number, (INFO, 2 * HEAD)).astype(jnp.bfloat16)


def select(used, kept, keys, values):
    length = keys.shape[0]
    rows = (KEEP, length - KEEP + INFO)
    return pl.pallas_call(
        select_kernel,
        out_shape=[jax.ShapeDtypeStruct((n, 2 * HEAD), jnp.bfloat16) for n in rows],
        in_specs=[SMEM, HBM, HBM, HBM],
        out_specs=[VMEM] * 2,
        scratch_shapes=[
            *[pltpu.VMEM(x.shape, x.dtype) for x in (kept, keys, values)],
            pltpu.SemaphoreType.DMA((3,)),
        ],
        compiler_params=PARAMS,
        name="select_kept",
    )(used, kept, keys, values)


def wide(column, width):
    return jnp.concatenate([column] * (width // HEAD), axis=1)


def widened(values):
    return jnp.concatenate([values, jnp.ones_like(values)], axis=1)


def scores(query, keys):
    return dot_nt(query, keys) * FACTOR


def local(query, keys, values, acc_ref, peak_ref):
    length = query.shape[0]
    causal = count_along((length, length), 1) <= count_along((length, length), 0)
    raw = jnp.where(causal, scores(query, keys), NEGATIVE)
    peak = jnp.broadcast_to(jnp.max(raw, axis=1, keepdims=True), (length, HEAD))
    peak_ref[...] = peak
    weights = jnp.exp2(raw - wide(peak, length)).astype(jnp.bfloat16)
    acc_ref[...] = dot(weights, widened(values))


def biased(raw, bias):
    if bias is None:
        return raw
    return (raw.reshape(-1, *bias.shape) + bias).reshape(raw.shape)


def fixed(query, acc_ref, peak_ref, keys, values, bias):
    raw = biased(scores(query, keys), bias)
    weights = jnp.exp2(raw - wide(peak_ref[...], keys.shape[0]))
    acc_ref[...] += dot(weights.astype(jnp.bfloat16), values)


def moving(query, acc_ref, peak_ref, keys, values, bias):
    raw = biased(scores(query, keys), bias)
    old = peak_ref[...]
    peak = jnp.maximum(old, jnp.max(raw, axis=1, keepdims=True))
    weights = jnp.exp2(raw - wide(peak, keys.shape[0])).astype(jnp.bfloat16)
    peak_ref[...] = peak
    acc_ref[...] = acc_ref[...] * wide(jnp.exp2(old - peak), 2 * HEAD) + dot(weights, values)


def absorb(acc_ref, chunks, view, start, masked, tiles, read):
    for c in range(chunks):
        start(c)

    @pl.loop(0, masked)
    def _(tile):
        keys = read(tile, True, True)
        for c in range(chunks):
            fixed(*view(c), *keys)

    @pl.loop(masked, tiles)
    def _(tile):
        keys = read(tile, False, True)
        for c in range(chunks):
            fixed(*view(c), *keys)

    largest = jnp.max(acc_ref[..., HEAD:])

    @pl.when(jnp.logical_not(largest < LIMIT))
    def _():
        @pl.loop(0, chunks)
        def _(c):
            start(c)

            @pl.loop(0, tiles)
            def _(tile):
                moving(*view(c), *read(tile, True, False))


def tile_of(ref, at):
    rows = pl.ds(pl.multiple_of(at * TILE, TILE), TILE)
    return ref[rows, :HEAD], widened(ref[rows, HEAD:])


def bias_where(allowed):
    return jnp.where(allowed, 0.0, NEGATIVE)


def own_row_kernel(
    place_ref, q_ref, k_ref, v_ref, row_a, row_b, acc_ref, peak_ref, row_ref, bias_ref, sems
):
    keys = place_ref[0] % WIDE * KEEP
    masked = jnp.where(keys % TILE > 0, 1, 0)
    tiles = (keys + TILE - 1) // TILE
    half = row_a.shape[0]
    copies = [
        pltpu.make_async_copy(ref, row_ref.at[pl.ds(at * half, half)], sems.at[at])
        for at, ref in enumerate((row_a, row_b))
    ]

    @pl.when(tiles > 0)
    def _():
        for copy in copies:
            copy.start()

    def view(c):
        columns = pl.ds(pl.multiple_of(c * HEAD, HEAD), HEAD)
        return q_ref[:, columns], acc_ref.at[c], peak_ref.at[c]

    def start(c):
        query, acc, peak = view(c)
        local(query, k_ref[...], v_ref[...], acc, peak)

    def read(tile, with_bias, first_time):
        if first_time:

            @pl.when(tile == 0)
            def _():
                for copy in copies:
                    copy.wait()

        at = jnp.where(tile < masked, tiles - 1, tile - masked)
        if not with_bias:
            return *tile_of(row_ref, at), None
        bias_ref[...] = bias_where(count_along(bias_ref.shape, 1) + at * TILE < keys)
        return *tile_of(row_ref, at), bias_ref[...]

    absorb(acc_ref, acc_ref.shape[0], view, start, masked, tiles, read)


def rest_kernel(
    place_ref, q_ref, rest_ref, row_ref, below_a, below_b, above_a, above_b, below2_ref,
    above2_ref, weight_ref, acc_in, peak_in, keep_ref, send_ref, bank_ref, w_ref, bias_ref,
    stack_ref, acc_ref, peak_ref, att_ref, sems,
):
    mine, used = place_ref[0], place_ref[1]
    y, tokens, heads = mine // WIDE, q_ref.shape[0], acc_in.shape[0]
    span = WIDE * KEEP
    part, row_tiles = span // 2, span // TILE
    copies = []

    def copy(source, at, rows, condition, tile):
        target = bank_ref.at[pl.ds(at, rows)]
        one = pltpu.make_async_copy(source, target, sems.at[len(copies)])
        copies.append((one, condition, tile))

    for row, ref in enumerate((row_ref, below_a, below2_ref, above_a)):
        copy(ref.at[pl.ds(0, KEEP)], 0, KEEP, (mine > 0) & (y == row), 0)
    at, tile = TILE, 1
    for condition, first, second in (
        (y > 0, below_a, below_b),
        (y > 1, below2_ref, above2_ref),
        (y == 3, above_a, above_b),
    ):
        copy(first, at, part, condition, tile)
        copy(second, at + part, part, condition, tile)
        at, tile = at + span, tile + row_tiles
    for one, condition, _ in copies:
        pl.when(condition)(one.start)
    weight_copy = pltpu.make_async_copy(weight_ref, w_ref, sems.at[len(copies)])
    weight_copy.start()
    bank_ref[KEEP:TILE] = rest_ref[: TILE - KEEP]
    number = wide(rest_ref[TILE - KEEP : TILE - KEEP + 1, :HEAD].astype(jnp.int32), TILE)
    at = count_along((1, TILE), 1)
    limit = jnp.where(at < KEEP, number, KEEP + used - number)
    bias_ref[0] = jnp.broadcast_to(bias_where(at < limit), bias_ref.shape[1:])
    bias_ref[1] = jnp.zeros(bias_ref.shape[1:], jnp.float32)
    for h in range(heads):
        stack_ref[h * tokens : (h + 1) * tokens] = q_ref[:, h * HEAD : (h + 1) * HEAD]
    together = CHUNK // tokens

    def view(c):
        rows = pl.ds(pl.multiple_of(c * CHUNK, CHUNK), CHUNK)
        return stack_ref[rows], acc_ref.at[rows], peak_ref.at[rows]

    def start(c):
        for h in range(together):
            rows = pl.ds(pl.multiple_of((c * together + h) * tokens, tokens), tokens)
            acc_ref[rows] = acc_in[c * together + h]
            peak_ref[rows] = peak_in[c * together + h]

    def read(tile, masked, first_time):
        if first_time:
            for one, condition, when in copies:
                if masked == (when == 0):
                    pl.when(condition & (tile == when))(one.wait)
        bias = bias_ref[jnp.minimum(tile, 1)] if masked else None
        return *tile_of(bank_ref, tile), bias

    masked = jnp.where(mine > 0, 1, 0)
    chunks = heads // together
    absorb(acc_ref, chunks, view, start, masked, masked + row_tiles * y, read)
    for h in range(heads):
        rows = slice(h * tokens, (h + 1) * tokens)
        att_ref[:, h * HEAD : (h + 1) * HEAD] = (
            acc_ref[rows, :HEAD] / acc_ref[rows, HEAD:]
        ).astype(jnp.bfloat16)
    weight_copy.wait()
    chips, _, columns = keep_ref.shape
    chip, core = place_ref[2], place_ref[3]

    @pl.loop(0, chips)
    def _(step):
        at = lax.rem(chip + step, chips) * 2
        for ref, side in ((keep_ref, core), (send_ref, 1 - core)):
            start = pl.multiple_of((at + side) * columns, columns)
            ref[step] = dot(att_ref[...], w_ref[:, pl.ds(start, columns)]).astype(jnp.bfloat16)


def pack_row_kernel(place_ref, *refs):
    z = place_ref[0] % WIDE
    at, middle = KEEP, WIDE * KEEP // 2
    for ref in refs[:-2]:
        rows = ref.shape[0]
        start = pl.multiple_of(lax.rem(z * KEEP + at, WIDE * KEEP), KEEP // 2)
        at += rows
        for out_ref, first in zip(refs[-2:], (0, middle)):

            @pl.when((start >= first) & (start < first + middle))
            def _():
                out_ref[pl.ds(pl.multiple_of(start - first, KEEP // 2), rows)] = ref[...]


def pack_row(place, pieces):
    return pl.pallas_call(
        pack_row_kernel,
        out_shape=[jax.ShapeDtypeStruct((WIDE * KEEP // 2, 2 * HEAD), jnp.bfloat16)] * 2,
        in_specs=[SMEM] + [VMEM] * len(pieces),
        out_specs=[VMEM] * 2,
        compiler_params=pltpu.CompilerParams(vmem_limit_bytes=8 * 2**20),
        name="pack_row",
    )(place, *pieces)


def cost(rows, keys):
    return pl.CostEstimate(
        flops=rows * keys * HEAD * 8, bytes_accessed=8 * 2**20, transcendentals=rows * keys
    )


def state_of(length, heads):
    return [
        jax.ShapeDtypeStruct((heads, length, 2 * HEAD), jnp.float32),
        jax.ShapeDtypeStruct((heads, length, HEAD), jnp.float32),
    ]


def own_row(place, queries, keys, values, row_a, row_b):
    length, width = queries.shape
    whole = lambda x: pl.BlockSpec(x.shape, lambda i: (0,) * x.ndim)
    state = state_of(length, width // HEAD)
    return pl.pallas_call(
        own_row_kernel,
        grid=(1,),
        out_shape=state,
        in_specs=[SMEM, *[whole(x) for x in (queries, keys, values)], ANY, ANY],
        out_specs=[whole(x) for x in state],
        scratch_shapes=[
            pltpu.VMEM((WIDE * KEEP, 2 * HEAD), jnp.bfloat16),
            pltpu.VMEM((8, TILE), jnp.float32),
            pltpu.SemaphoreType.DMA((2,)),
        ],
        compiler_params=PARAMS,
        cost_estimate=cost(length * width // HEAD, length + WIDE * KEEP),
        name="own_row",
    )(place, queries, keys, values, row_a, row_b)


def rest_rows(place, queries, rest, banks, weight, state, part, parts, chips):
    length, width = queries.shape
    rows, heads = length // parts, width // HEAD
    tiles = 13
    slab = lambda columns: pl.BlockSpec((heads, rows, columns), lambda i: (0, part, 0))
    out = jax.ShapeDtypeStruct((chips, rows, weight.shape[1] // chips // 2), jnp.bfloat16)
    return pl.pallas_call(
        rest_kernel,
        grid=(1,),
        out_shape=[out, out],
        in_specs=[
            SMEM,
            pl.BlockSpec((rows, width), lambda i: (part, 0)),
            pl.BlockSpec(rest.shape, lambda i: (0, 0)),
            *[ANY] * (len(banks) + 1),
            slab(2 * HEAD),
            slab(HEAD),
        ],
        out_specs=[pl.BlockSpec(out.shape, lambda i: (0, 0, 0))] * 2,
        scratch_shapes=[
            pltpu.VMEM((tiles * TILE, 2 * HEAD), jnp.bfloat16),
            pltpu.VMEM(weight.shape, weight.dtype),
            pltpu.VMEM((2, 8, TILE), jnp.float32),
            pltpu.VMEM((heads * rows, HEAD), jnp.bfloat16),
            pltpu.VMEM((heads * rows, 2 * HEAD), jnp.float32),
            pltpu.VMEM((heads * rows, HEAD), jnp.float32),
            pltpu.VMEM((rows, width), jnp.bfloat16),
            pltpu.SemaphoreType.DMA((11,)),
        ],
        compiler_params=PARAMS,
        cost_estimate=cost(rows * heads, tiles * TILE),
        name=f"rest_rows_{part}",
    )(place, queries, rest, *banks, weight, *state)


def added(*terms):
    return sum(term.astype(jnp.float32) for term in terms).astype(jnp.bfloat16)


def on_device(queries, key_rows, value_rows, kept_positions, anchor_length, output_weight):
    mine, head = lax.axis_index("ctx"), lax.axis_index("head")
    length, devices, blocks = queries.shape[0], lax.axis_size("head"), lax.axis_size("ctx")
    chips, chip, core = devices // 2, head // 2, head % 2
    tall = blocks // WIDE
    swap = [(i, i ^ 1) for i in range(devices)]
    up = [(i, (i + 2) % devices) for i in range(devices)]
    down = [(i, (i - 2) % devices) for i in range(devices)]
    along = lambda step: [
        (r * WIDE + c, r * WIDE + (c + step) % WIDE) for r in range(tall) for c in range(WIDE)
    ]
    across = lambda hops: [(a * WIDE + c, b * WIDE + c) for a, b in hops for c in range(WIDE)]
    permute = lambda x, pairs: lax.ppermute(x, "ctx", pairs)

    spots = jnp.stack([chip, core]).astype(jnp.int32)
    place = jnp.concatenate([mine.astype(jnp.int32)[None], anchor_length, spots])
    kept, rest = select(anchor_length, kept_positions, key_rows, value_rows)

    plus, minus = along(1), along(-1)
    half = KEEP // 2
    left, right = [kept], [kept]
    rest = jnp.where(mine == 0, rest, jnp.zeros_like(rest))
    upward = [[(0, WIDE)], [(0, 3 * WIDE), (WIDE, 2 * WIDE)]]
    for step in range(WIDE // 2 - 1):
        left.append(permute(left[-1], plus))
        right.append(permute(right[-1], minus))
        if step < len(upward):
            rest = rest + permute(rest, upward[step])
            left[-1], right[-1], rest = lax.optimization_barrier((left[-1], right[-1], rest))
    opposite = [permute(left[-1][:half], plus), permute(right[-1][half:], minus)]
    ends = pack_row(place, right[1:] + opposite + left[:0:-1] + [kept])

    below_a = permute(ends[0], across([(0, 1), (1, 2), (2, 3)]))
    above_b = permute(ends[1], across([(0, 3), (1, 0)]))
    below_b = permute(ends[1], across([(0, 1), (1, 2), (2, 3)]))
    above_a = permute(ends[0], across([(0, 3)]))

    rest, ends = lax.optimization_barrier((rest, ends))
    spread = lambda hops: [(r * WIDE + a, r * WIDE + b) for a, b in hops for r in range(tall)]
    rest = rest + permute(rest, spread([(0, 4)]))
    rest, below_a, above_b = lax.optimization_barrier((rest, below_a, above_b))
    below2 = permute(below_a, across([(1, 2), (2, 3)]))
    above2 = permute(above_b, across([(0, 3), (3, 2)]))
    rest = rest + permute(rest, spread([(0, 2), (4, 6)]))
    rest = rest + permute(rest, spread([(0, 1), (2, 3), (4, 5), (6, 7)]))

    parts = 2
    state = own_row(place, queries, key_rows, value_rows, *ends)
    banks = (ends[0], below_a, below_b, above_a, above_b, below2, above2)

    outs = []
    half = length // parts // 2
    for part in range(parts):
        own, send = rest_rows(
            place, queries, rest, banks, output_weight, state, part, parts, chips
        )
        other = lax.ppermute(send, "head", swap)
        across_x = added(own[2], other[2])
        from_below = lax.ppermute(across_x[:half], "head", up)
        from_above = lax.ppermute(across_x[half:], "head", down)
        upward = jnp.concatenate(
            [added(own[1, :half], other[1, :half], from_below), added(own[1, half:], other[1, half:])]
        )
        downward = jnp.concatenate(
            [added(own[3, :half], other[3, :half]), added(own[3, half:], other[3, half:], from_above)]
        )
        upward, downward = lax.ppermute(upward, "head", up), lax.ppermute(downward, "head", down)
        outs.append(added(own[0], other[0], upward, downward))
    return jnp.concatenate(outs)


def solution(mesh):
    placed = (
        P("ctx", "head"),
        P("ctx", "head"),
        P("ctx", "head"),
        P("head", "ctx"),
        P("head"),
        P("head", None),
    )
    return jax.shard_map(
        on_device, mesh=mesh, in_specs=placed, out_specs=P("ctx", "head"), check_vma=False
    )
```

```python
import functools

import jax
import jax.numpy as jnp
from jax import lax
from jax.experimental import pallas as pl
from jax.experimental.pallas import tpu as pltpu
from jax.sharding import PartitionSpec as P

HEAD = 128
WIDE = 8
INFO = 16
KEEP = 256
LOG2E = 1.4426950408889634
FACTOR = HEAD**-0.5 * LOG2E
LIMIT = 2.0**100
NEGATIVE = -1e30
NT = (((1,), (1,)), ((), ()))
VMEM = pl.BlockSpec(memory_space=pltpu.VMEM)
SMEM = pl.BlockSpec(memory_space=pltpu.SMEM)
HBM = pl.BlockSpec(memory_space=pltpu.HBM)
ANY = pl.BlockSpec(memory_space=pl.ANY)
TILE = 512
STEP = 1024
PARAMS = pltpu.CompilerParams(vmem_limit_bytes=60 * 2**20)


def dot(a, b):
    return jnp.dot(a, b, preferred_element_type=jnp.float32)


def dot_nt(a, b):
    return lax.dot_general(a, b, NT, preferred_element_type=jnp.float32)


def count_along(shape, dim):
    return lax.broadcasted_iota(jnp.int32, shape, dim)


def ones_where(condition):
    return jnp.where(condition, 1.0, 0.0).astype(jnp.bfloat16)


def select_kernel(used_ref, *refs):
    sources, (kept_rows_ref, rest_ref), targets, sems = refs[:3], refs[3:5], refs[5:8], refs[8]
    copies = [
        pltpu.make_async_copy(source, target, sems.at[at])
        for at, (source, target) in enumerate(zip(sources, targets))
    ]
    for copy in copies:
        copy.start()
    for copy in copies:
        copy.wait()
    kept_ref, key_ref, value_ref = targets
    length, keep = key_ref.shape[0], kept_ref.shape[1]
    hit = ones_where(count_along((length, keep), 0) == kept_ref[...])
    kept = dot_nt(jnp.ones((8, keep), jnp.bfloat16), hit)
    square = (length, length)
    before = ones_where(count_along(square, 0) < count_along(square, 1))
    rank = dot(kept.astype(jnp.bfloat16), before)
    column = count_along((8, length), 1)
    place = jnp.where(kept > 0.5, rank, column.astype(jnp.float32) + keep - rank)
    order = ones_where(count_along(square, 0).astype(jnp.float32) == place[:1])
    for at, ref in enumerate((key_ref, value_ref)):
        columns = slice(at * HEAD, (at + 1) * HEAD)
        rows = dot(order, ref[...]).astype(jnp.bfloat16)
        kept_rows_ref[:, columns] = rows[:keep]
        rest_ref[: length - keep, columns] = rows[keep:]
    in_both = jnp.where((kept > 0.5) & (column < used_ref[0]), 1.0, 0.0)[:1]
    number = jnp.sum(in_both, axis=1, keepdims=True)
    rest_ref[length - keep :] = jnp.broadcast_to(number, (INFO, 2 * HEAD)).astype(jnp.bfloat16)


def select(used, kept, keys, values):
    length = keys.shape[0]
    rows = (KEEP, length - KEEP + INFO)
    return pl.pallas_call(
        select_kernel,
        out_shape=[jax.ShapeDtypeStruct((n, 2 * HEAD), jnp.bfloat16) for n in rows],
        in_specs=[SMEM, HBM, HBM, HBM],
        out_specs=[VMEM] * 2,
        scratch_shapes=[
            *[pltpu.VMEM(x.shape, x.dtype) for x in (kept, keys, values)],
            pltpu.SemaphoreType.DMA((3,)),
        ],
        compiler_params=PARAMS,
        name="select_kept",
    )(used, kept, keys, values)


def wide(column, width):
    return jnp.concatenate([column] * (width // HEAD), axis=1)


def widened(values):
    return jnp.concatenate([values, jnp.ones_like(values)], axis=1)


def scores(query, keys):
    return dot_nt(query, keys) * FACTOR


def local(query, keys, values, acc_ref, peak_ref):
    length = query.shape[0]
    causal = count_along((length, length), 1) <= count_along((length, length), 0)
    raw = jnp.where(causal, scores(query, keys), NEGATIVE)
    peak = jnp.broadcast_to(jnp.max(raw, axis=1, keepdims=True), (length, HEAD))
    peak_ref[...] = peak
    weights = jnp.exp2(raw - wide(peak, length)).astype(jnp.bfloat16)
    acc_ref[...] = dot(weights, widened(values))


def biased(raw, bias):
    if bias is None:
        return raw
    return (raw.reshape(-1, *bias.shape) + bias).reshape(raw.shape)


def fixed(heads, view, keys, values, bias):
    raw = scores(view(0)[0], keys)
    for h in range(heads):
        _, acc_ref, peak_ref = view(h)
        ahead = scores(view(h + 1)[0], keys) if h + 1 < heads else None
        weights = jnp.exp2(biased(raw, bias) - wide(peak_ref[...], keys.shape[0]))
        acc_ref[...] += dot(weights.astype(jnp.bfloat16), values)
        raw = ahead


def moving(query, acc_ref, peak_ref, keys, values, bias):
    raw = biased(scores(query, keys), bias)
    old = peak_ref[...]
    peak = jnp.maximum(old, jnp.max(raw, axis=1, keepdims=True))
    weights = jnp.exp2(raw - wide(peak, keys.shape[0])).astype(jnp.bfloat16)
    peak_ref[...] = peak
    acc_ref[...] = acc_ref[...] * wide(jnp.exp2(old - peak), 2 * HEAD) + dot(weights, values)


def absorb(heads, view, masked, steps, read):
    @pl.loop(0, masked)
    def _(step):
        fixed(heads, view, *read(step, True))

    @pl.loop(0, steps)
    def _(step):
        fixed(heads, view, *read(step, False))


def absorb_again(acc_ref, view, start, tiles, read):
    largest = jnp.max(acc_ref[:, :, HEAD:])

    @pl.when(jnp.logical_not(largest < LIMIT))
    def _():
        @pl.loop(0, acc_ref.shape[0])
        def _(h):
            start(h)

            @pl.loop(0, tiles)
            def _(tile):
                moving(*view(h), *read(tile))


def tile_of(ref, start, size):
    rows = pl.ds(pl.multiple_of(start, TILE), size)
    return ref[rows, :HEAD], widened(ref[rows, HEAD:])


def head_view(q_ref, acc_ref, peak_ref):
    def view(h):
        columns = pl.ds(pl.multiple_of(h * HEAD, HEAD), HEAD)
        return q_ref[:, columns], acc_ref.at[h], peak_ref.at[h]

    return view


def bias_where(allowed):
    return jnp.where(allowed, 0.0, NEGATIVE)


def own_row_kernel(
    place_ref, q_ref, k_ref, v_ref, row_a, row_b, acc_ref, peak_ref, row_ref, bias_ref, sems
):
    keys = place_ref[0] % WIDE * KEEP
    tiles, part = keys // TILE, jnp.where(keys % TILE > 0, 1, 0)
    half = row_a.shape[0]
    copies = [
        pltpu.make_async_copy(ref, row_ref.at[pl.ds(at * half, half)], sems.at[at])
        for at, ref in enumerate((row_a, row_b))
    ]
    for copy in copies:
        copy.start()
    view, heads = head_view(q_ref, acc_ref, peak_ref), acc_ref.shape[0]

    def start(h):
        query, acc, peak = view(h)
        local(query, k_ref[...], v_ref[...], acc, peak)

    def read(tile):
        bias_ref[...] = bias_where(count_along(bias_ref.shape, 1) + tile * TILE < keys)
        return *tile_of(row_ref, tile * TILE, TILE), bias_ref[...]

    def read_fast(step, masked):
        return read(tiles) if masked else (*tile_of(row_ref, step * TILE, TILE), None)

    for h in range(heads):
        start(h)
    for copy in copies:
        copy.wait()
    absorb(heads, view, part, tiles, read_fast)
    absorb_again(acc_ref, view, start, tiles + part, read)


def rest_kernel(
    place_ref, q_ref, rest_ref, row_ref, below_a, below_b, above_a, above_b, below2_ref,
    above2_ref, weight_ref, acc_in, peak_in, *refs,
):
    outs, (bank_ref, w_ref, bias_ref, acc_ref, carried_ref, peak_ref, att_ref, sems) = (
        refs[:-8],
        refs[-8:],
    )
    mine, used = place_ref[0], place_ref[1]
    y, heads = mine // WIDE, acc_ref.shape[0]
    span = WIDE * KEEP
    part, row_steps = span // 2, span // STEP
    copies = []

    def copy(source, at, rows, condition, step):
        target = bank_ref.at[pl.ds(at, rows)]
        one = pltpu.make_async_copy(source, target, sems.at[len(copies)])
        copies.append((one, condition, step))

    for row, ref in enumerate((row_ref, below_a, below2_ref, above_a)):
        copy(ref.at[pl.ds(0, KEEP)], 0, KEEP, (mine > 0) & (y == row), None)
    at, step = TILE, 0
    for condition, first, second in (
        (y > 0, below_a, below_b),
        (y > 1, below2_ref, above2_ref),
        (y == 3, above_a, above_b),
    ):
        copy(first, at, part, condition, step)
        copy(second, at + part, part, condition, step)
        at, step = at + span, step + row_steps
    for one, condition, _ in copies:
        pl.when(condition)(one.start)
    whole = [
        pltpu.make_async_copy(source, target, sems.at[len(copies) + at])
        for at, (source, target) in enumerate(
            ((peak_in, peak_ref), (acc_in, carried_ref), (weight_ref, w_ref))
        )
    ]
    for one in whole:
        one.start()
    acc_ref[...] = jnp.zeros_like(acc_ref)
    bank_ref[KEEP:TILE] = rest_ref[: TILE - KEEP]
    number = wide(rest_ref[TILE - KEEP : TILE - KEEP + 1, :HEAD].astype(jnp.int32), TILE)
    at = count_along((1, TILE), 1)
    limit = jnp.where(at < KEEP, number, KEEP + used - number)
    bias_ref[0] = jnp.broadcast_to(bias_where(at < limit), bias_ref.shape[1:])
    bias_ref[1] = jnp.zeros(bias_ref.shape[1:], jnp.float32)
    view = head_view(q_ref, acc_ref, peak_ref)

    def start(h):
        acc_ref[h] = carried_ref[h]

    def read_fast(step, masked):
        for one, condition, when in copies:
            if masked and when is None:
                pl.when(condition)(one.wait)
            elif when is not None and not masked:
                pl.when(condition & (step == when))(one.wait)
        if masked:
            return read(0)
        return *tile_of(bank_ref, TILE + step * STEP, STEP), None

    def read(tile):
        return *tile_of(bank_ref, tile * TILE, TILE), bias_ref[jnp.minimum(tile, 1)]

    masked = jnp.where(mine > 0, 1, 0)
    whole[0].wait()
    absorb(heads, view, masked, row_steps * y, read_fast)
    whole[1].wait()
    acc_ref[...] += carried_ref[...]
    absorb_again(acc_ref, view, start, masked + span // TILE * y, read)
    for h in range(heads):
        att_ref[:, h * HEAD : (h + 1) * HEAD] = (
            acc_ref[h, :, :HEAD] / acc_ref[h, :, HEAD:]
        ).astype(jnp.bfloat16)
    whole[2].wait()
    chips, rows, columns = outs[0].shape
    chip, core = place_ref[2], place_ref[3]

    @pl.loop(0, chips)
    def _(step):
        at = lax.rem(chip + step, chips) * 2
        for first, side in enumerate((core, 1 - core)):
            start = pl.multiple_of((at + side) * columns, columns)
            product = dot(att_ref[...], w_ref[:, pl.ds(start, columns)]).astype(jnp.bfloat16)
            for part, ref in enumerate(outs[first::2]):
                ref[step] = product[part * rows : (part + 1) * rows]


def pack_row_kernel(place_ref, *refs):
    z = place_ref[0] % WIDE
    at, middle = KEEP, WIDE * KEEP // 2
    for ref in refs[:-2]:
        rows = ref.shape[0]
        start = pl.multiple_of(lax.rem(z * KEEP + at, WIDE * KEEP), KEEP // 2)
        at += rows
        for out_ref, first in zip(refs[-2:], (0, middle)):

            @pl.when((start >= first) & (start < first + middle))
            def _():
                out_ref[pl.ds(pl.multiple_of(start - first, KEEP // 2), rows)] = ref[...]


def pack_row(place, pieces):
    return pl.pallas_call(
        pack_row_kernel,
        out_shape=[jax.ShapeDtypeStruct((WIDE * KEEP // 2, 2 * HEAD), jnp.bfloat16)] * 2,
        in_specs=[SMEM] + [VMEM] * len(pieces),
        out_specs=[VMEM] * 2,
        compiler_params=pltpu.CompilerParams(vmem_limit_bytes=8 * 2**20),
        name="pack_row",
    )(place, *pieces)


def cost(rows, keys):
    return pl.CostEstimate(
        flops=rows * keys * HEAD * 8, bytes_accessed=8 * 2**20, transcendentals=rows * keys
    )


def state_of(length, heads):
    return [
        jax.ShapeDtypeStruct((heads, length, 2 * HEAD), jnp.float32),
        jax.ShapeDtypeStruct((heads, length, HEAD), jnp.float32),
    ]


def own_row(place, queries, keys, values, row_a, row_b):
    length, width = queries.shape
    whole = lambda x: pl.BlockSpec(x.shape, lambda i: (0,) * x.ndim)
    state = state_of(length, width // HEAD)
    return pl.pallas_call(
        own_row_kernel,
        grid=(1,),
        out_shape=state,
        in_specs=[SMEM, *[whole(x) for x in (queries, keys, values)], ANY, ANY],
        out_specs=[whole(x) for x in state],
        scratch_shapes=[
            pltpu.VMEM((WIDE * KEEP, 2 * HEAD), jnp.bfloat16),
            pltpu.VMEM((8, TILE), jnp.float32),
            pltpu.SemaphoreType.DMA((2,)),
        ],
        compiler_params=PARAMS,
        cost_estimate=cost(length * width // HEAD, length + WIDE * KEEP),
        name="own_row",
    )(place, queries, keys, values, row_a, row_b)


def rest_rows(place, queries, rest, banks, weight, state, parts, chips):
    length, width = queries.shape
    heads = width // HEAD
    keys = TILE + 3 * WIDE * KEEP
    whole = lambda x: pl.BlockSpec(x.shape, lambda i: (0,) * len(x.shape))
    out = jax.ShapeDtypeStruct((chips, length // parts, weight.shape[1] // chips // 2), jnp.bfloat16)
    return pl.pallas_call(
        rest_kernel,
        grid=(1,),
        out_shape=[out] * (2 * parts),
        in_specs=[SMEM, whole(queries), whole(rest), *[ANY] * (len(banks) + 3)],
        out_specs=[whole(out)] * (2 * parts),
        scratch_shapes=[
            pltpu.VMEM((keys, 2 * HEAD), jnp.bfloat16),
            pltpu.VMEM(weight.shape, weight.dtype),
            pltpu.VMEM((2, 8, TILE), jnp.float32),
            pltpu.VMEM((heads, length, 2 * HEAD), jnp.float32),
            pltpu.VMEM((heads, length, 2 * HEAD), jnp.float32),
            pltpu.VMEM((heads, length, HEAD), jnp.float32),
            pltpu.VMEM((length, width), jnp.bfloat16),
            pltpu.SemaphoreType.DMA((13,)),
        ],
        compiler_params=PARAMS,
        cost_estimate=cost(length * heads, keys),
        name="rest_rows",
    )(place, queries, rest, *banks, weight, *state)


def added(*terms):
    return sum(term.astype(jnp.float32) for term in terms).astype(jnp.bfloat16)


def on_device(queries, key_rows, value_rows, kept_positions, anchor_length, output_weight):
    mine, head = lax.axis_index("ctx"), lax.axis_index("head")
    length, devices, blocks = queries.shape[0], lax.axis_size("head"), lax.axis_size("ctx")
    chips, chip, core = devices // 2, head // 2, head % 2
    tall = blocks // WIDE
    swap = [(i, i ^ 1) for i in range(devices)]
    up = [(i, (i + 2) % devices) for i in range(devices)]
    down = [(i, (i - 2) % devices) for i in range(devices)]
    along = lambda step: [
        (r * WIDE + c, r * WIDE + (c + step) % WIDE) for r in range(tall) for c in range(WIDE)
    ]
    across = lambda hops: [(a * WIDE + c, b * WIDE + c) for a, b in hops for c in range(WIDE)]
    permute = lambda x, pairs: lax.ppermute(x, "ctx", pairs)

    spots = jnp.stack([chip, core]).astype(jnp.int32)
    place = jnp.concatenate([mine.astype(jnp.int32)[None], anchor_length, spots])
    kept, rest = select(anchor_length, kept_positions, key_rows, value_rows)

    plus, minus = along(1), along(-1)
    half = KEEP // 2
    left, right = [kept], [kept]
    rest = jnp.where(mine == 0, rest, jnp.zeros_like(rest))
    upward = [[(0, WIDE)], [(0, 3 * WIDE), (WIDE, 2 * WIDE)]]
    for step in range(WIDE // 2 - 1):
        left.append(permute(left[-1], plus))
        right.append(permute(right[-1], minus))
        if step < len(upward):
            rest = rest + permute(rest, upward[step])
            left[-1], right[-1], rest = lax.optimization_barrier((left[-1], right[-1], rest))
    opposite = [permute(left[-1][:half], plus), permute(right[-1][half:], minus)]
    ends = pack_row(place, right[1:] + opposite + left[:0:-1] + [kept])

    below_a = permute(ends[0], across([(0, 1), (1, 2), (2, 3)]))
    above_b = permute(ends[1], across([(0, 3), (1, 0)]))
    below_b = permute(ends[1], across([(0, 1), (1, 2), (2, 3)]))
    above_a = permute(ends[0], across([(0, 3)]))

    rest, ends = lax.optimization_barrier((rest, ends))
    spread = lambda hops: [(r * WIDE + a, r * WIDE + b) for a, b in hops for r in range(tall)]
    rest = rest + permute(rest, spread([(0, 4)]))
    rest, below_a, above_b = lax.optimization_barrier((rest, below_a, above_b))
    below2 = permute(below_a, across([(1, 2), (2, 3)]))
    above2 = permute(above_b, across([(0, 3), (3, 2)]))
    rest = rest + permute(rest, spread([(0, 2), (4, 6)]))
    rest = rest + permute(rest, spread([(0, 1), (2, 3), (4, 5), (6, 7)]))

    parts = 2
    state = own_row(place, queries, key_rows, value_rows, *ends)
    banks = (ends[0], below_a, below_b, above_a, above_b, below2, above2)

    outs = []
    half = length // parts // 2
    terms = rest_rows(place, queries, rest, banks, output_weight, state, parts, chips)
    others = [lax.ppermute(send, "head", swap) for send in terms[1::2]]
    for own, other in zip(terms[::2], others):
        across_x = added(own[2], other[2])
        from_below = lax.ppermute(across_x[:half], "head", up)
        from_above = lax.ppermute(across_x[half:], "head", down)
        upward = jnp.concatenate(
            [added(own[1, :half], other[1, :half], from_below), added(own[1, half:], other[1, half:])]
        )
        downward = jnp.concatenate(
            [added(own[3, :half], other[3, :half]), added(own[3, half:], other[3, half:], from_above)]
        )
        upward, downward = lax.ppermute(upward, "head", up), lax.ppermute(downward, "head", down)
        outs.append(added(own[0], other[0], upward, downward))
    return jnp.concatenate(outs)


def solution(mesh):
    placed = (
        P("ctx", "head"),
        P("ctx", "head"),
        P("ctx", "head"),
        P("head", "ctx"),
        P("head"),
        P("head", None),
    )
    return jax.shard_map(
        on_device, mesh=mesh, in_specs=placed, out_specs=P("ctx", "head"), check_vma=False
    )
```

```python
import functools

import jax
import jax.numpy as jnp
from jax import lax
from jax.experimental import pallas as pl
from jax.experimental.pallas import tpu as pltpu
from jax.sharding import PartitionSpec as P

HEAD = 128
WIDE = 8
INFO = 16
KEEP = 256
LOG2E = 1.4426950408889634
FACTOR = HEAD**-0.5 * LOG2E
LIMIT = 2.0**100
NEGATIVE = -1e30
NT = (((1,), (1,)), ((), ()))
VMEM = pl.BlockSpec(memory_space=pltpu.VMEM)
SMEM = pl.BlockSpec(memory_space=pltpu.SMEM)
HBM = pl.BlockSpec(memory_space=pltpu.HBM)
ANY = pl.BlockSpec(memory_space=pl.ANY)
TILE = 512
STEP = 1024
PARAMS = pltpu.CompilerParams(vmem_limit_bytes=60 * 2**20)


def dot(a, b):
    return jnp.dot(a, b, preferred_element_type=jnp.float32)


def dot_nt(a, b):
    return lax.dot_general(a, b, NT, preferred_element_type=jnp.float32)


def count_along(shape, dim):
    return lax.broadcasted_iota(jnp.int32, shape, dim)


def ones_where(condition):
    return jnp.where(condition, 1.0, 0.0).astype(jnp.bfloat16)


def select_kernel(used_ref, *refs):
    sources, (kept_rows_ref, rest_ref), targets, sems = refs[:3], refs[3:5], refs[5:8], refs[8]
    copies = [
        pltpu.make_async_copy(source, target, sems.at[at])
        for at, (source, target) in enumerate(zip(sources, targets))
    ]
    for copy in copies:
        copy.start()
    for copy in copies:
        copy.wait()
    kept_ref, key_ref, value_ref = targets
    length, keep = key_ref.shape[0], kept_ref.shape[1]
    hit = ones_where(count_along((length, keep), 0) == kept_ref[...])
    kept = dot_nt(jnp.ones((8, keep), jnp.bfloat16), hit)
    square = (length, length)
    before = ones_where(count_along(square, 0) < count_along(square, 1))
    rank = dot(kept.astype(jnp.bfloat16), before)
    column = count_along((8, length), 1)
    place = jnp.where(kept > 0.5, rank, column.astype(jnp.float32) + keep - rank)
    order = ones_where(count_along(square, 0).astype(jnp.float32) == place[:1])
    for at, ref in enumerate((key_ref, value_ref)):
        columns = slice(at * HEAD, (at + 1) * HEAD)
        rows = dot(order, ref[...]).astype(jnp.bfloat16)
        kept_rows_ref[:, columns] = rows[:keep]
        rest_ref[: length - keep, columns] = rows[keep:]
    in_both = jnp.where((kept > 0.5) & (column < used_ref[0]), 1.0, 0.0)[:1]
    number = jnp.sum(in_both, axis=1, keepdims=True)
    rest_ref[length - keep :] = jnp.broadcast_to(number, (INFO, 2 * HEAD)).astype(jnp.bfloat16)


def select(used, kept, keys, values):
    length = keys.shape[0]
    rows = (KEEP, length - KEEP + INFO)
    return pl.pallas_call(
        select_kernel,
        out_shape=[jax.ShapeDtypeStruct((n, 2 * HEAD), jnp.bfloat16) for n in rows],
        in_specs=[SMEM, HBM, HBM, HBM],
        out_specs=[VMEM] * 2,
        scratch_shapes=[
            *[pltpu.VMEM(x.shape, x.dtype) for x in (kept, keys, values)],
            pltpu.SemaphoreType.DMA((3,)),
        ],
        compiler_params=PARAMS,
        name="select_kept",
    )(used, kept, keys, values)


def wide(column, width):
    return jnp.concatenate([column] * (width // HEAD), axis=1)


def widened(values):
    return jnp.concatenate([values, jnp.ones_like(values)], axis=1)


def scores(query, keys):
    return dot_nt(query, keys) * FACTOR


def local(query, keys, values, acc_ref, peak_ref):
    length = query.shape[0]
    causal = count_along((length, length), 1) <= count_along((length, length), 0)
    raw = jnp.where(causal, scores(query, keys), NEGATIVE)
    peak = jnp.broadcast_to(jnp.max(raw, axis=1, keepdims=True), (length, HEAD))
    peak_ref[...] = peak
    weights = jnp.exp2(raw - wide(peak, length)).astype(jnp.bfloat16)
    acc_ref[...] = dot(weights, widened(values))


def biased(raw, bias):
    if bias is None:
        return raw
    return (raw.reshape(-1, *bias.shape) + bias).reshape(raw.shape)


def fixed(heads, view, keys, values, bias):
    raw = scores(view(0)[0], keys)
    for h in range(heads):
        _, acc_ref, peak_ref = view(h)
        ahead = scores(view(h + 1)[0], keys) if h + 1 < heads else None
        weights = jnp.exp2(biased(raw, bias) - wide(peak_ref[...], keys.shape[0]))
        acc_ref[...] += dot(weights.astype(jnp.bfloat16), values)
        raw = ahead


def moving(query, acc_ref, peak_ref, keys, values, bias):
    raw = biased(scores(query, keys), bias)
    old = peak_ref[...]
    peak = jnp.maximum(old, jnp.max(raw, axis=1, keepdims=True))
    weights = jnp.exp2(raw - wide(peak, keys.shape[0])).astype(jnp.bfloat16)
    peak_ref[...] = peak
    acc_ref[...] = acc_ref[...] * wide(jnp.exp2(old - peak), 2 * HEAD) + dot(weights, values)


def absorb(heads, view, masked, steps, read):
    if masked is not None:

        @pl.loop(0, masked)
        def _(step):
            fixed(heads, view, *read(step, True))

    @pl.loop(0, steps)
    def _(step):
        fixed(heads, view, *read(step, False))


def absorb_again(acc_ref, view, start, tiles, read):
    largest = jnp.max(acc_ref[:, :, HEAD:])

    @pl.when(jnp.logical_not(largest < LIMIT))
    def _():
        @pl.loop(0, acc_ref.shape[0])
        def _(h):
            start(h)

            @pl.loop(0, tiles)
            def _(tile):
                moving(*view(h), *read(tile))


def tile_of(ref, start, size):
    rows = pl.ds(pl.multiple_of(start, TILE), size)
    return ref[rows, :HEAD], widened(ref[rows, HEAD:])


def head_view(q_ref, acc_ref, peak_ref):
    def view(h):
        columns = pl.ds(pl.multiple_of(h * HEAD, HEAD), HEAD)
        return q_ref[:, columns], acc_ref.at[h], peak_ref.at[h]

    return view


def bias_where(allowed):
    return jnp.where(allowed, 0.0, NEGATIVE)


def own_row_kernel(
    place_ref, q_ref, k_ref, v_ref, row_a, row_b, acc_ref, peak_ref, row_ref, bias_ref, sems
):
    keys = place_ref[0] % WIDE * KEEP
    tiles, part = keys // TILE, jnp.where(keys % TILE > 0, 1, 0)
    half = row_a.shape[0]
    copies = [
        pltpu.make_async_copy(ref, row_ref.at[pl.ds(at * half, half)], sems.at[at])
        for at, ref in enumerate((row_a, row_b))
    ]
    for copy in copies:
        copy.start()
    view, heads = head_view(q_ref, acc_ref, peak_ref), acc_ref.shape[0]

    def start(h):
        query, acc, peak = view(h)
        local(query, k_ref[...], v_ref[...], acc, peak)

    def read(tile):
        bias_ref[...] = bias_where(count_along(bias_ref.shape, 1) + tile * TILE < keys)
        return *tile_of(row_ref, tile * TILE, TILE), bias_ref[...]

    def read_fast(step, masked):
        return read(tiles) if masked else (*tile_of(row_ref, step * TILE, TILE), None)

    for h in range(heads):
        start(h)
    for copy in copies:
        copy.wait()
    absorb(heads, view, part, tiles, read_fast)
    absorb_again(acc_ref, view, start, tiles + part, read)


def early_kernel(
    place_ref, q_ref, below_a, above_b, acc_in, peak_in, acc_ref, peak_ref, bank_ref, carried_ref,
    sems,
):
    y, heads = place_ref[0] // WIDE, acc_ref.shape[0]
    steps = jnp.where(y == 3, 2, jnp.minimum(y, 1))
    sources = (peak_in, peak_ref), (below_a, bank_ref.at[pl.ds(0, STEP)]), (
        above_b,
        bank_ref.at[pl.ds(STEP, STEP)],
    )
    copies = [
        pltpu.make_async_copy(source, target, sems.at[at])
        for at, (source, target) in enumerate((*sources, (acc_in, carried_ref)))
    ]
    for copy in copies:
        copy.start()
    acc_ref[...] = jnp.zeros_like(acc_ref)
    view = head_view(q_ref, acc_ref, peak_ref)

    def start(h):
        acc_ref[h] = carried_ref[h]

    def read(tile):
        return *tile_of(bank_ref, tile * TILE, TILE), None

    for copy in copies[:3]:
        copy.wait()
    absorb(heads, view, None, steps, lambda at, _: (*tile_of(bank_ref, at * STEP, STEP), None))
    copies[3].wait()
    acc_ref[...] += carried_ref[...]
    absorb_again(acc_ref, view, start, steps * (STEP // TILE), read)


def rest_kernel(
    place_ref, q_ref, rest_ref, row_a, below_a, below_b, above_a, below2_ref, above2_ref,
    weight_ref, acc_in, peak_in, *refs,
):
    outs, made = refs[:4], refs[4:8]
    bank_ref, w_ref, bias_ref, acc_ref, carried_ref, peak_ref, att_ref, sems, out_sems = refs[8:]
    mine, used = place_ref[0], place_ref[1]
    y, heads = mine // WIDE, acc_ref.shape[0]
    copies = []

    def copy(source, at, rows, condition, step):
        target = bank_ref.at[pl.ds(at, rows)]
        one = pltpu.make_async_copy(source, target, sems.at[len(copies)])
        copies.append((one, condition, step))

    for row, ref in enumerate((row_a, below_a, below2_ref, above_a)):
        copy(ref.at[pl.ds(0, KEEP)], 0, KEEP, (mine > 0) & (y == row), None)
    for step, (ref, condition) in enumerate(
        ((below_b, y > 0), (below2_ref, y > 1), (above2_ref, y > 1), (above_a, y == 3))
    ):
        copy(ref, TILE + step * STEP, STEP, condition, step)
    for one, condition, _ in copies:
        pl.when(condition)(one.start)
    whole = [
        pltpu.make_async_copy(source, target, sems.at[len(copies) + at])
        for at, (source, target) in enumerate(
            ((peak_in, peak_ref), (acc_in, carried_ref), (weight_ref, w_ref))
        )
    ]
    for one in whole:
        one.start()
    acc_ref[...] = jnp.zeros_like(acc_ref)
    bank_ref[KEEP:TILE] = rest_ref[: TILE - KEEP]
    number = wide(rest_ref[TILE - KEEP : TILE - KEEP + 1, :HEAD].astype(jnp.int32), TILE)
    at = count_along((1, TILE), 1)
    limit = jnp.where(at < KEEP, number, KEEP + used - number)
    bias_ref[0] = jnp.broadcast_to(bias_where(at < limit), bias_ref.shape[1:])
    bias_ref[1] = jnp.zeros(bias_ref.shape[1:], jnp.float32)
    view = head_view(q_ref, acc_ref, peak_ref)

    def start(h):
        acc_ref[h] = carried_ref[h]

    def read_fast(step, masked):
        for one, condition, when in copies:
            if masked and when is None:
                pl.when(condition)(one.wait)
            elif when is not None and not masked:
                pl.when(condition & (step == when))(one.wait)
        if masked:
            return read(0)
        return *tile_of(bank_ref, TILE + step * STEP, STEP), None

    def read(tile):
        return *tile_of(bank_ref, tile * TILE, TILE), bias_ref[jnp.minimum(tile, 1)]

    masked = jnp.where(mine > 0, 1, 0)
    whole[0].wait()
    steps = jnp.where(y == 3, 4, jnp.where(y == 2, 3, y))
    absorb(heads, view, masked, steps, read_fast)
    whole[1].wait()
    acc_ref[...] += carried_ref[...]
    absorb_again(acc_ref, view, start, masked + STEP // TILE * steps, read)
    for h in range(heads):
        att_ref[:, h * HEAD : (h + 1) * HEAD] = (
            acc_ref[h, :, :HEAD] / acc_ref[h, :, HEAD:]
        ).astype(jnp.bfloat16)
    whole[2].wait()
    chips, rows, columns = outs[0].shape
    chip, core = place_ref[2], place_ref[3]

    def written(at, step):
        return pltpu.make_async_copy(made[at].at[step], outs[at].at[step], out_sems.at[at])

    @pl.loop(0, chips)
    def _(step):
        column = lax.rem(chip + step, chips) * 2
        for first, side in enumerate((core, 1 - core)):
            start = pl.multiple_of((column + side) * columns, columns)
            product = dot(att_ref[...], w_ref[:, pl.ds(start, columns)]).astype(jnp.bfloat16)
            for part in range(2):
                made[2 * part + first][step] = product[part * rows : (part + 1) * rows]
        for at in range(4):
            written(at, step).start()

    for at in range(4):
        pltpu.make_async_copy(made[at], outs[at], out_sems.at[at]).wait()


def pack_row_kernel(place_ref, *refs):
    z = place_ref[0] % WIDE
    at, middle = KEEP, WIDE * KEEP // 2
    for ref in refs[:-2]:
        rows = ref.shape[0]
        start = pl.multiple_of(lax.rem(z * KEEP + at, WIDE * KEEP), KEEP // 2)
        at += rows
        for out_ref, first in zip(refs[-2:], (0, middle)):

            @pl.when((start >= first) & (start < first + middle))
            def _():
                out_ref[pl.ds(pl.multiple_of(start - first, KEEP // 2), rows)] = ref[...]


def pack_row(place, pieces):
    return pl.pallas_call(
        pack_row_kernel,
        out_shape=[jax.ShapeDtypeStruct((WIDE * KEEP // 2, 2 * HEAD), jnp.bfloat16)] * 2,
        in_specs=[SMEM] + [VMEM] * len(pieces),
        out_specs=[VMEM] * 2,
        compiler_params=pltpu.CompilerParams(vmem_limit_bytes=8 * 2**20),
        name="pack_row",
    )(place, *pieces)


def cost(rows, keys):
    return pl.CostEstimate(
        flops=rows * keys * HEAD * 8, bytes_accessed=8 * 2**20, transcendentals=rows * keys
    )


def state_of(length, heads):
    return [
        jax.ShapeDtypeStruct((heads, length, 2 * HEAD), jnp.float32),
        jax.ShapeDtypeStruct((heads, length, HEAD), jnp.float32),
    ]


def own_row(place, queries, keys, values, row_a, row_b):
    length, width = queries.shape
    whole = lambda x: pl.BlockSpec(x.shape, lambda i: (0,) * x.ndim)
    state = state_of(length, width // HEAD)
    return pl.pallas_call(
        own_row_kernel,
        grid=(1,),
        out_shape=state,
        in_specs=[SMEM, *[whole(x) for x in (queries, keys, values)], ANY, ANY],
        out_specs=[whole(x) for x in state],
        scratch_shapes=[
            pltpu.VMEM((WIDE * KEEP, 2 * HEAD), jnp.bfloat16),
            pltpu.VMEM((8, TILE), jnp.float32),
            pltpu.SemaphoreType.DMA((2,)),
        ],
        compiler_params=PARAMS,
        cost_estimate=cost(length * width // HEAD, length + WIDE * KEEP),
        name="own_row",
    )(place, queries, keys, values, row_a, row_b)


def early_rows(place, queries, below_a, above_b, state):
    length, width = queries.shape
    whole = lambda x: pl.BlockSpec(x.shape, lambda i: (0,) * len(x.shape))
    return pl.pallas_call(
        early_kernel,
        grid=(1,),
        out_shape=state_of(length, width // HEAD),
        in_specs=[SMEM, whole(queries), *[ANY] * 4],
        out_specs=[whole(x) for x in state],
        scratch_shapes=[
            pltpu.VMEM((2 * STEP, 2 * HEAD), jnp.bfloat16),
            pltpu.VMEM(state[0].shape, jnp.float32),
            pltpu.SemaphoreType.DMA((4,)),
        ],
        compiler_params=PARAMS,
        cost_estimate=cost(length * width // HEAD, 2 * STEP),
        name="early_rows",
    )(place, queries, below_a, above_b, *state)


def rest_rows(place, queries, rest, banks, weight, state, chips):
    length, width = queries.shape
    heads, keys = width // HEAD, TILE + 4 * STEP
    whole = lambda x: pl.BlockSpec(x.shape, lambda i: (0,) * len(x.shape))
    out = jax.ShapeDtypeStruct((chips, length // 2, weight.shape[1] // chips // 2), jnp.bfloat16)
    return pl.pallas_call(
        rest_kernel,
        grid=(1,),
        out_shape=[out] * 4,
        in_specs=[SMEM, whole(queries), whole(rest), *[ANY] * (len(banks) + 3)],
        out_specs=[ANY] * 4,
        scratch_shapes=[
            *[pltpu.VMEM(out.shape, out.dtype)] * 4,
            pltpu.VMEM((keys, 2 * HEAD), jnp.bfloat16),
            pltpu.VMEM(weight.shape, weight.dtype),
            pltpu.VMEM((2, 8, TILE), jnp.float32),
            pltpu.VMEM((heads, length, 2 * HEAD), jnp.float32),
            pltpu.VMEM((heads, length, 2 * HEAD), jnp.float32),
            pltpu.VMEM((heads, length, HEAD), jnp.float32),
            pltpu.VMEM((length, width), jnp.bfloat16),
            pltpu.SemaphoreType.DMA((11,)),
            pltpu.SemaphoreType.DMA((4,)),
        ],
        compiler_params=pltpu.CompilerParams(vmem_limit_bytes=44 * 2**20),
        cost_estimate=cost(length * heads, keys),
        name="rest_rows",
    )(place, queries, rest, *banks, weight, *state)


def summed(*refs):
    return sum(ref[...].astype(jnp.float32) for ref in refs)


def cross_kernel(own_ref, other_ref, upper_ref, lower_ref):
    total = summed(own_ref, other_ref).astype(jnp.bfloat16)
    half = upper_ref.shape[0]
    upper_ref[...] = total[:half]
    lower_ref[...] = total[half:]


def turn_kernel(own1, other1, own3, other3, below_ref, above_ref, up_ref, down_ref):
    half = below_ref.shape[0]
    up, down = summed(own1, other1), summed(own3, other3)
    up_ref[:half] = (up[:half] + summed(below_ref)).astype(jnp.bfloat16)
    up_ref[half:] = up[half:].astype(jnp.bfloat16)
    down_ref[:half] = down[:half].astype(jnp.bfloat16)
    down_ref[half:] = (down[half:] + summed(above_ref)).astype(jnp.bfloat16)


def finish_kernel(own_ref, other_ref, up_ref, down_ref, *refs):
    refs[-1][...] = summed(own_ref, other_ref, up_ref, down_ref).astype(jnp.bfloat16)


def small_call(kernel, name, args, chunks, shapes, out_specs=None, **more):
    specs = [
        pl.BlockSpec(x.shape, lambda i: (0, 0))
        if chunk is None
        else pl.BlockSpec((None, *x.shape[1:]), lambda i, chunk=chunk: (chunk, 0, 0))
        for x, chunk in zip(args, chunks)
    ]
    if out_specs is None:
        out_specs = [pl.BlockSpec(shape, lambda i: (0, 0)) for shape in shapes]
    return pl.pallas_call(
        kernel,
        grid=(1,),
        out_shape=[jax.ShapeDtypeStruct(shape, jnp.bfloat16) for shape in shapes],
        in_specs=specs + more.pop("extra", []),
        out_specs=out_specs,
        compiler_params=pltpu.CompilerParams(vmem_limit_bytes=8 * 2**20),
        name=name,
        **more,
    )


def on_device(queries, key_rows, value_rows, kept_positions, anchor_length, output_weight):
    mine, head = lax.axis_index("ctx"), lax.axis_index("head")
    length, devices, blocks = queries.shape[0], lax.axis_size("head"), lax.axis_size("ctx")
    chips, chip, core = devices // 2, head // 2, head % 2
    tall = blocks // WIDE
    swap = [(i, i ^ 1) for i in range(devices)]
    up = [(i, (i + 2) % devices) for i in range(devices)]
    down = [(i, (i - 2) % devices) for i in range(devices)]
    along = lambda step: [
        (r * WIDE + c, r * WIDE + (c + step) % WIDE) for r in range(tall) for c in range(WIDE)
    ]
    across = lambda hops: [(a * WIDE + c, b * WIDE + c) for a, b in hops for c in range(WIDE)]
    permute = lambda x, pairs: lax.ppermute(x, "ctx", pairs)

    spots = jnp.stack([chip, core]).astype(jnp.int32)
    place = jnp.concatenate([mine.astype(jnp.int32)[None], anchor_length, spots])
    kept, rest = select(anchor_length, kept_positions, key_rows, value_rows)

    plus, minus = along(1), along(-1)
    half = KEEP // 2
    left, right = [kept], [kept]
    rest = jnp.where(mine == 0, rest, jnp.zeros_like(rest))
    upward = [[(0, WIDE)], [(0, 3 * WIDE), (WIDE, 2 * WIDE)]]
    for step in range(WIDE // 2 - 1):
        left.append(permute(left[-1], plus))
        right.append(permute(right[-1], minus))
        if step < len(upward):
            rest = rest + permute(rest, upward[step])
            left[-1], right[-1], rest = lax.optimization_barrier((left[-1], right[-1], rest))
    opposite = [permute(left[-1][:half], plus), permute(right[-1][half:], minus)]
    ends = pack_row(place, right[1:] + opposite + left[:0:-1] + [kept])

    below_a = permute(ends[0], across([(0, 1), (1, 2), (2, 3)]))
    above_b = permute(ends[1], across([(0, 3), (1, 0)]))
    below_b = permute(ends[1], across([(0, 1), (1, 2), (2, 3)]))
    above_a = permute(ends[0], across([(0, 3)]))

    rest, ends = lax.optimization_barrier((rest, ends))
    spread = lambda hops: [(r * WIDE + a, r * WIDE + b) for a, b in hops for r in range(tall)]
    rest = rest + permute(rest, spread([(0, 4)]))
    state = own_row(place, queries, key_rows, value_rows, *ends)
    rest, below_a, above_b, state = lax.optimization_barrier((rest, below_a, above_b, state))
    below2 = permute(below_a, across([(1, 2), (2, 3)]))
    above2 = permute(above_b, across([(0, 3), (3, 2)]))
    rest = rest + permute(rest, spread([(0, 2), (4, 6)]))
    rest = rest + permute(rest, spread([(0, 1), (2, 3), (4, 5), (6, 7)]))

    state = early_rows(place, queries, below_a, above_b, state)
    banks = (ends[0], below_a, below_b, above_a, below2, above2)
    terms = rest_rows(place, queries, rest, banks, output_weight, state, chips)
    others = [lax.ppermute(send, "head", swap) for send in terms[1::2]]

    rows, columns = terms[0].shape[1:]
    shape, half = (rows, columns), (rows // 2, columns)
    out = None
    for part, (own, other) in enumerate(zip(terms[::2], others)):
        pair = (own, other)
        upper, lower = small_call(cross_kernel, "cross", pair, (2, 2), [half, half])(*pair)
        below, above = lax.ppermute(upper, "head", up), lax.ppermute(lower, "head", down)
        args = (own, other, own, other, below, above)
        upward, downward = small_call(
            turn_kernel, "turn", args, (1, 1, 3, 3, None, None), [shape, shape]
        )(*args)
        upward, downward = lax.ppermute(upward, "head", up), lax.ppermute(downward, "head", down)
        args = (own, other, upward, downward)
        extra = {} if out is None else dict(extra=[ANY], input_output_aliases={4: 0})
        (out,) = small_call(
            finish_kernel, f"finish_{part}", args, (0, 0, None, None), [(length, columns)],
            [pl.BlockSpec(shape, lambda i, part=part: (part, 0))], **extra,
        )(*args, *([] if out is None else [out]))
    return out


def solution(mesh):
    placed = (
        P("ctx", "head"),
        P("ctx", "head"),
        P("ctx", "head"),
        P("head", "ctx"),
        P("head"),
        P("head", None),
    )
    return jax.shard_map(
        on_device, mesh=mesh, in_specs=placed, out_specs=P("ctx", "head"), check_vma=False
    )
```

```python
import functools

import jax
import jax.numpy as jnp
from jax import lax
from jax.experimental import pallas as pl
from jax.experimental.pallas import tpu as pltpu
from jax.sharding import PartitionSpec as P

HEAD = 128
WIDE = 8
INFO = 16
KEEP = 256
LOG2E = 1.4426950408889634
FACTOR = HEAD**-0.5 * LOG2E
LIMIT = 2.0**100
NEGATIVE = -1e30
NT = (((1,), (1,)), ((), ()))
VMEM = pl.BlockSpec(memory_space=pltpu.VMEM)
SMEM = pl.BlockSpec(memory_space=pltpu.SMEM)
HBM = pl.BlockSpec(memory_space=pltpu.HBM)
ANY = pl.BlockSpec(memory_space=pl.ANY)
TILE = 512
STEP = 1024
PARAMS = pltpu.CompilerParams(vmem_limit_bytes=60 * 2**20)


def dot(a, b):
    return jnp.dot(a, b, preferred_element_type=jnp.float32)


def dot_nt(a, b):
    return lax.dot_general(a, b, NT, preferred_element_type=jnp.float32)


def count_along(shape, dim):
    return lax.broadcasted_iota(jnp.int32, shape, dim)


def ones_where(condition):
    return jnp.where(condition, 1.0, 0.0).astype(jnp.bfloat16)


def select_kernel(used_ref, *refs):
    sources, (kept_rows_ref, rest_ref), targets, sems = refs[:3], refs[3:5], refs[5:8], refs[8]
    copies = [
        pltpu.make_async_copy(source, target, sems.at[at])
        for at, (source, target) in enumerate(zip(sources, targets))
    ]
    for copy in copies:
        copy.start()
    for copy in copies:
        copy.wait()
    kept_ref, key_ref, value_ref = targets
    length, keep = key_ref.shape[0], kept_ref.shape[1]
    hit = ones_where(count_along((length, keep), 0) == kept_ref[...])
    kept = dot_nt(jnp.ones((8, keep), jnp.bfloat16), hit)
    square = (length, length)
    before = ones_where(count_along(square, 0) < count_along(square, 1))
    rank = dot(kept.astype(jnp.bfloat16), before)
    column = count_along((8, length), 1)
    place = jnp.where(kept > 0.5, rank, column.astype(jnp.float32) + keep - rank)
    order = ones_where(count_along(square, 0).astype(jnp.float32) == place[:1])
    for at, ref in enumerate((key_ref, value_ref)):
        columns = slice(at * HEAD, (at + 1) * HEAD)
        rows = dot(order, ref[...]).astype(jnp.bfloat16)
        kept_rows_ref[:, columns] = rows[:keep]
        rest_ref[: length - keep, columns] = rows[keep:]
    in_both = jnp.where((kept > 0.5) & (column < used_ref[0]), 1.0, 0.0)[:1]
    number = jnp.sum(in_both, axis=1, keepdims=True)
    rest_ref[length - keep :] = jnp.broadcast_to(number, (INFO, 2 * HEAD)).astype(jnp.bfloat16)


def select(used, kept, keys, values):
    length = keys.shape[0]
    rows = (KEEP, length - KEEP + INFO)
    return pl.pallas_call(
        select_kernel,
        out_shape=[jax.ShapeDtypeStruct((n, 2 * HEAD), jnp.bfloat16) for n in rows],
        in_specs=[SMEM, HBM, HBM, HBM],
        out_specs=[VMEM] * 2,
        scratch_shapes=[
            *[pltpu.VMEM(x.shape, x.dtype) for x in (kept, keys, values)],
            pltpu.SemaphoreType.DMA((3,)),
        ],
        compiler_params=PARAMS,
        name="select_kept",
    )(used, kept, keys, values)


def wide(column, width):
    return jnp.concatenate([column] * (width // HEAD), axis=1)


def widened(values):
    return jnp.concatenate([values, jnp.ones_like(values)], axis=1)


def scores(query, keys):
    return dot_nt(query, keys) * FACTOR


def local(query, keys, values, acc_ref, peak_ref):
    length = query.shape[0]
    causal = count_along((length, length), 1) <= count_along((length, length), 0)
    raw = jnp.where(causal, scores(query, keys), NEGATIVE)
    peak = jnp.broadcast_to(jnp.max(raw, axis=1, keepdims=True), (length, HEAD))
    peak_ref[...] = peak
    weights = jnp.exp2(raw - wide(peak, length)).astype(jnp.bfloat16)
    acc_ref[...] = dot(weights, widened(values))


def biased(raw, bias):
    if bias is None:
        return raw
    return (raw.reshape(-1, *bias.shape) + bias).reshape(raw.shape)


def fixed(heads, view, keys, values, bias):
    raw = scores(view(0)[0], keys)
    for h in range(heads):
        _, acc_ref, peak_ref = view(h)
        ahead = scores(view(h + 1)[0], keys) if h + 1 < heads else None
        weights = jnp.exp2(biased(raw, bias) - wide(peak_ref[...], keys.shape[0]))
        acc_ref[...] += dot(weights.astype(jnp.bfloat16), values)
        raw = ahead


def moving(query, acc_ref, peak_ref, keys, values, bias):
    raw = biased(scores(query, keys), bias)
    old = peak_ref[...]
    peak = jnp.maximum(old, jnp.max(raw, axis=1, keepdims=True))
    weights = jnp.exp2(raw - wide(peak, keys.shape[0])).astype(jnp.bfloat16)
    peak_ref[...] = peak
    acc_ref[...] = acc_ref[...] * wide(jnp.exp2(old - peak), 2 * HEAD) + dot(weights, values)


def absorb(heads, view, masked, steps, read):
    if masked is not None:

        @pl.loop(0, masked)
        def _(step):
            fixed(heads, view, *read(step, True))

    @pl.loop(0, steps)
    def _(step):
        fixed(heads, view, *read(step, False))


def absorb_again(acc_ref, view, start, tiles, read):
    largest = jnp.max(acc_ref[:, :, HEAD:])

    @pl.when(jnp.logical_not(largest < LIMIT))
    def _():
        @pl.loop(0, acc_ref.shape[0])
        def _(h):
            start(h)

            @pl.loop(0, tiles)
            def _(tile):
                moving(*view(h), *read(tile))


def tile_of(ref, start, size):
    rows = pl.ds(pl.multiple_of(start, TILE), size)
    return ref[rows, :HEAD], widened(ref[rows, HEAD:])


def head_view(q_ref, acc_ref, peak_ref):
    def view(h):
        columns = pl.ds(pl.multiple_of(h * HEAD, HEAD), HEAD)
        return q_ref[:, columns], acc_ref.at[h], peak_ref.at[h]

    return view


def bias_where(allowed):
    return jnp.where(allowed, 0.0, NEGATIVE)


def sums(state_ref):
    return state_ref.at[:, :, pl.ds(0, 2 * HEAD)], state_ref.at[:, :, pl.ds(2 * HEAD, HEAD)]


def own_row_kernel(
    place_ref, q_ref, k_ref, v_ref, row_a, row_b, state_ref, row_ref, bias_ref, sems
):
    acc_ref, peak_ref = sums(state_ref)
    keys = place_ref[0] % WIDE * KEEP
    tiles, part = keys // TILE, jnp.where(keys % TILE > 0, 1, 0)
    half = row_a.shape[0]
    copies = [
        pltpu.make_async_copy(ref, row_ref.at[pl.ds(at * half, half)], sems.at[at])
        for at, ref in enumerate((row_a, row_b))
    ]
    for copy in copies:
        copy.start()
    view, heads = head_view(q_ref, acc_ref, peak_ref), acc_ref.shape[0]

    def start(h):
        query, acc, peak = view(h)
        local(query, k_ref[...], v_ref[...], acc, peak)

    def read(tile):
        bias_ref[...] = bias_where(count_along(bias_ref.shape, 1) + tile * TILE < keys)
        return *tile_of(row_ref, tile * TILE, TILE), bias_ref[...]

    def read_fast(step, masked):
        return read(tiles) if masked else (*tile_of(row_ref, step * TILE, TILE), None)

    for h in range(heads):
        start(h)
    for copy in copies:
        copy.wait()
    absorb(heads, view, part, tiles, read_fast)
    absorb_again(acc_ref, view, start, tiles + part, read)


def more_keys(q_ref, rest_ref, state_in, refs, used, firsts, pieces, steps):
    acc_ref, peak_ref, bank_ref, carried_ref, bias_ref, sems = refs
    acc_in, peak_in = sums(state_in)
    copies = [(peak_in, peak_ref, True), (acc_in, carried_ref, True)]
    copies += [(ref.at[pl.ds(0, KEEP)], bank_ref.at[pl.ds(0, KEEP)], on) for ref, on in firsts]
    for at, (ref, on) in enumerate(pieces):
        copies.append((ref, bank_ref.at[pl.ds(TILE + at * STEP, STEP)], on))
    copies = [
        (pltpu.make_async_copy(source, target, sems.at[at]), on)
        for at, (source, target, on) in enumerate(copies)
    ]

    def under(condition, act):
        if condition is True:
            act()
        else:
            pl.when(condition)(act)

    for one, on in copies:
        under(on, one.start)
    acc_ref[...] = jnp.zeros(acc_ref.shape, jnp.float32)
    bank_ref[KEEP:TILE] = rest_ref[: TILE - KEEP]
    number = wide(rest_ref[TILE - KEEP : TILE - KEEP + 1, :HEAD].astype(jnp.int32), TILE)
    at = count_along((1, TILE), 1)
    limit = jnp.where(at < KEEP, number, KEEP + used - number)
    bias_ref[0] = jnp.broadcast_to(bias_where(at < limit), bias_ref.shape[1:])
    bias_ref[1] = jnp.zeros(bias_ref.shape[1:], jnp.float32)
    view = head_view(q_ref, acc_ref, peak_ref)
    masked = sum(jnp.where(on, 1, 0) for _, on in firsts)

    def start(h):
        acc_ref[h] = carried_ref[h]

    def read(step):
        tile = jnp.where(masked > 0, step, step + 1)
        return *tile_of(bank_ref, tile * TILE, TILE), bias_ref[jnp.minimum(tile, 1)]

    def read_fast(step, with_bias):
        if with_bias:
            return *tile_of(bank_ref, 0, TILE), bias_ref[0]
        return *tile_of(bank_ref, TILE + step * STEP, STEP), None

    for one, on in copies[:1] + copies[2:]:
        under(on, one.wait)
    absorb(acc_ref.shape[0], view, masked, steps, read_fast)
    copies[1][0].wait()
    acc_ref[...] += carried_ref[...]
    absorb_again(acc_ref, view, start, masked + STEP // TILE * steps, read)


def early_kernel(
    place_ref, q_ref, rest_ref, row_a, below_a, below_b, above_a, above_b, state_in, state_ref,
    *refs,
):
    mine, used = place_ref[0], place_ref[1]
    y = mine // WIDE
    firsts = (row_a, (mine > 0) & (y == 0)), (below_a, y == 1), (above_a, y == 3)
    pieces = (below_a, y > 0), (below_b, y > 0), (above_a, y == 3), (above_b, y == 3)
    steps = jnp.where(y == 3, 4, jnp.where(y > 0, 2, 0))
    refs = *sums(state_ref), *refs
    more_keys(q_ref, rest_ref, state_in, refs, used, firsts, pieces, steps)


def rest_kernel(
    place_ref, q_ref, rest_ref, below2_ref, above2_ref, weight_ref, state_in,
    own_out, far_out, near_out, own_ref, send_ref, w_ref, att_ref, out_sems, *refs,
):
    y, used = place_ref[0] // WIDE, place_ref[1]
    weight_copy = pltpu.make_async_copy(weight_ref, w_ref, out_sems.at[3])
    weight_copy.start()
    pieces = (below2_ref, y > 1), (above2_ref, y > 1)
    firsts = ((below2_ref, y == 2),)
    more_keys(q_ref, rest_ref, state_in, refs, used, firsts, pieces, jnp.where(y > 1, 2, 0))
    acc_ref = refs[0]
    for h in range(acc_ref.shape[0]):
        att_ref[:, h * HEAD : (h + 1) * HEAD] = (
            acc_ref[h, :, :HEAD] / acc_ref[h, :, HEAD:]
        ).astype(jnp.bfloat16)
    weight_copy.wait()
    chips, _, columns = own_out.shape
    chip, core = place_ref[2], place_ref[3]

    @pl.loop(0, chips)
    def _(step):
        ahead = jnp.where(step == 0, 2, jnp.where(step == 1, 1, jnp.where(step == 2, 3, 0)))
        column = lax.rem(chip + ahead, chips) * 2
        for ref, side in ((own_ref, core), (send_ref, 1 - core)):
            start = pl.multiple_of((column + side) * columns, columns)
            ref[step] = dot(att_ref[...], w_ref[:, pl.ds(start, columns)]).astype(jnp.bfloat16)
        pltpu.make_async_copy(own_ref.at[step], own_out.at[step], out_sems.at[0]).start()

        @pl.when(step == 0)
        def _():
            pltpu.make_async_copy(send_ref.at[0], far_out, out_sems.at[1]).start()

        @pl.when(step > 0)
        def _():
            target = near_out.at[step - 1]
            pltpu.make_async_copy(send_ref.at[step], target, out_sems.at[2]).start()

    pltpu.make_async_copy(own_ref, own_out, out_sems.at[0]).wait()
    pltpu.make_async_copy(send_ref.at[0], far_out, out_sems.at[1]).wait()
    pltpu.make_async_copy(send_ref.at[pl.ds(1, chips - 1)], near_out, out_sems.at[2]).wait()


def pack_row_kernel(place_ref, *refs):
    z = place_ref[0] % WIDE
    at, middle = KEEP, WIDE * KEEP // 2
    for ref in refs[:-2]:
        rows = ref.shape[0]
        start = pl.multiple_of(lax.rem(z * KEEP + at, WIDE * KEEP), KEEP // 2)
        at += rows
        for out_ref, first in zip(refs[-2:], (0, middle)):

            @pl.when((start >= first) & (start < first + middle))
            def _():
                out_ref[pl.ds(pl.multiple_of(start - first, KEEP // 2), rows)] = ref[...]


def pack_row(place, pieces):
    return pl.pallas_call(
        pack_row_kernel,
        out_shape=[jax.ShapeDtypeStruct((WIDE * KEEP // 2, 2 * HEAD), jnp.bfloat16)] * 2,
        in_specs=[SMEM] + [VMEM] * len(pieces),
        out_specs=[VMEM] * 2,
        compiler_params=pltpu.CompilerParams(vmem_limit_bytes=8 * 2**20),
        name="pack_row",
    )(place, *pieces)


def cost(rows, keys):
    return pl.CostEstimate(
        flops=rows * keys * HEAD * 8, bytes_accessed=8 * 2**20, transcendentals=rows * keys
    )


def state_of(length, heads):
    return jax.ShapeDtypeStruct((heads, length, 3 * HEAD), jnp.float32)


def work_of(length, heads, steps):
    return [
        pltpu.VMEM((TILE + steps * STEP, 2 * HEAD), jnp.bfloat16),
        pltpu.VMEM((heads, length, 2 * HEAD), jnp.float32),
        pltpu.VMEM((2, 8, TILE), jnp.float32),
        pltpu.SemaphoreType.DMA((9,)),
    ]


def own_row(place, queries, keys, values, row_a, row_b):
    length, width = queries.shape
    whole = lambda x: pl.BlockSpec(x.shape, lambda i: (0,) * x.ndim)
    state = state_of(length, width // HEAD)
    return pl.pallas_call(
        own_row_kernel,
        grid=(1,),
        out_shape=state,
        in_specs=[SMEM, *[whole(x) for x in (queries, keys, values)], ANY, ANY],
        out_specs=whole(state),
        scratch_shapes=[
            pltpu.VMEM((WIDE * KEEP, 2 * HEAD), jnp.bfloat16),
            pltpu.VMEM((8, TILE), jnp.float32),
            pltpu.SemaphoreType.DMA((2,)),
        ],
        compiler_params=PARAMS,
        cost_estimate=cost(length * width // HEAD, length + WIDE * KEEP),
        name="own_row",
    )(place, queries, keys, values, row_a, row_b)


def early_rows(place, queries, rest, banks, state):
    length, width = queries.shape
    heads = width // HEAD
    whole = lambda x: pl.BlockSpec(x.shape, lambda i: (0,) * len(x.shape))
    return pl.pallas_call(
        early_kernel,
        grid=(1,),
        out_shape=state_of(length, heads),
        in_specs=[SMEM, whole(queries), whole(rest), *[ANY] * (len(banks) + 1)],
        out_specs=whole(state),
        scratch_shapes=work_of(length, heads, 4),
        compiler_params=PARAMS,
        cost_estimate=cost(length * heads, TILE + 4 * STEP),
        name="early_rows",
    )(place, queries, rest, *banks, state)


def rest_rows(place, queries, rest, banks, weight, state, chips):
    length, width = queries.shape
    heads, keys = width // HEAD, TILE + 2 * STEP
    whole = lambda x: pl.BlockSpec(x.shape, lambda i: (0,) * len(x.shape))
    one = (length, weight.shape[1] // chips // 2)
    shapes = (chips, *one), one, (chips - 1, *one)
    return pl.pallas_call(
        rest_kernel,
        grid=(1,),
        out_shape=[jax.ShapeDtypeStruct(shape, jnp.bfloat16) for shape in shapes],
        in_specs=[SMEM, whole(queries), whole(rest), *[ANY] * (len(banks) + 2)],
        out_specs=[ANY] * 3,
        scratch_shapes=[
            *[pltpu.VMEM((chips, *one), jnp.bfloat16)] * 2,
            pltpu.VMEM(weight.shape, weight.dtype),
            pltpu.VMEM((length, width), jnp.bfloat16),
            pltpu.SemaphoreType.DMA((4,)),
            pltpu.VMEM((heads, length, 2 * HEAD), jnp.float32),
            pltpu.VMEM((heads, length, HEAD), jnp.float32),
            *work_of(length, heads, 2),
        ],
        compiler_params=pltpu.CompilerParams(vmem_limit_bytes=47 * 2**20),
        cost_estimate=cost(length * heads, keys),
        name="rest_rows",
    )(place, queries, rest, *banks, weight, state)


def summed(*refs):
    return sum(ref[...].astype(jnp.float32) for ref in refs)


def cross_kernel(own_ref, other_ref, upper_ref, lower_ref):
    total = summed(own_ref, other_ref).astype(jnp.bfloat16)
    half = upper_ref.shape[0]
    upper_ref[...] = total[:half]
    lower_ref[...] = total[half:]


def add_kernel(*refs):
    terms = refs[:-2]
    middle = len(terms) // 2
    refs[-2][...] = summed(*terms[:middle]).astype(jnp.bfloat16)
    refs[-1][...] = summed(*terms[middle:]).astype(jnp.bfloat16)


def halves_kernel(*refs):
    (*terms, upper_ref, lower_ref), out_ref = refs[:-1], refs[-1]
    half, total = upper_ref.shape[0], summed(*terms)
    out_ref[:half] = (total[:half] + summed(upper_ref)).astype(out_ref.dtype)
    out_ref[half:] = (total[half:] + summed(lower_ref)).astype(out_ref.dtype)


def small_call(kernel, name, terms, shapes, dtype=jnp.bfloat16):
    def spec(term):
        if not isinstance(term, tuple):
            return pl.BlockSpec(term.shape, lambda i: (0, 0))
        x, chunk, half = term
        rows = x.shape[1] // (1 if half is None else 2)
        return pl.BlockSpec((None, rows, x.shape[2]), lambda i: (chunk, half or 0, 0))

    return pl.pallas_call(
        kernel,
        grid=(1,),
        out_shape=[jax.ShapeDtypeStruct(shape, dtype) for shape in shapes],
        in_specs=[spec(term) for term in terms],
        out_specs=[pl.BlockSpec(shape, lambda i: (0, 0)) for shape in shapes],
        compiler_params=pltpu.CompilerParams(vmem_limit_bytes=8 * 2**20),
        name=name,
    )(*[term[0] if isinstance(term, tuple) else term for term in terms])


def on_device(queries, key_rows, value_rows, kept_positions, anchor_length, output_weight):
    mine, head = lax.axis_index("ctx"), lax.axis_index("head")
    length, devices, blocks = queries.shape[0], lax.axis_size("head"), lax.axis_size("ctx")
    chips, chip, core = devices // 2, head // 2, head % 2
    tall = blocks // WIDE
    swap = [(i, i ^ 1) for i in range(devices)]
    up = [(i, (i + 2) % devices) for i in range(devices)]
    down = [(i, (i - 2) % devices) for i in range(devices)]
    along = lambda step: [
        (r * WIDE + c, r * WIDE + (c + step) % WIDE) for r in range(tall) for c in range(WIDE)
    ]
    across = lambda hops: [(a * WIDE + c, b * WIDE + c) for a, b in hops for c in range(WIDE)]
    permute = lambda x, pairs: lax.ppermute(x, "ctx", pairs)

    spots = jnp.stack([chip, core]).astype(jnp.int32)
    place = jnp.concatenate([mine.astype(jnp.int32)[None], anchor_length, spots])
    kept, rest = select(anchor_length, kept_positions, key_rows, value_rows)

    plus, minus = along(1), along(-1)
    half = KEEP // 2
    left, right = [kept], [kept]
    rest = jnp.where(mine == 0, rest, jnp.zeros_like(rest))
    spread = lambda hops: [(r * WIDE + a, r * WIDE + b) for a, b in hops for r in range(tall)]
    upward = [(0, WIDE)], [(0, 3 * WIDE), (WIDE, 2 * WIDE)], spread([(0, 4)])
    for step in range(WIDE // 2 - 1):
        left.append(permute(left[-1], plus))
        right.append(permute(right[-1], minus))
        rest = rest + permute(rest, upward[step])
        left[-1], right[-1], rest = lax.optimization_barrier((left[-1], right[-1], rest))
    opposite = [permute(left[-1][:half], plus), permute(right[-1][half:], minus)]
    ends = pack_row(place, right[1:] + opposite + left[:0:-1] + [kept])

    below_a = permute(ends[0], across([(0, 1), (1, 2), (2, 3)]))
    above_b = permute(ends[1], across([(0, 3), (1, 0)]))
    below_b = permute(ends[1], across([(0, 1), (1, 2), (2, 3)]))
    above_a = permute(ends[0], across([(0, 3)]))

    rest, ends = lax.optimization_barrier((rest, ends))
    rest = rest + permute(rest, spread([(0, 2), (4, 6)]))
    state = own_row(place, queries, key_rows, value_rows, *ends)
    rest, below_a, above_b, state = lax.optimization_barrier((rest, below_a, above_b, state))
    below2 = permute(below_a, across([(1, 2), (2, 3)]))
    above2 = permute(above_b, across([(0, 3), (3, 2)]))
    rest = rest + permute(rest, spread([(0, 1), (2, 3), (4, 5), (6, 7)]))

    state = early_rows(place, queries, rest, (ends[0], below_a, below_b, above_a, above_b), state)
    own, far, near = rest_rows(
        place, queries, rest, (below2, above2), output_weight, state, chips
    )

    far, near = lax.optimization_barrier((lax.ppermute(far, "head", swap), near))
    near = lax.ppermute(near, "head", swap)
    columns = own.shape[2]
    whole, half = (length, columns), (length // 2, columns)
    upper, lower = small_call(cross_kernel, "cross", [(own, 0, None), far], [half, half])
    upper, lower = lax.ppermute(upper, "head", up), lax.ppermute(lower, "head", down)
    terms = [(own, 1, 1), (near, 0, 1), (own, 2, 0), (near, 1, 0)]
    lower_up, upper_down = small_call(add_kernel, "direct", terms, [half, half])
    upper, lower, _, _ = lax.optimization_barrier((upper, lower, lower_up, upper_down))
    lower_up, upper_down = lax.ppermute(lower_up, "head", up), lax.ppermute(upper_down, "head", down)
    terms = [(own, 1, 0), (near, 0, 0), upper, (own, 2, 1), (near, 1, 1), lower]
    upper_up, lower_down = small_call(add_kernel, "turn", terms, [half, half])
    upper_up, lower_down = lax.ppermute(upper_up, "head", up), lax.ppermute(lower_down, "head", down)
    terms = [(own, 3, None), (near, 2, None), upper_down, lower_up]
    (total,) = small_call(halves_kernel, "collect", terms, [whole], jnp.float32)
    return small_call(halves_kernel, "finish", [total, upper_up, lower_down], [whole])[0]


def solution(mesh):
    placed = (
        P("ctx", "head"),
        P("ctx", "head"),
        P("ctx", "head"),
        P("head", "ctx"),
        P("head"),
        P("head", None),
    )
    return jax.shard_map(
        on_device, mesh=mesh, in_specs=placed, out_specs=P("ctx", "head"), check_vma=False
    )
```

```python
import functools

import jax
import jax.numpy as jnp
from jax import lax
from jax.experimental import pallas as pl
from jax.experimental.pallas import tpu as pltpu
from jax.sharding import PartitionSpec as P

HEAD = 128
WIDE = 8
INFO = 16
KEEP = 256
LOG2E = 1.4426950408889634
FACTOR = HEAD**-0.5 * LOG2E
LIMIT = 2.0**100
NEGATIVE = -1e30
NT = (((1,), (1,)), ((), ()))
VMEM = pl.BlockSpec(memory_space=pltpu.VMEM)
SMEM = pl.BlockSpec(memory_space=pltpu.SMEM)
HBM = pl.BlockSpec(memory_space=pltpu.HBM)
ANY = pl.BlockSpec(memory_space=pl.ANY)
TILE = 512
STEP = 1024
PARAMS = pltpu.CompilerParams(vmem_limit_bytes=60 * 2**20)


def dot(a, b):
    return jnp.dot(a, b, preferred_element_type=jnp.float32)


def dot_nt(a, b):
    return lax.dot_general(a, b, NT, preferred_element_type=jnp.float32)


def count_along(shape, dim):
    return lax.broadcasted_iota(jnp.int32, shape, dim)


def ones_where(condition):
    return jnp.where(condition, 1.0, 0.0).astype(jnp.bfloat16)


def select_kernel(used_ref, *refs):
    sources, (kept_rows_ref, rest_ref), targets, sems = refs[:3], refs[3:5], refs[5:8], refs[8]
    copies = [
        pltpu.make_async_copy(source, target, sems.at[at])
        for at, (source, target) in enumerate(zip(sources, targets))
    ]
    for copy in copies:
        copy.start()
    for copy in copies:
        copy.wait()
    kept_ref, key_ref, value_ref = targets
    length, keep = key_ref.shape[0], kept_ref.shape[1]
    hit = ones_where(count_along((length, keep), 0) == kept_ref[...])
    kept = dot_nt(jnp.ones((8, keep), jnp.bfloat16), hit)
    square = (length, length)
    before = ones_where(count_along(square, 0) < count_along(square, 1))
    rank = dot(kept.astype(jnp.bfloat16), before)
    column = count_along((8, length), 1)
    place = jnp.where(kept > 0.5, rank, column.astype(jnp.float32) + keep - rank)
    order = ones_where(count_along(square, 0).astype(jnp.float32) == place[:1])
    for at, ref in enumerate((key_ref, value_ref)):
        columns = slice(at * HEAD, (at + 1) * HEAD)
        rows = dot(order, ref[...]).astype(jnp.bfloat16)
        kept_rows_ref[:, columns] = rows[:keep]
        rest_ref[: length - keep, columns] = rows[keep:]
    in_both = jnp.where((kept > 0.5) & (column < used_ref[0]), 1.0, 0.0)[:1]
    number = jnp.sum(in_both, axis=1, keepdims=True)
    rest_ref[length - keep :] = jnp.broadcast_to(number, (INFO, 2 * HEAD)).astype(jnp.bfloat16)


def select(used, kept, keys, values):
    length = keys.shape[0]
    rows = (KEEP, length - KEEP + INFO)
    return pl.pallas_call(
        select_kernel,
        out_shape=[jax.ShapeDtypeStruct((n, 2 * HEAD), jnp.bfloat16) for n in rows],
        in_specs=[SMEM, HBM, HBM, HBM],
        out_specs=[VMEM] * 2,
        scratch_shapes=[
            *[pltpu.VMEM(x.shape, x.dtype) for x in (kept, keys, values)],
            pltpu.SemaphoreType.DMA((3,)),
        ],
        compiler_params=PARAMS,
        name="select_kept",
    )(used, kept, keys, values)


def wide(column, width):
    return jnp.concatenate([column] * (width // HEAD), axis=1)


def widened(values):
    return jnp.concatenate([values, jnp.ones_like(values)], axis=1)


def scores(query, keys):
    return dot_nt(query, keys) * FACTOR


def local(query, keys, values, acc_ref, peak_ref):
    length = query.shape[0]
    causal = count_along((length, length), 1) <= count_along((length, length), 0)
    raw = jnp.where(causal, scores(query, keys), NEGATIVE)
    peak = jnp.broadcast_to(jnp.max(raw, axis=1, keepdims=True), (length, HEAD))
    peak_ref[...] = peak
    weights = jnp.exp2(raw - wide(peak, length)).astype(jnp.bfloat16)
    acc_ref[...] = dot(weights, widened(values))


def biased(raw, bias):
    if bias is None:
        return raw
    return (raw.reshape(-1, *bias.shape) + bias).reshape(raw.shape)


def fixed(heads, view, keys, values, bias):
    raw = scores(view(0)[0], keys)
    for h in range(heads):
        _, acc_ref, peak_ref = view(h)
        ahead = scores(view(h + 1)[0], keys) if h + 1 < heads else None
        weights = jnp.exp2(biased(raw, bias) - wide(peak_ref[...], keys.shape[0]))
        acc_ref[...] += dot(weights.astype(jnp.bfloat16), values)
        raw = ahead


def moving(query, acc_ref, peak_ref, keys, values, bias):
    raw = biased(scores(query, keys), bias)
    old = peak_ref[...]
    peak = jnp.maximum(old, jnp.max(raw, axis=1, keepdims=True))
    weights = jnp.exp2(raw - wide(peak, keys.shape[0])).astype(jnp.bfloat16)
    peak_ref[...] = peak
    acc_ref[...] = acc_ref[...] * wide(jnp.exp2(old - peak), 2 * HEAD) + dot(weights, values)


def absorb(heads, view, masked, steps, read):
    if masked is not None:

        @pl.loop(0, masked)
        def _(step):
            fixed(heads, view, *read(step, True))

    @pl.loop(0, steps)
    def _(step):
        fixed(heads, view, *read(step, False))


def absorb_again(acc_ref, view, start, tiles, read):
    largest = jnp.max(acc_ref[:, :, HEAD:])

    @pl.when(jnp.logical_not(largest < LIMIT))
    def _():
        @pl.loop(0, acc_ref.shape[0])
        def _(h):
            start(h)

            @pl.loop(0, tiles)
            def _(tile):
                moving(*view(h), *read(tile))


def tile_of(ref, start, size):
    rows = pl.ds(pl.multiple_of(start, TILE), size)
    return ref[rows, :HEAD], widened(ref[rows, HEAD:])


def head_view(q_ref, acc_ref, peak_ref):
    def view(h):
        columns = pl.ds(pl.multiple_of(h * HEAD, HEAD), HEAD)
        return q_ref[:, columns], acc_ref.at[h], peak_ref.at[h]

    return view


def bias_where(allowed):
    return jnp.where(allowed, 0.0, NEGATIVE)


def sums(state_ref):
    return state_ref.at[:, :, pl.ds(0, 2 * HEAD)], state_ref.at[:, :, pl.ds(2 * HEAD, HEAD)]


def own_row_kernel(
    place_ref, q_ref, k_ref, v_ref, row_a, row_b, state_ref, row_ref, bias_ref, sems
):
    acc_ref, peak_ref = sums(state_ref)
    keys = place_ref[0] % WIDE * KEEP
    tiles, part = keys // TILE, jnp.where(keys % TILE > 0, 1, 0)
    half = row_a.shape[0]
    copies = [
        pltpu.make_async_copy(ref, row_ref.at[pl.ds(at * half, half)], sems.at[at])
        for at, ref in enumerate((row_a, row_b))
    ]
    for copy in copies:
        copy.start()
    view, heads = head_view(q_ref, acc_ref, peak_ref), acc_ref.shape[0]

    def start(h):
        query, acc, peak = view(h)
        local(query, k_ref[...], v_ref[...], acc, peak)

    def read(tile):
        bias_ref[...] = bias_where(count_along(bias_ref.shape, 1) + tile * TILE < keys)
        return *tile_of(row_ref, tile * TILE, TILE), bias_ref[...]

    def read_fast(step, masked):
        return read(tiles) if masked else (*tile_of(row_ref, step * TILE, TILE), None)

    for h in range(heads):
        start(h)
    for copy in copies:
        copy.wait()
    absorb(heads, view, part, tiles, read_fast)
    absorb_again(acc_ref, view, start, tiles + part, read)


def more_keys(q_ref, rest_ref, state_in, refs, used, firsts, pieces, steps):
    acc_ref, peak_ref, bank_ref, carried_ref, bias_ref, sems = refs
    acc_in, peak_in = sums(state_in)
    copies = [(peak_in, peak_ref, True), (acc_in, carried_ref, True)]
    copies += [(ref.at[pl.ds(0, KEEP)], bank_ref.at[pl.ds(0, KEEP)], on) for ref, on in firsts]
    for at, (ref, on) in enumerate(pieces):
        copies.append((ref, bank_ref.at[pl.ds(TILE + at * STEP, STEP)], on))
    copies = [
        (pltpu.make_async_copy(source, target, sems.at[at]), on)
        for at, (source, target, on) in enumerate(copies)
    ]

    def under(condition, act):
        if condition is True:
            act()
        else:
            pl.when(condition)(act)

    for one, on in copies:
        under(on, one.start)
    acc_ref[...] = jnp.zeros(acc_ref.shape, jnp.float32)
    bank_ref[KEEP:TILE] = rest_ref[: TILE - KEEP]
    number = wide(rest_ref[TILE - KEEP : TILE - KEEP + 1, :HEAD].astype(jnp.int32), TILE)
    at = count_along((1, TILE), 1)
    limit = jnp.where(at < KEEP, number, KEEP + used - number)
    bias_ref[0] = jnp.broadcast_to(bias_where(at < limit), bias_ref.shape[1:])
    bias_ref[1] = jnp.zeros(bias_ref.shape[1:], jnp.float32)
    view = head_view(q_ref, acc_ref, peak_ref)
    masked = sum(jnp.where(on, 1, 0) for _, on in firsts)

    def start(h):
        acc_ref[h] = carried_ref[h]

    def read(step):
        tile = jnp.where(masked > 0, step, step + 1)
        return *tile_of(bank_ref, tile * TILE, TILE), bias_ref[jnp.minimum(tile, 1)]

    here, later = copies[2 : 2 + len(firsts)], copies[2 + len(firsts) :]

    def read_fast(step, with_bias):
        if with_bias:
            for one, on in here:
                under(on, one.wait)
            return *tile_of(bank_ref, 0, TILE), bias_ref[0]
        for at, (one, on) in enumerate(later):
            pl.when(on & (step == at))(one.wait)
        return *tile_of(bank_ref, TILE + step * STEP, STEP), None

    copies[0][0].wait()
    absorb(acc_ref.shape[0], view, masked, steps, read_fast)
    copies[1][0].wait()
    acc_ref[...] += carried_ref[...]
    absorb_again(acc_ref, view, start, masked + STEP // TILE * steps, read)


def early_kernel(
    place_ref, q_ref, rest_ref, row_a, below_a, below_b, above_a, above_b, state_in, state_ref,
    *refs,
):
    mine, used = place_ref[0], place_ref[1]
    y = mine // WIDE
    firsts = (row_a, (mine > 0) & (y == 0)), (below_a, y == 1), (above_a, y == 3)
    pieces = (below_a, y > 0), (below_b, y > 0), (above_a, y == 3), (above_b, y == 3)
    steps = jnp.where(y == 3, 4, jnp.where(y > 0, 2, 0))
    refs = *sums(state_ref), *refs
    more_keys(q_ref, rest_ref, state_in, refs, used, firsts, pieces, steps)


def rest_kernel(
    place_ref, q_ref, rest_ref, below2_ref, above2_ref, weight_ref, state_in,
    own_out, far_out, near_out, own_ref, send_ref, w_ref, att_ref, out_sems, *refs,
):
    y, used = place_ref[0] // WIDE, place_ref[1]
    weight_copy = pltpu.make_async_copy(weight_ref, w_ref, out_sems.at[3])
    weight_copy.start()
    pieces = (below2_ref, y > 1), (above2_ref, y > 1)
    firsts = ((below2_ref, y == 2),)
    more_keys(q_ref, rest_ref, state_in, refs, used, firsts, pieces, jnp.where(y > 1, 2, 0))
    acc_ref = refs[0]
    for h in range(acc_ref.shape[0]):
        att_ref[:, h * HEAD : (h + 1) * HEAD] = (
            acc_ref[h, :, :HEAD] / acc_ref[h, :, HEAD:]
        ).astype(jnp.bfloat16)
    weight_copy.wait()
    chips, _, columns = own_out.shape
    chip, core = place_ref[2], place_ref[3]

    @pl.loop(0, chips)
    def _(step):
        ahead = jnp.where(step == 0, 2, jnp.where(step == 1, 1, jnp.where(step == 2, 3, 0)))
        column = lax.rem(chip + ahead, chips) * 2
        for ref, side in ((own_ref, core), (send_ref, 1 - core)):
            start = pl.multiple_of((column + side) * columns, columns)
            ref[step] = dot(att_ref[...], w_ref[:, pl.ds(start, columns)]).astype(jnp.bfloat16)
        pltpu.make_async_copy(own_ref.at[step], own_out.at[step], out_sems.at[0]).start()

        @pl.when(step == 0)
        def _():
            pltpu.make_async_copy(send_ref.at[0], far_out, out_sems.at[1]).start()

        @pl.when(step > 0)
        def _():
            target = near_out.at[step - 1]
            pltpu.make_async_copy(send_ref.at[step], target, out_sems.at[2]).start()

    pltpu.make_async_copy(own_ref, own_out, out_sems.at[0]).wait()
    pltpu.make_async_copy(send_ref.at[0], far_out, out_sems.at[1]).wait()
    pltpu.make_async_copy(send_ref.at[pl.ds(1, chips - 1)], near_out, out_sems.at[2]).wait()


def pack_row_kernel(place_ref, *refs):
    z = place_ref[0] % WIDE
    at, middle = KEEP, WIDE * KEEP // 2
    for ref in refs[:-2]:
        rows = ref.shape[0]
        start = pl.multiple_of(lax.rem(z * KEEP + at, WIDE * KEEP), KEEP // 2)
        at += rows
        for out_ref, first in zip(refs[-2:], (0, middle)):

            @pl.when((start >= first) & (start < first + middle))
            def _():
                out_ref[pl.ds(pl.multiple_of(start - first, KEEP // 2), rows)] = ref[...]


def pack_row(place, pieces):
    return pl.pallas_call(
        pack_row_kernel,
        out_shape=[jax.ShapeDtypeStruct((WIDE * KEEP // 2, 2 * HEAD), jnp.bfloat16)] * 2,
        in_specs=[SMEM] + [VMEM] * len(pieces),
        out_specs=[VMEM] * 2,
        compiler_params=pltpu.CompilerParams(vmem_limit_bytes=8 * 2**20),
        name="pack_row",
    )(place, *pieces)


def cost(rows, keys):
    return pl.CostEstimate(
        flops=rows * keys * HEAD * 8, bytes_accessed=8 * 2**20, transcendentals=rows * keys
    )


def state_of(length, heads):
    return jax.ShapeDtypeStruct((heads, length, 3 * HEAD), jnp.float32)


def work_of(length, heads, steps):
    return [
        pltpu.VMEM((TILE + steps * STEP, 2 * HEAD), jnp.bfloat16),
        pltpu.VMEM((heads, length, 2 * HEAD), jnp.float32),
        pltpu.VMEM((2, 8, TILE), jnp.float32),
        pltpu.SemaphoreType.DMA((9,)),
    ]


def own_row(place, queries, keys, values, row_a, row_b):
    length, width = queries.shape
    whole = lambda x: pl.BlockSpec(x.shape, lambda i: (0,) * x.ndim)
    state = state_of(length, width // HEAD)
    return pl.pallas_call(
        own_row_kernel,
        grid=(1,),
        out_shape=state,
        in_specs=[SMEM, *[whole(x) for x in (queries, keys, values)], ANY, ANY],
        out_specs=whole(state),
        scratch_shapes=[
            pltpu.VMEM((WIDE * KEEP, 2 * HEAD), jnp.bfloat16),
            pltpu.VMEM((8, TILE), jnp.float32),
            pltpu.SemaphoreType.DMA((2,)),
        ],
        compiler_params=PARAMS,
        cost_estimate=cost(length * width // HEAD, length + WIDE * KEEP),
        name="own_row",
    )(place, queries, keys, values, row_a, row_b)


def early_rows(place, queries, rest, banks, state):
    length, width = queries.shape
    heads = width // HEAD
    whole = lambda x: pl.BlockSpec(x.shape, lambda i: (0,) * len(x.shape))
    return pl.pallas_call(
        early_kernel,
        grid=(1,),
        out_shape=state_of(length, heads),
        in_specs=[SMEM, whole(queries), whole(rest), *[ANY] * (len(banks) + 1)],
        out_specs=whole(state),
        scratch_shapes=work_of(length, heads, 4),
        compiler_params=PARAMS,
        cost_estimate=cost(length * heads, TILE + 4 * STEP),
        name="early_rows",
    )(place, queries, rest, *banks, state)


def rest_rows(place, queries, rest, banks, weight, state, chips):
    length, width = queries.shape
    heads, keys = width // HEAD, TILE + 2 * STEP
    whole = lambda x: pl.BlockSpec(x.shape, lambda i: (0,) * len(x.shape))
    one = (length, weight.shape[1] // chips // 2)
    shapes = (chips, *one), one, (chips - 1, *one)
    return pl.pallas_call(
        rest_kernel,
        grid=(1,),
        out_shape=[jax.ShapeDtypeStruct(shape, jnp.bfloat16) for shape in shapes],
        in_specs=[SMEM, whole(queries), whole(rest), *[ANY] * (len(banks) + 2)],
        out_specs=[ANY] * 3,
        scratch_shapes=[
            *[pltpu.VMEM((chips, *one), jnp.bfloat16)] * 2,
            pltpu.VMEM(weight.shape, weight.dtype),
            pltpu.VMEM((length, width), jnp.bfloat16),
            pltpu.SemaphoreType.DMA((4,)),
            pltpu.VMEM((heads, length, 2 * HEAD), jnp.float32),
            pltpu.VMEM((heads, length, HEAD), jnp.float32),
            *work_of(length, heads, 2),
        ],
        compiler_params=pltpu.CompilerParams(vmem_limit_bytes=47 * 2**20),
        cost_estimate=cost(length * heads, keys),
        name="rest_rows",
    )(place, queries, rest, *banks, weight, state)


def summed(*refs):
    return sum(ref[...].astype(jnp.float32) for ref in refs)


def cross_kernel(own_ref, other_ref, upper_ref, lower_ref):
    total = summed(own_ref, other_ref).astype(jnp.bfloat16)
    half = upper_ref.shape[0]
    upper_ref[...] = total[:half]
    lower_ref[...] = total[half:]


def add_kernel(*refs):
    terms = refs[:-2]
    middle = len(terms) // 2
    refs[-2][...] = summed(*terms[:middle]).astype(jnp.bfloat16)
    refs[-1][...] = summed(*terms[middle:]).astype(jnp.bfloat16)


def halves_kernel(*refs):
    (*terms, upper_ref, lower_ref), out_ref = refs[:-1], refs[-1]
    half, total = upper_ref.shape[0], summed(*terms)
    out_ref[:half] = (total[:half] + summed(upper_ref)).astype(out_ref.dtype)
    out_ref[half:] = (total[half:] + summed(lower_ref)).astype(out_ref.dtype)


def small_call(kernel, name, terms, shapes, dtype=jnp.bfloat16):
    def spec(term):
        if not isinstance(term, tuple):
            return pl.BlockSpec(term.shape, lambda i: (0, 0))
        x, chunk, half = term
        rows = x.shape[1] // (1 if half is None else 2)
        return pl.BlockSpec((None, rows, x.shape[2]), lambda i: (chunk, half or 0, 0))

    return pl.pallas_call(
        kernel,
        grid=(1,),
        out_shape=[jax.ShapeDtypeStruct(shape, dtype) for shape in shapes],
        in_specs=[spec(term) for term in terms],
        out_specs=[pl.BlockSpec(shape, lambda i: (0, 0)) for shape in shapes],
        compiler_params=pltpu.CompilerParams(vmem_limit_bytes=8 * 2**20),
        name=name,
    )(*[term[0] if isinstance(term, tuple) else term for term in terms])


def on_device(queries, key_rows, value_rows, kept_positions, anchor_length, output_weight):
    mine, head = lax.axis_index("ctx"), lax.axis_index("head")
    length, devices, blocks = queries.shape[0], lax.axis_size("head"), lax.axis_size("ctx")
    chips, chip, core = devices // 2, head // 2, head % 2
    tall = blocks // WIDE
    swap = [(i, i ^ 1) for i in range(devices)]
    up = [(i, (i + 2) % devices) for i in range(devices)]
    down = [(i, (i - 2) % devices) for i in range(devices)]
    along = lambda step: [
        (r * WIDE + c, r * WIDE + (c + step) % WIDE) for r in range(tall) for c in range(WIDE)
    ]
    across = lambda hops: [(a * WIDE + c, b * WIDE + c) for a, b in hops for c in range(WIDE)]
    permute = lambda x, pairs: lax.ppermute(x, "ctx", pairs)

    spots = jnp.stack([chip, core]).astype(jnp.int32)
    place = jnp.concatenate([mine.astype(jnp.int32)[None], anchor_length, spots])
    kept, rest = select(anchor_length, kept_positions, key_rows, value_rows)

    plus, minus = along(1), along(-1)
    half = KEEP // 2
    left, right = [kept], [kept]
    rest = jnp.where(mine == 0, rest, jnp.zeros_like(rest))
    spread = lambda hops: [(r * WIDE + a, r * WIDE + b) for a, b in hops for r in range(tall)]
    upward = [(0, WIDE)], [(0, 3 * WIDE), (WIDE, 2 * WIDE)]
    for step in range(WIDE // 2 - 1):
        left.append(permute(left[-1], plus))
        right.append(permute(right[-1], minus))
        if step < len(upward):
            rest = rest + permute(rest, upward[step])
            left[-1], right[-1], rest = lax.optimization_barrier((left[-1], right[-1], rest))
    opposite = [permute(left[-1][:half], plus), permute(right[-1][half:], minus)]
    ends = pack_row(place, right[1:] + opposite + left[:0:-1] + [kept])

    below_a = permute(ends[0], across([(0, 1), (1, 2), (2, 3)]))
    above_b = permute(ends[1], across([(0, 3), (1, 0)]))
    rest, ends = lax.optimization_barrier((rest, ends))
    rest = rest + permute(rest, spread([(0, 4)]))
    rest, ends = lax.optimization_barrier((rest, ends))
    below_b = permute(ends[1], across([(0, 1), (1, 2), (2, 3)]))
    above_a = permute(ends[0], across([(0, 3)]))
    state = own_row(place, queries, key_rows, value_rows, *ends)
    rest, below_a, above_b, state = lax.optimization_barrier((rest, below_a, above_b, state))
    rest = rest + permute(rest, spread([(0, 2), (4, 6)]))
    below2 = permute(below_a, across([(1, 2), (2, 3)]))
    above2 = permute(above_b, across([(0, 3), (3, 2)]))
    rest = rest + permute(rest, spread([(0, 1), (2, 3), (4, 5), (6, 7)]))

    state = early_rows(place, queries, rest, (ends[0], below_a, below_b, above_a, above_b), state)
    own, far, near = rest_rows(
        place, queries, rest, (below2, above2), output_weight, state, chips
    )

    far, near = lax.optimization_barrier((lax.ppermute(far, "head", swap), near))
    near = lax.ppermute(near, "head", swap)
    columns = own.shape[2]
    whole, half = (length, columns), (length // 2, columns)
    upper, lower = small_call(cross_kernel, "cross", [(own, 0, None), far], [half, half])
    upper, lower = lax.ppermute(upper, "head", up), lax.ppermute(lower, "head", down)
    terms = [(own, 1, 1), (near, 0, 1), (own, 2, 0), (near, 1, 0)]
    lower_up, upper_down = small_call(add_kernel, "direct", terms, [half, half])
    upper, lower, _, _ = lax.optimization_barrier((upper, lower, lower_up, upper_down))
    lower_up, upper_down = lax.ppermute(lower_up, "head", up), lax.ppermute(upper_down, "head", down)
    terms = [(own, 1, 0), (near, 0, 0), upper, (own, 2, 1), (near, 1, 1), lower]
    upper_up, lower_down = small_call(add_kernel, "turn", terms, [half, half])
    upper_up, lower_down = lax.ppermute(upper_up, "head", up), lax.ppermute(lower_down, "head", down)
    terms = [(own, 3, None), (near, 2, None), upper_down, lower_up]
    (total,) = small_call(halves_kernel, "collect", terms, [whole], jnp.float32)
    return small_call(halves_kernel, "finish", [total, upper_up, lower_down], [whole])[0]


def solution(mesh):
    placed = (
        P("ctx", "head"),
        P("ctx", "head"),
        P("ctx", "head"),
        P("head", "ctx"),
        P("head"),
        P("head", None),
    )
    return jax.shard_map(
        on_device, mesh=mesh, in_specs=placed, out_specs=P("ctx", "head"), check_vma=False
    )
```

```python
import functools

import jax
import jax.numpy as jnp
from jax import lax
from jax.experimental import pallas as pl
from jax.experimental.pallas import tpu as pltpu
from jax.sharding import PartitionSpec as P

HEAD = 128
WIDE = 8
INFO = 16
KEEP = 256
LOG2E = 1.4426950408889634
FACTOR = HEAD**-0.5 * LOG2E
LIMIT = 2.0**100
NEGATIVE = -1e30
NT = (((1,), (1,)), ((), ()))
VMEM = pl.BlockSpec(memory_space=pltpu.VMEM)
SMEM = pl.BlockSpec(memory_space=pltpu.SMEM)
HBM = pl.BlockSpec(memory_space=pltpu.HBM)
ANY = pl.BlockSpec(memory_space=pl.ANY)
TILE = 512
STEP = 1024
PARAMS = pltpu.CompilerParams(vmem_limit_bytes=60 * 2**20)


def dot(a, b):
    return jnp.dot(a, b, preferred_element_type=jnp.float32)


def dot_nt(a, b):
    return lax.dot_general(a, b, NT, preferred_element_type=jnp.float32)


def count_along(shape, dim):
    return lax.broadcasted_iota(jnp.int32, shape, dim)


def ones_where(condition):
    return jnp.where(condition, 1.0, 0.0).astype(jnp.bfloat16)


def select_kernel(used_ref, *refs):
    sources, (kept_rows_ref, rest_ref), targets, sems = refs[:3], refs[3:5], refs[5:8], refs[8]
    copies = [
        pltpu.make_async_copy(source, target, sems.at[at])
        for at, (source, target) in enumerate(zip(sources, targets))
    ]
    for copy in copies:
        copy.start()
    for copy in copies:
        copy.wait()
    kept_ref, key_ref, value_ref = targets
    length, keep = key_ref.shape[0], kept_ref.shape[1]
    hit = ones_where(count_along((length, keep), 0) == kept_ref[...])
    kept = dot_nt(jnp.ones((8, keep), jnp.bfloat16), hit)
    square = (length, length)
    before = ones_where(count_along(square, 0) < count_along(square, 1))
    rank = dot(kept.astype(jnp.bfloat16), before)
    column = count_along((8, length), 1)
    place = jnp.where(kept > 0.5, rank, column.astype(jnp.float32) + keep - rank)
    order = ones_where(count_along(square, 0).astype(jnp.float32) == place[:1])
    for at, ref in enumerate((key_ref, value_ref)):
        columns = slice(at * HEAD, (at + 1) * HEAD)
        rows = dot(order, ref[...]).astype(jnp.bfloat16)
        kept_rows_ref[:, columns] = rows[:keep]
        rest_ref[: length - keep, columns] = rows[keep:]
    in_both = jnp.where((kept > 0.5) & (column < used_ref[0]), 1.0, 0.0)[:1]
    number = jnp.sum(in_both, axis=1, keepdims=True)
    rest_ref[length - keep :] = jnp.broadcast_to(number, (INFO, 2 * HEAD)).astype(jnp.bfloat16)


def select(used, kept, keys, values):
    length = keys.shape[0]
    rows = (KEEP, length - KEEP + INFO)
    return pl.pallas_call(
        select_kernel,
        out_shape=[jax.ShapeDtypeStruct((n, 2 * HEAD), jnp.bfloat16) for n in rows],
        in_specs=[SMEM, HBM, HBM, HBM],
        out_specs=[VMEM] * 2,
        scratch_shapes=[
            *[pltpu.VMEM(x.shape, x.dtype) for x in (kept, keys, values)],
            pltpu.SemaphoreType.DMA((3,)),
        ],
        compiler_params=PARAMS,
        name="select_kept",
    )(used, kept, keys, values)


def wide(column, width):
    return jnp.concatenate([column] * (width // HEAD), axis=1)


def widened(values):
    return jnp.concatenate([values, jnp.ones_like(values)], axis=1)


def scores(query, keys):
    return dot_nt(query, keys) * FACTOR


def local(query, keys, values, acc_ref, peak_ref):
    length = query.shape[0]
    causal = count_along((length, length), 1) <= count_along((length, length), 0)
    raw = jnp.where(causal, scores(query, keys), NEGATIVE)
    peak = jnp.broadcast_to(jnp.max(raw, axis=1, keepdims=True), (length, HEAD))
    peak_ref[...] = peak
    weights = jnp.exp2(raw - wide(peak, length)).astype(jnp.bfloat16)
    acc_ref[...] = dot(weights, widened(values))


def biased(raw, bias):
    if bias is None:
        return raw
    return (raw.reshape(-1, *bias.shape) + bias).reshape(raw.shape)


def fixed(heads, view, keys, values, bias):
    raw = scores(view(0)[0], keys)
    for h in range(heads):
        _, acc_ref, peak_ref = view(h)
        ahead = scores(view(h + 1)[0], keys) if h + 1 < heads else None
        weights = jnp.exp2(biased(raw, bias) - wide(peak_ref[...], keys.shape[0]))
        acc_ref[...] += dot(weights.astype(jnp.bfloat16), values)
        raw = ahead


def moving(query, acc_ref, peak_ref, keys, values, bias):
    raw = biased(scores(query, keys), bias)
    old = peak_ref[...]
    peak = jnp.maximum(old, jnp.max(raw, axis=1, keepdims=True))
    weights = jnp.exp2(raw - wide(peak, keys.shape[0])).astype(jnp.bfloat16)
    peak_ref[...] = peak
    acc_ref[...] = acc_ref[...] * wide(jnp.exp2(old - peak), 2 * HEAD) + dot(weights, values)


def absorb(heads, view, masked, steps, read):
    if masked is not None:

        @pl.loop(0, masked)
        def _(step):
            fixed(heads, view, *read(step, True))

    @pl.loop(0, steps)
    def _(step):
        fixed(heads, view, *read(step, False))


def absorb_again(acc_ref, view, start, tiles, read):
    largest = jnp.max(acc_ref[:, :, HEAD:])

    @pl.when(jnp.logical_not(largest < LIMIT))
    def _():
        @pl.loop(0, acc_ref.shape[0])
        def _(h):
            start(h)

            @pl.loop(0, tiles)
            def _(tile):
                moving(*view(h), *read(tile))


def tile_of(ref, start, size):
    rows = pl.ds(pl.multiple_of(start, TILE), size)
    return ref[rows, :HEAD], widened(ref[rows, HEAD:])


def head_view(q_ref, acc_ref, peak_ref):
    def view(h):
        columns = pl.ds(pl.multiple_of(h * HEAD, HEAD), HEAD)
        return q_ref[:, columns], acc_ref.at[h], peak_ref.at[h]

    return view


def bias_where(allowed):
    return jnp.where(allowed, 0.0, NEGATIVE)


def sums(state_ref):
    return state_ref.at[:, :, pl.ds(0, 2 * HEAD)], state_ref.at[:, :, pl.ds(2 * HEAD, HEAD)]


def own_row_kernel(
    place_ref, q_ref, k_ref, v_ref, row_a, row_b, state_ref, row_ref, bias_ref, sems
):
    acc_ref, peak_ref = sums(state_ref)
    keys = place_ref[0] % WIDE * KEEP
    tiles, part = keys // TILE, jnp.where(keys % TILE > 0, 1, 0)
    half = row_a.shape[0]
    copies = [
        pltpu.make_async_copy(ref, row_ref.at[pl.ds(at * half, half)], sems.at[at])
        for at, ref in enumerate((row_a, row_b))
    ]
    for copy in copies:
        copy.start()
    view, heads = head_view(q_ref, acc_ref, peak_ref), acc_ref.shape[0]

    def start(h):
        query, acc, peak = view(h)
        local(query, k_ref[...], v_ref[...], acc, peak)

    def read(tile):
        bias_ref[...] = bias_where(count_along(bias_ref.shape, 1) + tile * TILE < keys)
        return *tile_of(row_ref, tile * TILE, TILE), bias_ref[...]

    def read_fast(step, masked):
        return read(tiles) if masked else (*tile_of(row_ref, step * TILE, TILE), None)

    for h in range(heads):
        start(h)
    for copy in copies:
        copy.wait()
    absorb(heads, view, part, tiles, read_fast)
    absorb_again(acc_ref, view, start, tiles + part, read)


def more_keys(q_ref, rest_ref, state_in, refs, used, firsts, pieces, steps):
    acc_ref, peak_ref, bank_ref, carried_ref, bias_ref, sems = refs
    acc_in, peak_in = sums(state_in)
    copies = [(peak_in, peak_ref, True), (acc_in, carried_ref, True)]
    copies += [(ref.at[pl.ds(0, KEEP)], bank_ref.at[pl.ds(0, KEEP)], on) for ref, on in firsts]
    for at, (ref, on) in enumerate(pieces):
        copies.append((ref, bank_ref.at[pl.ds(TILE + at * STEP, STEP)], on))
    copies = [
        (pltpu.make_async_copy(source, target, sems.at[at]), on)
        for at, (source, target, on) in enumerate(copies)
    ]

    def under(condition, act):
        if condition is True:
            act()
        else:
            pl.when(condition)(act)

    for one, on in copies:
        under(on, one.start)
    acc_ref[...] = jnp.zeros(acc_ref.shape, jnp.float32)
    view, masked = head_view(q_ref, acc_ref, peak_ref), None
    if firsts:
        bank_ref[KEEP:TILE] = rest_ref[: TILE - KEEP]
        number = wide(rest_ref[TILE - KEEP : TILE - KEEP + 1, :HEAD].astype(jnp.int32), TILE)
        at = count_along((1, TILE), 1)
        limit = jnp.where(at < KEEP, number, KEEP + used - number)
        bias_ref[0] = jnp.broadcast_to(bias_where(at < limit), bias_ref.shape[1:])
        bias_ref[1] = jnp.zeros(bias_ref.shape[1:], jnp.float32)
        masked = sum(jnp.where(on, 1, 0) for _, on in firsts)

    def start(h):
        acc_ref[h] = carried_ref[h]

    def read(step):
        if masked is None:
            return *tile_of(bank_ref, TILE + step * TILE, TILE), None
        tile = jnp.where(masked > 0, step, step + 1)
        return *tile_of(bank_ref, tile * TILE, TILE), bias_ref[jnp.minimum(tile, 1)]

    here, later = copies[2 : 2 + len(firsts)], copies[2 + len(firsts) :]

    def read_fast(step, with_bias):
        if with_bias:
            for one, on in here:
                under(on, one.wait)
            return *tile_of(bank_ref, 0, TILE), bias_ref[0]
        for at, (one, on) in enumerate(later):
            pl.when(on & (step == at))(one.wait)
        return *tile_of(bank_ref, TILE + step * STEP, STEP), None

    copies[0][0].wait()
    absorb(acc_ref.shape[0], view, masked, steps, read_fast)
    copies[1][0].wait()
    acc_ref[...] += carried_ref[...]
    tiles = STEP // TILE * steps + (0 if masked is None else masked)
    absorb_again(acc_ref, view, start, tiles, read)


def early_kernel(place_ref, q_ref, below_ref, above_ref, state_in, state_ref, *refs):
    y = place_ref[0] // WIDE
    pieces = (below_ref, y > 0), (above_ref, y == 3)
    steps = jnp.where(y == 3, 2, jnp.minimum(y, 1))
    refs = *sums(state_ref), *refs
    more_keys(q_ref, None, state_in, refs, None, (), pieces, steps)


def hand_on_kernel(place_ref, q_ref, below_ref, above_ref, row_a, below_a, state_in, *refs):
    y = place_ref[0] // WIDE
    state_ref, first_ref, *refs, first_sem = refs
    copies = [
        (y == row, pltpu.make_async_copy(ref.at[pl.ds(0, KEEP)], first_ref, first_sem))
        for row, ref in ((0, row_a), (1, below_a), (3, above_ref))
    ]
    for on, copy in copies:
        pl.when(on)(copy.start)
    early_kernel(place_ref, q_ref, below_ref, above_ref, state_in, state_ref, *refs)
    for on, copy in copies:
        pl.when(on)(copy.wait)


def rest_kernel(
    place_ref, q_ref, rest_ref, first_ref, below2_ref, above2_ref, weight_ref, state_in,
    own_out, far_out, near_out, own_ref, send_ref, w_ref, att_ref, out_sems, *refs,
):
    mine, used = place_ref[0], place_ref[1]
    y = mine // WIDE
    weight_copy = pltpu.make_async_copy(weight_ref, w_ref, out_sems.at[3])
    weight_copy.start()
    pieces = (below2_ref, y > 1), (above2_ref, y > 1)
    firsts = (first_ref, (mine > 0) & (y != 2)), (below2_ref, y == 2)
    more_keys(q_ref, rest_ref, state_in, refs, used, firsts, pieces, jnp.where(y > 1, 2, 0))
    acc_ref = refs[0]
    for h in range(acc_ref.shape[0]):
        att_ref[:, h * HEAD : (h + 1) * HEAD] = (
            acc_ref[h, :, :HEAD] / acc_ref[h, :, HEAD:]
        ).astype(jnp.bfloat16)
    weight_copy.wait()
    chips, _, columns = own_out.shape
    chip, core = place_ref[2], place_ref[3]

    @pl.loop(0, chips)
    def _(step):
        ahead = jnp.where(step == 0, 2, jnp.where(step == 1, 1, jnp.where(step == 2, 3, 0)))
        column = lax.rem(chip + ahead, chips) * 2
        for ref, side in ((own_ref, core), (send_ref, 1 - core)):
            start = pl.multiple_of((column + side) * columns, columns)
            ref[step] = dot(att_ref[...], w_ref[:, pl.ds(start, columns)]).astype(jnp.bfloat16)
        pltpu.make_async_copy(own_ref.at[step], own_out.at[step], out_sems.at[0]).start()

        @pl.when(step == 0)
        def _():
            pltpu.make_async_copy(send_ref.at[0], far_out, out_sems.at[1]).start()

        @pl.when(step > 0)
        def _():
            target = near_out.at[step - 1]
            pltpu.make_async_copy(send_ref.at[step], target, out_sems.at[2]).start()

    pltpu.make_async_copy(own_ref, own_out, out_sems.at[0]).wait()
    pltpu.make_async_copy(send_ref.at[0], far_out, out_sems.at[1]).wait()
    pltpu.make_async_copy(send_ref.at[pl.ds(1, chips - 1)], near_out, out_sems.at[2]).wait()


def pack_row_kernel(place_ref, *refs):
    z = place_ref[0] % WIDE
    at, middle = KEEP, WIDE * KEEP // 2
    for ref in refs[:-2]:
        rows = ref.shape[0]
        start = pl.multiple_of(lax.rem(z * KEEP + at, WIDE * KEEP), KEEP // 2)
        at += rows
        for out_ref, first in zip(refs[-2:], (0, middle)):

            @pl.when((start >= first) & (start < first + middle))
            def _():
                out_ref[pl.ds(pl.multiple_of(start - first, KEEP // 2), rows)] = ref[...]


def pack_row(place, pieces):
    return pl.pallas_call(
        pack_row_kernel,
        out_shape=[jax.ShapeDtypeStruct((WIDE * KEEP // 2, 2 * HEAD), jnp.bfloat16)] * 2,
        in_specs=[SMEM] + [VMEM] * len(pieces),
        out_specs=[VMEM] * 2,
        compiler_params=pltpu.CompilerParams(vmem_limit_bytes=8 * 2**20),
        name="pack_row",
    )(place, *pieces)


def cost(rows, keys):
    return pl.CostEstimate(
        flops=rows * keys * HEAD * 8, bytes_accessed=8 * 2**20, transcendentals=rows * keys
    )


def state_of(length, heads):
    return jax.ShapeDtypeStruct((heads, length, 3 * HEAD), jnp.float32)


def work_of(length, heads, steps):
    return [
        pltpu.VMEM((TILE + steps * STEP, 2 * HEAD), jnp.bfloat16),
        pltpu.VMEM((heads, length, 2 * HEAD), jnp.float32),
        pltpu.VMEM((2, 8, TILE), jnp.float32),
        pltpu.SemaphoreType.DMA((9,)),
    ]


def own_row(place, queries, keys, values, row_a, row_b):
    length, width = queries.shape
    whole = lambda x: pl.BlockSpec(x.shape, lambda i: (0,) * x.ndim)
    state = state_of(length, width // HEAD)
    return pl.pallas_call(
        own_row_kernel,
        grid=(1,),
        out_shape=state,
        in_specs=[SMEM, *[whole(x) for x in (queries, keys, values)], ANY, ANY],
        out_specs=whole(state),
        scratch_shapes=[
            pltpu.VMEM((WIDE * KEEP, 2 * HEAD), jnp.bfloat16),
            pltpu.VMEM((8, TILE), jnp.float32),
            pltpu.SemaphoreType.DMA((2,)),
        ],
        compiler_params=PARAMS,
        cost_estimate=cost(length * width // HEAD, length + WIDE * KEEP),
        name="own_row",
    )(place, queries, keys, values, row_a, row_b)


def early_rows(place, queries, pieces, state, hand_on):
    length, width = queries.shape
    heads = width // HEAD
    whole = lambda x: pl.BlockSpec(x.shape, lambda i: (0,) * len(x.shape))
    sources = hand_on or ()
    first = jax.ShapeDtypeStruct((KEEP, 2 * HEAD), jnp.bfloat16)
    return pl.pallas_call(
        hand_on_kernel if hand_on else early_kernel,
        grid=(1,),
        out_shape=[state_of(length, heads)] + [first] * bool(hand_on),
        in_specs=[SMEM, whole(queries), *[ANY] * (len(pieces) + len(sources) + 1)],
        out_specs=[whole(state)] + [ANY] * bool(hand_on),
        scratch_shapes=work_of(length, heads, 2) + [pltpu.SemaphoreType.DMA] * bool(hand_on),
        compiler_params=PARAMS,
        cost_estimate=cost(length * heads, 2 * STEP),
        name="early_rows",
    )(place, queries, *pieces, *sources, state)


def rest_rows(place, queries, rest, banks, weight, state, chips):
    length, width = queries.shape
    heads, keys = width // HEAD, TILE + 2 * STEP
    whole = lambda x: pl.BlockSpec(x.shape, lambda i: (0,) * len(x.shape))
    one = (length, weight.shape[1] // chips // 2)
    shapes = (chips, *one), one, (chips - 1, *one)
    return pl.pallas_call(
        rest_kernel,
        grid=(1,),
        out_shape=[jax.ShapeDtypeStruct(shape, jnp.bfloat16) for shape in shapes],
        in_specs=[SMEM, whole(queries), whole(rest), *[ANY] * (len(banks) + 2)],
        out_specs=[ANY] * 3,
        scratch_shapes=[
            *[pltpu.VMEM((chips, *one), jnp.bfloat16)] * 2,
            pltpu.VMEM(weight.shape, weight.dtype),
            pltpu.VMEM((length, width), jnp.bfloat16),
            pltpu.SemaphoreType.DMA((4,)),
            pltpu.VMEM((heads, length, 2 * HEAD), jnp.float32),
            pltpu.VMEM((heads, length, HEAD), jnp.float32),
            *work_of(length, heads, 2),
        ],
        compiler_params=pltpu.CompilerParams(vmem_limit_bytes=47 * 2**20),
        cost_estimate=cost(length * heads, keys),
        name="rest_rows",
    )(place, queries, rest, *banks, weight, state)


def summed(*refs):
    return sum(ref[...].astype(jnp.float32) for ref in refs)


def cross_kernel(own_ref, other_ref, upper_ref, lower_ref):
    total = summed(own_ref, other_ref).astype(jnp.bfloat16)
    half = upper_ref.shape[0]
    upper_ref[...] = total[:half]
    lower_ref[...] = total[half:]


def add_kernel(*refs):
    terms = refs[:-2]
    middle = len(terms) // 2
    refs[-2][...] = summed(*terms[:middle]).astype(jnp.bfloat16)
    refs[-1][...] = summed(*terms[middle:]).astype(jnp.bfloat16)


def halves_kernel(*refs):
    (*terms, upper_ref, lower_ref), out_ref = refs[:-1], refs[-1]
    half, total = upper_ref.shape[0], summed(*terms)
    out_ref[:half] = (total[:half] + summed(upper_ref)).astype(out_ref.dtype)
    out_ref[half:] = (total[half:] + summed(lower_ref)).astype(out_ref.dtype)


def small_call(kernel, name, terms, shapes, dtype=jnp.bfloat16):
    def spec(term):
        if not isinstance(term, tuple):
            return pl.BlockSpec(term.shape, lambda i: (0, 0))
        x, chunk, half = term
        rows = x.shape[1] // (1 if half is None else 2)
        return pl.BlockSpec((None, rows, x.shape[2]), lambda i: (chunk, half or 0, 0))

    return pl.pallas_call(
        kernel,
        grid=(1,),
        out_shape=[jax.ShapeDtypeStruct(shape, dtype) for shape in shapes],
        in_specs=[spec(term) for term in terms],
        out_specs=[pl.BlockSpec(shape, lambda i: (0, 0)) for shape in shapes],
        compiler_params=pltpu.CompilerParams(vmem_limit_bytes=8 * 2**20),
        name=name,
    )(*[term[0] if isinstance(term, tuple) else term for term in terms])


def on_device(queries, key_rows, value_rows, kept_positions, anchor_length, output_weight):
    mine, head = lax.axis_index("ctx"), lax.axis_index("head")
    length, devices, blocks = queries.shape[0], lax.axis_size("head"), lax.axis_size("ctx")
    chips, chip, core = devices // 2, head // 2, head % 2
    tall = blocks // WIDE
    swap = [(i, i ^ 1) for i in range(devices)]
    up = [(i, (i + 2) % devices) for i in range(devices)]
    down = [(i, (i - 2) % devices) for i in range(devices)]
    along = lambda step: [
        (r * WIDE + c, r * WIDE + (c + step) % WIDE) for r in range(tall) for c in range(WIDE)
    ]
    across = lambda hops: [(a * WIDE + c, b * WIDE + c) for a, b in hops for c in range(WIDE)]
    permute = lambda x, pairs: lax.ppermute(x, "ctx", pairs)

    spots = jnp.stack([chip, core]).astype(jnp.int32)
    place = jnp.concatenate([mine.astype(jnp.int32)[None], anchor_length, spots])
    kept, rest = select(anchor_length, kept_positions, key_rows, value_rows)

    plus, minus = along(1), along(-1)
    half = KEEP // 2
    left, right = [kept], [kept]
    rest = jnp.where(mine == 0, rest, jnp.zeros_like(rest))
    spread = lambda hops: [(r * WIDE + a, r * WIDE + b) for a, b in hops for r in range(tall)]
    upward = [(0, WIDE)], [(0, 3 * WIDE), (WIDE, 2 * WIDE)]
    for step in range(WIDE // 2 - 1):
        left.append(permute(left[-1], plus))
        right.append(permute(right[-1], minus))
        if step < len(upward):
            rest = rest + permute(rest, upward[step])
            left[-1], right[-1], rest = lax.optimization_barrier((left[-1], right[-1], rest))
    opposite = [permute(left[-1][:half], plus), permute(right[-1][half:], minus)]
    ends = pack_row(place, right[1:] + opposite + left[:0:-1] + [kept])

    below_a = permute(ends[0], across([(0, 1), (1, 2), (2, 3)]))
    above_b = permute(ends[1], across([(0, 3), (1, 0)]))
    rest, ends = lax.optimization_barrier((rest, ends))
    rest = rest + permute(rest, spread([(0, 4)]))
    state = own_row(place, queries, key_rows, value_rows, *ends)
    rest, below_a, above_b, state, ends = lax.optimization_barrier(
        (rest, below_a, above_b, state, ends)
    )
    below_b = permute(ends[1], across([(0, 1), (1, 2), (2, 3)]))
    above_a = permute(ends[0], across([(0, 3)]))
    rest = rest + permute(rest, spread([(0, 2), (4, 6)]))
    (state,) = early_rows(place, queries, (below_a, above_b), state, None)
    rest, below_a, above_b, below_b, above_a, state = lax.optimization_barrier(
        (rest, below_a, above_b, below_b, above_a, state)
    )
    below2 = permute(below_a, across([(1, 2), (2, 3)]))
    above2 = permute(above_b, across([(0, 3), (3, 2)]))
    rest = rest + permute(rest, spread([(0, 1), (2, 3), (4, 5), (6, 7)]))
    state, first = early_rows(place, queries, (below_b, above_a), state, (ends[0], below_a))
    own, far, near = rest_rows(
        place, queries, rest, (first, below2, above2), output_weight, state, chips
    )

    far, near = lax.optimization_barrier((lax.ppermute(far, "head", swap), near))
    near = lax.ppermute(near, "head", swap)
    columns = own.shape[2]
    whole, half = (length, columns), (length // 2, columns)
    upper, lower = small_call(cross_kernel, "cross", [(own, 0, None), far], [half, half])
    upper, lower = lax.ppermute(upper, "head", up), lax.ppermute(lower, "head", down)
    terms = [(own, 1, 1), (near, 0, 1), (own, 2, 0), (near, 1, 0)]
    lower_up, upper_down = small_call(add_kernel, "direct", terms, [half, half])
    upper, lower, _, _ = lax.optimization_barrier((upper, lower, lower_up, upper_down))
    lower_up, upper_down = lax.ppermute(lower_up, "head", up), lax.ppermute(upper_down, "head", down)
    terms = [(own, 1, 0), (near, 0, 0), upper, (own, 2, 1), (near, 1, 1), lower]
    upper_up, lower_down = small_call(add_kernel, "turn", terms, [half, half])
    upper_up, lower_down = lax.ppermute(upper_up, "head", up), lax.ppermute(lower_down, "head", down)
    terms = [(own, 3, None), (near, 2, None), upper_down, lower_up]
    (total,) = small_call(halves_kernel, "collect", terms, [whole], jnp.float32)
    return small_call(halves_kernel, "finish", [total, upper_up, lower_down], [whole])[0]


def solution(mesh):
    placed = (
        P("ctx", "head"),
        P("ctx", "head"),
        P("ctx", "head"),
        P("head", "ctx"),
        P("head"),
        P("head", None),
    )
    return jax.shard_map(
        on_device, mesh=mesh, in_specs=placed, out_specs=P("ctx", "head"), check_vma=False
    )
```

```python
import functools

import jax
import jax.numpy as jnp
from jax import lax
from jax.experimental import pallas as pl
from jax.experimental.pallas import tpu as pltpu
from jax.sharding import PartitionSpec as P

HEAD = 128
WIDE = 8
INFO = 16
KEEP = 256
LOG2E = 1.4426950408889634
FACTOR = HEAD**-0.5 * LOG2E
LIMIT = 2.0**100
NEGATIVE = -1e30
NT = (((1,), (1,)), ((), ()))
VMEM = pl.BlockSpec(memory_space=pltpu.VMEM)
SMEM = pl.BlockSpec(memory_space=pltpu.SMEM)
HBM = pl.BlockSpec(memory_space=pltpu.HBM)
ANY = pl.BlockSpec(memory_space=pl.ANY)
TILE = 512
STEP = 1024
PARAMS = pltpu.CompilerParams(vmem_limit_bytes=60 * 2**20)


def dot(a, b):
    return jnp.dot(a, b, preferred_element_type=jnp.float32)


def dot_nt(a, b):
    return lax.dot_general(a, b, NT, preferred_element_type=jnp.float32)


def count_along(shape, dim):
    return lax.broadcasted_iota(jnp.int32, shape, dim)


def ones_where(condition):
    return jnp.where(condition, 1.0, 0.0).astype(jnp.bfloat16)


def select_kernel(used_ref, *refs):
    sources, (kept_rows_ref, rest_ref), targets, sems = refs[:3], refs[3:5], refs[5:8], refs[8]
    copies = [
        pltpu.make_async_copy(source, target, sems.at[at])
        for at, (source, target) in enumerate(zip(sources, targets))
    ]
    for copy in copies:
        copy.start()
    for copy in copies:
        copy.wait()
    kept_ref, key_ref, value_ref = targets
    length, keep = key_ref.shape[0], kept_ref.shape[1]
    hit = ones_where(count_along((length, keep), 0) == kept_ref[...])
    kept = dot_nt(jnp.ones((8, keep), jnp.bfloat16), hit)
    square = (length, length)
    before = ones_where(count_along(square, 0) < count_along(square, 1))
    rank = dot(kept.astype(jnp.bfloat16), before)
    column = count_along((8, length), 1)
    place = jnp.where(kept > 0.5, rank, column.astype(jnp.float32) + keep - rank)
    order = ones_where(count_along(square, 0).astype(jnp.float32) == place[:1])
    for at, ref in enumerate((key_ref, value_ref)):
        columns = slice(at * HEAD, (at + 1) * HEAD)
        rows = dot(order, ref[...]).astype(jnp.bfloat16)
        kept_rows_ref[:, columns] = rows[:keep]
        rest_ref[: length - keep, columns] = rows[keep:]
    in_both = jnp.where((kept > 0.5) & (column < used_ref[0]), 1.0, 0.0)[:1]
    number = jnp.sum(in_both, axis=1, keepdims=True)
    rest_ref[length - keep :] = jnp.broadcast_to(number, (INFO, 2 * HEAD)).astype(jnp.bfloat16)


def select(used, kept, keys, values):
    length = keys.shape[0]
    rows = (KEEP, length - KEEP + INFO)
    return pl.pallas_call(
        select_kernel,
        out_shape=[jax.ShapeDtypeStruct((n, 2 * HEAD), jnp.bfloat16) for n in rows],
        in_specs=[SMEM, HBM, HBM, HBM],
        out_specs=[VMEM] * 2,
        scratch_shapes=[
            *[pltpu.VMEM(x.shape, x.dtype) for x in (kept, keys, values)],
            pltpu.SemaphoreType.DMA((3,)),
        ],
        compiler_params=PARAMS,
        name="select_kept",
    )(used, kept, keys, values)


def wide(column, width):
    return jnp.concatenate([column] * (width // HEAD), axis=1)


def widened(values):
    return jnp.concatenate([values, jnp.ones_like(values)], axis=1)


def scores(query, keys):
    return dot_nt(query, keys) * FACTOR


def local(query, keys, values, acc_ref, peak_ref):
    length = query.shape[0]
    causal = count_along((length, length), 1) <= count_along((length, length), 0)
    raw = jnp.where(causal, scores(query, keys), NEGATIVE)
    peak = jnp.broadcast_to(jnp.max(raw, axis=1, keepdims=True), (length, HEAD))
    peak_ref[...] = peak
    weights = jnp.exp2(raw - wide(peak, length)).astype(jnp.bfloat16)
    acc_ref[...] = dot(weights, widened(values))


def biased(raw, bias):
    if bias is None:
        return raw
    return (raw.reshape(-1, *bias.shape) + bias).reshape(raw.shape)


def fixed(heads, view, keys, values, bias):
    raw = scores(view(0)[0], keys)
    for h in range(heads):
        _, acc_ref, peak_ref = view(h)
        ahead = scores(view(h + 1)[0], keys) if h + 1 < heads else None
        weights = jnp.exp2(biased(raw, bias) - wide(peak_ref[...], keys.shape[0]))
        acc_ref[...] += dot(weights.astype(jnp.bfloat16), values)
        raw = ahead


def moving(query, acc_ref, peak_ref, keys, values, bias):
    raw = biased(scores(query, keys), bias)
    old = peak_ref[...]
    peak = jnp.maximum(old, jnp.max(raw, axis=1, keepdims=True))
    weights = jnp.exp2(raw - wide(peak, keys.shape[0])).astype(jnp.bfloat16)
    peak_ref[...] = peak
    acc_ref[...] = acc_ref[...] * wide(jnp.exp2(old - peak), 2 * HEAD) + dot(weights, values)


def absorb(heads, view, masked, steps, read):
    if masked is not None:

        @pl.loop(0, masked)
        def _(step):
            fixed(heads, view, *read(step, True))

    @pl.loop(0, steps)
    def _(step):
        fixed(heads, view, *read(step, False))


def absorb_again(acc_ref, view, start, tiles, read):
    largest = jnp.max(acc_ref[:, :, HEAD:])

    @pl.when(jnp.logical_not(largest < LIMIT))
    def _():
        @pl.loop(0, acc_ref.shape[0])
        def _(h):
            start(h)

            @pl.loop(0, tiles)
            def _(tile):
                moving(*view(h), *read(tile))


def tile_of(ref, start, size):
    rows = pl.ds(pl.multiple_of(start, TILE), size)
    return ref[rows, :HEAD], widened(ref[rows, HEAD:])


def head_view(q_ref, acc_ref, peak_ref):
    def view(h):
        columns = pl.ds(pl.multiple_of(h * HEAD, HEAD), HEAD)
        return q_ref[:, columns], acc_ref.at[h], peak_ref.at[h]

    return view


def bias_where(allowed):
    return jnp.where(allowed, 0.0, NEGATIVE)


def sums(state_ref):
    return state_ref.at[:, :, pl.ds(0, 2 * HEAD)], state_ref.at[:, :, pl.ds(2 * HEAD, HEAD)]


def own_row_kernel(
    place_ref, q_ref, k_ref, v_ref, row_a, row_b, below_a, above_b, state_ref, first_ref,
    bank_ref, bias_ref, sems,
):
    y, z = place_ref[0] // WIDE, place_ref[0] % WIDE
    acc_ref, peak_ref = sums(state_ref)
    keys, half = z * KEEP, row_a.shape[0]
    row_steps = keys // STEP
    masked = (keys - row_steps * STEP + TILE - 1) // TILE
    copies = [
        (row_a, bank_ref.at[pl.ds(0, half)], z >= 0),
        (row_b, bank_ref.at[pl.ds(half, half)], z >= 0),
        (below_a, bank_ref.at[pl.ds(2 * half, half)], y > 0),
        (above_b, bank_ref.at[pl.ds(3 * half, half)], y == 3),
        (row_a.at[pl.ds(0, KEEP)], first_ref, y == 0),
        (below_a.at[pl.ds(0, KEEP)], first_ref, y == 1),
    ]
    copies = [
        (pltpu.make_async_copy(source, target, sems.at[at]), on)
        for at, (source, target, on) in enumerate(copies)
    ]
    for one, on in copies:
        pl.when(on)(one.start)
    view, heads = head_view(q_ref, acc_ref, peak_ref), acc_ref.shape[0]

    def start(h):
        query, acc, peak = view(h)
        local(query, k_ref[...], v_ref[...], acc, peak)

    def read_masked(tile):
        at = row_steps * STEP + tile * TILE
        bias_ref[...] = bias_where(count_along(bias_ref.shape, 1) + at < keys)
        return *tile_of(bank_ref, at, TILE), bias_ref[...]

    def step_start(step):
        return jnp.where(step < row_steps, step, step - row_steps + 2 * half // STEP) * STEP

    def read_fast(step, with_bias):
        if with_bias:
            return read_masked(step)
        for at, (one, on) in enumerate(copies[2:4]):
            pl.when(on & (step == row_steps + at))(one.wait)
        return *tile_of(bank_ref, step_start(step), STEP), None

    def read(tile):
        after = jnp.maximum(tile - masked, 0)
        plain = step_start(after // 2) + after % 2 * TILE
        at = jnp.where(tile < masked, row_steps * STEP + tile * TILE, plain)
        limit = jnp.where(tile < masked, keys, bank_ref.shape[0])
        bias_ref[...] = bias_where(count_along(bias_ref.shape, 1) + at < limit)
        return *tile_of(bank_ref, at, TILE), bias_ref[...]

    for h in range(heads):
        start(h)
    for one, on in copies[:2]:
        pl.when(on)(one.wait)
    steps = row_steps + jnp.where(y == 3, 2, jnp.minimum(y, 1))
    absorb(heads, view, masked, steps, read_fast)
    absorb_again(acc_ref, view, start, masked + STEP // TILE * steps, read)
    for one, on in copies[4:]:
        pl.when(on)(one.wait)


def more_keys(queries, rest_ref, state_in, refs, used, firsts, pieces, steps, then):
    acc_ref, peak_ref, q_ref, bank_ref, carried_ref, bias_ref, sems = refs
    acc_in, peak_in = sums(state_in)
    copies = [(queries, q_ref, True), (peak_in, peak_ref, True)]
    copies += [(ref.at[pl.ds(0, KEEP)], bank_ref.at[pl.ds(0, KEEP)], on) for ref, on in firsts]
    for at, (ref, on) in enumerate(pieces):
        copies.append((ref, bank_ref.at[pl.ds(TILE + at * STEP, STEP)], on))
    copies.append((acc_in, carried_ref, True))
    copies = [
        (pltpu.make_async_copy(source, target, sems.at[at]), on)
        for at, (source, target, on) in enumerate(copies)
    ]

    def under(condition, act):
        if condition is True:
            act()
        else:
            pl.when(condition)(act)

    for one, on in copies:
        under(on, one.start)
    then()
    acc_ref[...] = jnp.zeros(acc_ref.shape, jnp.float32)
    view, masked = head_view(q_ref, acc_ref, peak_ref), None
    if firsts:
        bank_ref[KEEP:TILE] = rest_ref[: TILE - KEEP]
        number = wide(rest_ref[TILE - KEEP : TILE - KEEP + 1, :HEAD].astype(jnp.int32), TILE)
        at = count_along((1, TILE), 1)
        limit = jnp.where(at < KEEP, number, KEEP + used - number)
        bias_ref[0] = jnp.broadcast_to(bias_where(at < limit), bias_ref.shape[1:])
        bias_ref[1] = jnp.zeros(bias_ref.shape[1:], jnp.float32)
        masked = sum(jnp.where(on, 1, 0) for _, on in firsts)

    def start(h):
        acc_ref[h] = carried_ref[h]

    def read(step):
        if masked is None:
            return *tile_of(bank_ref, TILE + step * TILE, TILE), None
        tile = jnp.where(masked > 0, step, step + 1)
        return *tile_of(bank_ref, tile * TILE, TILE), bias_ref[jnp.minimum(tile, 1)]

    here, later = copies[2 : 2 + len(firsts)], copies[2 + len(firsts) : -1]

    def read_fast(step, with_bias):
        if with_bias:
            for one, on in here:
                under(on, one.wait)
            return *tile_of(bank_ref, 0, TILE), bias_ref[0]
        for at, (one, on) in enumerate(later):
            pl.when(on & (step == at))(one.wait)
        return *tile_of(bank_ref, TILE + step * STEP, STEP), None

    for one, _ in copies[:2]:
        one.wait()
    absorb(acc_ref.shape[0], view, masked, steps, read_fast)
    copies[-1][0].wait()
    acc_ref[...] += carried_ref[...]
    tiles = STEP // TILE * steps + (0 if masked is None else masked)
    absorb_again(acc_ref, view, start, tiles, read)


def rest_kernel(
    place_ref, rest_ref, queries, first_ref, below_b, above_a, below2_ref, above2_ref, weight_ref, state_in,
    own_out, far_out, near_out, own_ref, send_ref, w_ref, att_ref, out_sems, *refs,
):
    mine, used = place_ref[0], place_ref[1]
    y = mine // WIDE
    pieces = (below_b, y > 0), (below2_ref, y > 1), (above2_ref, y > 1), (above_a, y == 3)
    firsts = (first_ref, (mine > 0) & (y < 2)), (below2_ref, y == 2), (above_a, y == 3)
    steps = jnp.where(y == 3, 4, jnp.where(y == 2, 3, y))
    weight_copy = pltpu.make_async_copy(weight_ref, w_ref, out_sems.at[3])
    more_keys(
        queries, rest_ref, state_in, refs, used, firsts, pieces, steps, weight_copy.start
    )
    acc_ref = refs[0]
    for h in range(acc_ref.shape[0]):
        att_ref[:, h * HEAD : (h + 1) * HEAD] = (
            acc_ref[h, :, :HEAD] / acc_ref[h, :, HEAD:]
        ).astype(jnp.bfloat16)
    weight_copy.wait()
    chips, _, columns = own_out.shape
    chip, core = place_ref[2], place_ref[3]

    @pl.loop(0, chips)
    def _(step):
        ahead = jnp.where(step == 0, 2, jnp.where(step == 1, 1, jnp.where(step == 2, 3, 0)))
        column = lax.rem(chip + ahead, chips) * 2
        for ref, side in ((own_ref, core), (send_ref, 1 - core)):
            start = pl.multiple_of((column + side) * columns, columns)
            ref[step] = dot(att_ref[...], w_ref[:, pl.ds(start, columns)]).astype(jnp.bfloat16)
        pltpu.make_async_copy(own_ref.at[step], own_out.at[step], out_sems.at[0]).start()

        @pl.when(step == 0)
        def _():
            pltpu.make_async_copy(send_ref.at[0], far_out, out_sems.at[1]).start()

        @pl.when(step > 0)
        def _():
            target = near_out.at[step - 1]
            pltpu.make_async_copy(send_ref.at[step], target, out_sems.at[2]).start()

    pltpu.make_async_copy(own_ref, own_out, out_sems.at[0]).wait()
    pltpu.make_async_copy(send_ref.at[0], far_out, out_sems.at[1]).wait()
    pltpu.make_async_copy(send_ref.at[pl.ds(1, chips - 1)], near_out, out_sems.at[2]).wait()


def pack_row_kernel(place_ref, *refs):
    z = place_ref[0] % WIDE
    at, middle = KEEP, WIDE * KEEP // 2
    for ref in refs[:-2]:
        rows = ref.shape[0]
        start = pl.multiple_of(lax.rem(z * KEEP + at, WIDE * KEEP), KEEP // 2)
        at += rows
        for out_ref, first in zip(refs[-2:], (0, middle)):

            @pl.when((start >= first) & (start < first + middle))
            def _():
                out_ref[pl.ds(pl.multiple_of(start - first, KEEP // 2), rows)] = ref[...]


def pack_row(place, pieces):
    return pl.pallas_call(
        pack_row_kernel,
        out_shape=[jax.ShapeDtypeStruct((WIDE * KEEP // 2, 2 * HEAD), jnp.bfloat16)] * 2,
        in_specs=[SMEM] + [VMEM] * len(pieces),
        out_specs=[VMEM] * 2,
        compiler_params=pltpu.CompilerParams(vmem_limit_bytes=8 * 2**20),
        name="pack_row",
    )(place, *pieces)


def cost(rows, keys):
    return pl.CostEstimate(
        flops=rows * keys * HEAD * 8, bytes_accessed=8 * 2**20, transcendentals=rows * keys
    )


def state_of(length, heads):
    return jax.ShapeDtypeStruct((heads, length, 3 * HEAD), jnp.float32)


def own_row(place, queries, keys, values, *pieces):
    length, width = queries.shape
    whole = lambda x: pl.BlockSpec(x.shape, lambda i: (0,) * len(x.shape))
    state = state_of(length, width // HEAD)
    first = jax.ShapeDtypeStruct((KEEP, 2 * HEAD), jnp.bfloat16)
    return pl.pallas_call(
        own_row_kernel,
        grid=(1,),
        out_shape=[state, first],
        in_specs=[SMEM, *[whole(x) for x in (queries, keys, values)], *[ANY] * len(pieces)],
        out_specs=[whole(state), ANY],
        scratch_shapes=[
            pltpu.VMEM((4 * STEP, 2 * HEAD), jnp.bfloat16),
            pltpu.VMEM((8, TILE), jnp.float32),
            pltpu.SemaphoreType.DMA((6,)),
        ],
        compiler_params=PARAMS,
        cost_estimate=cost(length * width // HEAD, length + 4 * STEP),
        name="own_row",
    )(place, queries, keys, values, *pieces)


def rest_rows(place, queries, rest, banks, weight, state, chips):
    length, width = queries.shape
    heads, keys = width // HEAD, TILE + 4 * STEP
    whole = lambda x: pl.BlockSpec(x.shape, lambda i: (0,) * len(x.shape))
    one = (length, weight.shape[1] // chips // 2)
    shapes = (chips, *one), one, (chips - 1, *one)
    return pl.pallas_call(
        rest_kernel,
        grid=(1,),
        out_shape=[jax.ShapeDtypeStruct(shape, jnp.bfloat16) for shape in shapes],
        in_specs=[SMEM, whole(rest), *[ANY] * (len(banks) + 3)],
        out_specs=[ANY] * 3,
        scratch_shapes=[
            *[pltpu.VMEM((chips, *one), jnp.bfloat16)] * 2,
            pltpu.VMEM(weight.shape, weight.dtype),
            pltpu.VMEM((length, width), jnp.bfloat16),
            pltpu.SemaphoreType.DMA((4,)),
            pltpu.VMEM((heads, length, 2 * HEAD), jnp.float32),
            pltpu.VMEM((heads, length, HEAD), jnp.float32),
            pltpu.VMEM((length, width), jnp.bfloat16),
            pltpu.VMEM((keys, 2 * HEAD), jnp.bfloat16),
            pltpu.VMEM((heads, length, 2 * HEAD), jnp.float32),
            pltpu.VMEM((2, 8, TILE), jnp.float32),
            pltpu.SemaphoreType.DMA((10,)),
        ],
        compiler_params=pltpu.CompilerParams(vmem_limit_bytes=47 * 2**20),
        cost_estimate=cost(length * heads, keys),
        name="rest_rows",
    )(place, rest, queries, *banks, weight, state)


def summed(*refs):
    return sum(ref[...].astype(jnp.float32) for ref in refs)


def cross_kernel(own_ref, other_ref, upper_ref, lower_ref):
    total = summed(own_ref, other_ref).astype(jnp.bfloat16)
    half = upper_ref.shape[0]
    upper_ref[...] = total[:half]
    lower_ref[...] = total[half:]


def add_kernel(*refs):
    terms = refs[:-2]
    middle = len(terms) // 2
    refs[-2][...] = summed(*terms[:middle]).astype(jnp.bfloat16)
    refs[-1][...] = summed(*terms[middle:]).astype(jnp.bfloat16)


def halves_kernel(*refs):
    (*terms, upper_ref, lower_ref), out_ref = refs[:-1], refs[-1]
    half, total = upper_ref.shape[0], summed(*terms)
    out_ref[:half] = (total[:half] + summed(upper_ref)).astype(out_ref.dtype)
    out_ref[half:] = (total[half:] + summed(lower_ref)).astype(out_ref.dtype)


def small_call(kernel, name, terms, shapes, dtype=jnp.bfloat16):
    def spec(term):
        if not isinstance(term, tuple):
            return pl.BlockSpec(term.shape, lambda i: (0, 0))
        x, chunk, half = term
        rows = x.shape[1] // (1 if half is None else 2)
        return pl.BlockSpec((None, rows, x.shape[2]), lambda i: (chunk, half or 0, 0))

    return pl.pallas_call(
        kernel,
        grid=(1,),
        out_shape=[jax.ShapeDtypeStruct(shape, dtype) for shape in shapes],
        in_specs=[spec(term) for term in terms],
        out_specs=[pl.BlockSpec(shape, lambda i: (0, 0)) for shape in shapes],
        compiler_params=pltpu.CompilerParams(vmem_limit_bytes=8 * 2**20),
        name=name,
    )(*[term[0] if isinstance(term, tuple) else term for term in terms])


def on_device(queries, key_rows, value_rows, kept_positions, anchor_length, output_weight):
    mine, head = lax.axis_index("ctx"), lax.axis_index("head")
    length, devices, blocks = queries.shape[0], lax.axis_size("head"), lax.axis_size("ctx")
    chips, chip, core = devices // 2, head // 2, head % 2
    tall = blocks // WIDE
    swap = [(i, i ^ 1) for i in range(devices)]
    up = [(i, (i + 2) % devices) for i in range(devices)]
    down = [(i, (i - 2) % devices) for i in range(devices)]
    along = lambda step: [
        (r * WIDE + c, r * WIDE + (c + step) % WIDE) for r in range(tall) for c in range(WIDE)
    ]
    across = lambda hops: [(a * WIDE + c, b * WIDE + c) for a, b in hops for c in range(WIDE)]
    permute = lambda x, pairs: lax.ppermute(x, "ctx", pairs)

    spots = jnp.stack([chip, core]).astype(jnp.int32)
    place = jnp.concatenate([mine.astype(jnp.int32)[None], anchor_length, spots])
    kept, rest = select(anchor_length, kept_positions, key_rows, value_rows)

    plus, minus = along(1), along(-1)
    half = KEEP // 2
    left, right = [kept], [kept]
    rest = jnp.where(mine == 0, rest, jnp.zeros_like(rest))
    spread = lambda hops: [(r * WIDE + a, r * WIDE + b) for a, b in hops for r in range(tall)]
    upward = [(0, WIDE)], [(0, 3 * WIDE), (WIDE, 2 * WIDE)]
    for step in range(WIDE // 2 - 1):
        left.append(permute(left[-1], plus))
        right.append(permute(right[-1], minus))
        if step < len(upward):
            rest = rest + permute(rest, upward[step])
            left[-1], right[-1], rest = lax.optimization_barrier((left[-1], right[-1], rest))
    opposite = [permute(left[-1][:half], plus), permute(right[-1][half:], minus)]
    ends = pack_row(place, right[1:] + opposite + left[:0:-1] + [kept])

    below_a = permute(ends[0], across([(0, 1), (1, 2), (2, 3)]))
    above_b = permute(ends[1], across([(0, 3), (1, 0)]))
    rest, ends = lax.optimization_barrier((rest, ends))
    rest = rest + permute(rest, spread([(0, 4)]))
    rest = rest + permute(rest, spread([(0, 2), (4, 6)]))
    rest, below_a, above_b, ends = lax.optimization_barrier((rest, below_a, above_b, ends))
    below_b = permute(ends[1], across([(0, 1), (1, 2), (2, 3)]))
    above_a = permute(ends[0], across([(0, 3)]))
    below2 = permute(below_a, across([(1, 2), (2, 3)]))
    above2 = permute(above_b, across([(0, 3), (3, 2)]))
    rest = rest + permute(rest, spread([(0, 1), (2, 3), (4, 5), (6, 7)]))
    state, first = own_row(place, queries, key_rows, value_rows, *ends, below_a, above_b)
    banks = (first, below_b, above_a, below2, above2)
    own, far, near = rest_rows(place, queries, rest, banks, output_weight, state, chips)

    far, near = lax.optimization_barrier((lax.ppermute(far, "head", swap), near))
    near = lax.ppermute(near, "head", swap)
    columns = own.shape[2]
    whole, half = (length, columns), (length // 2, columns)
    upper, lower = small_call(cross_kernel, "cross", [(own, 0, None), far], [half, half])
    upper, lower = lax.ppermute(upper, "head", up), lax.ppermute(lower, "head", down)
    terms = [(own, 1, 1), (near, 0, 1), (own, 2, 0), (near, 1, 0)]
    lower_up, upper_down = small_call(add_kernel, "direct", terms, [half, half])
    upper, lower, _, _ = lax.optimization_barrier((upper, lower, lower_up, upper_down))
    lower_up, upper_down = lax.ppermute(lower_up, "head", up), lax.ppermute(upper_down, "head", down)
    terms = [(own, 1, 0), (near, 0, 0), upper, (own, 2, 1), (near, 1, 1), lower]
    upper_up, lower_down = small_call(add_kernel, "turn", terms, [half, half])
    upper_up, lower_down = lax.ppermute(upper_up, "head", up), lax.ppermute(lower_down, "head", down)
    terms = [(own, 3, None), (near, 2, None), upper_down, lower_up]
    (total,) = small_call(halves_kernel, "collect", terms, [whole], jnp.float32)
    return small_call(halves_kernel, "finish", [total, upper_up, lower_down], [whole])[0]


def solution(mesh):
    placed = (
        P("ctx", "head"),
        P("ctx", "head"),
        P("ctx", "head"),
        P("head", "ctx"),
        P("head"),
        P("head", None),
    )
    return jax.shard_map(
        on_device, mesh=mesh, in_specs=placed, out_specs=P("ctx", "head"), check_vma=False
    )
```

```python
import functools

import jax
import jax.numpy as jnp
from jax import lax
from jax.experimental import pallas as pl
from jax.experimental.pallas import tpu as pltpu
from jax.sharding import PartitionSpec as P

HEAD = 128
WIDE = 8
INFO = 16
KEEP = 256
LOG2E = 1.4426950408889634
FACTOR = HEAD**-0.5 * LOG2E
LIMIT = 2.0**100
NEGATIVE = -1e30
NT = (((1,), (1,)), ((), ()))
VMEM = pl.BlockSpec(memory_space=pltpu.VMEM)
SMEM = pl.BlockSpec(memory_space=pltpu.SMEM)
HBM = pl.BlockSpec(memory_space=pltpu.HBM)
ANY = pl.BlockSpec(memory_space=pl.ANY)
TILE = 512
STEP = 1024
PARAMS = pltpu.CompilerParams(vmem_limit_bytes=60 * 2**20)


def dot(a, b):
    return jnp.dot(a, b, preferred_element_type=jnp.float32)


def dot_nt(a, b):
    return lax.dot_general(a, b, NT, preferred_element_type=jnp.float32)


def count_along(shape, dim):
    return lax.broadcasted_iota(jnp.int32, shape, dim)


def ones_where(condition):
    return jnp.where(condition, 1.0, 0.0).astype(jnp.bfloat16)


def select_kernel(used_ref, *refs):
    sources, (kept_rows_ref, rest_ref), targets, sems = refs[:3], refs[3:5], refs[5:8], refs[8]
    copies = [
        pltpu.make_async_copy(source, target, sems.at[at])
        for at, (source, target) in enumerate(zip(sources, targets))
    ]
    for copy in copies:
        copy.start()
    for copy in copies:
        copy.wait()
    kept_ref, key_ref, value_ref = targets
    length, keep = key_ref.shape[0], kept_ref.shape[1]
    hit = ones_where(count_along((length, keep), 0) == kept_ref[...])
    kept = dot_nt(jnp.ones((8, keep), jnp.bfloat16), hit)
    square = (length, length)
    before = ones_where(count_along(square, 0) < count_along(square, 1))
    rank = dot(kept.astype(jnp.bfloat16), before)
    column = count_along((8, length), 1)
    place = jnp.where(kept > 0.5, rank, column.astype(jnp.float32) + keep - rank)
    order = ones_where(count_along(square, 0).astype(jnp.float32) == place[:1])
    for at, ref in enumerate((key_ref, value_ref)):
        columns = slice(at * HEAD, (at + 1) * HEAD)
        rows = dot(order, ref[...]).astype(jnp.bfloat16)
        kept_rows_ref[:, columns] = rows[:keep]
        rest_ref[: length - keep, columns] = rows[keep:]
    in_both = jnp.where((kept > 0.5) & (column < used_ref[0]), 1.0, 0.0)[:1]
    number = jnp.sum(in_both, axis=1, keepdims=True)
    rest_ref[length - keep :] = jnp.broadcast_to(number, (INFO, 2 * HEAD)).astype(jnp.bfloat16)


def select(used, kept, keys, values):
    length = keys.shape[0]
    rows = (KEEP, length - KEEP + INFO)
    return pl.pallas_call(
        select_kernel,
        out_shape=[jax.ShapeDtypeStruct((n, 2 * HEAD), jnp.bfloat16) for n in rows],
        in_specs=[SMEM, HBM, HBM, HBM],
        out_specs=[VMEM] * 2,
        scratch_shapes=[
            *[pltpu.VMEM(x.shape, x.dtype) for x in (kept, keys, values)],
            pltpu.SemaphoreType.DMA((3,)),
        ],
        compiler_params=PARAMS,
        name="select_kept",
    )(used, kept, keys, values)


def wide(column, width):
    return jnp.concatenate([column] * (width // HEAD), axis=1)


def widened(values):
    return jnp.concatenate([values, jnp.ones_like(values)], axis=1)


def scores(query, keys):
    return dot_nt(query, keys) * FACTOR


def local(query, keys, values, acc_ref, peak_ref):
    length = query.shape[0]
    causal = count_along((length, length), 1) <= count_along((length, length), 0)
    raw = jnp.where(causal, scores(query, keys), NEGATIVE)
    peak = jnp.broadcast_to(jnp.max(raw, axis=1, keepdims=True), (length, HEAD))
    peak_ref[...] = peak
    weights = jnp.exp2(raw - wide(peak, length)).astype(jnp.bfloat16)
    acc_ref[...] = dot(weights, widened(values))


def biased(raw, bias):
    if bias is None:
        return raw
    return (raw.reshape(-1, *bias.shape) + bias).reshape(raw.shape)


def fixed(heads, view, keys, values, bias):
    raw = scores(view(0)[0], keys)
    for h in range(heads):
        _, acc_ref, peak_ref = view(h)
        ahead = scores(view(h + 1)[0], keys) if h + 1 < heads else None
        weights = jnp.exp2(biased(raw, bias) - wide(peak_ref[...], keys.shape[0]))
        acc_ref[...] += dot(weights.astype(jnp.bfloat16), values)
        raw = ahead


def moving(query, acc_ref, peak_ref, keys, values, bias):
    raw = biased(scores(query, keys), bias)
    old = peak_ref[...]
    peak = jnp.maximum(old, jnp.max(raw, axis=1, keepdims=True))
    weights = jnp.exp2(raw - wide(peak, keys.shape[0])).astype(jnp.bfloat16)
    peak_ref[...] = peak
    acc_ref[...] = acc_ref[...] * wide(jnp.exp2(old - peak), 2 * HEAD) + dot(weights, values)


def absorb(heads, view, masked, steps, read):
    if masked is not None:

        @pl.loop(0, masked)
        def _(step):
            fixed(heads, view, *read(step, True))

    @pl.loop(0, steps)
    def _(step):
        fixed(heads, view, *read(step, False))


def absorb_again(acc_ref, view, start, tiles, read):
    largest = jnp.max(acc_ref[:, :, HEAD:])

    @pl.when(jnp.logical_not(largest < LIMIT))
    def _():
        @pl.loop(0, acc_ref.shape[0])
        def _(h):
            start(h)

            @pl.loop(0, tiles)
            def _(tile):
                moving(*view(h), *read(tile))


def tile_of(ref, start, size):
    rows = pl.ds(pl.multiple_of(start, TILE), size)
    return ref[rows, :HEAD], widened(ref[rows, HEAD:])


def head_view(q_ref, acc_ref, peak_ref):
    def view(h):
        columns = pl.ds(pl.multiple_of(h * HEAD, HEAD), HEAD)
        return q_ref[:, columns], acc_ref.at[h], peak_ref.at[h]

    return view


def bias_where(allowed):
    return jnp.where(allowed, 0.0, NEGATIVE)


def sums(state_ref):
    return state_ref.at[:, :, pl.ds(0, 2 * HEAD)], state_ref.at[:, :, pl.ds(2 * HEAD, HEAD)]


def own_row_kernel(
    place_ref, q_ref, k_ref, v_ref, row_a, row_b, below_a, above_b, state_ref, bank_ref, bias_ref,
    sems,
):
    y, z = place_ref[0] // WIDE, place_ref[0] % WIDE
    acc_ref, peak_ref = sums(state_ref)
    keys, half = z * KEEP, row_a.shape[0]
    row_steps = keys // STEP
    masked = (keys - row_steps * STEP + TILE - 1) // TILE
    copies = [
        (row_a, bank_ref.at[pl.ds(0, half)], z >= 0),
        (row_b, bank_ref.at[pl.ds(half, half)], z >= 0),
        (below_a, bank_ref.at[pl.ds(2 * half, half)], y > 0),
        (above_b, bank_ref.at[pl.ds(3 * half, half)], y == 3),
    ]
    copies = [
        (pltpu.make_async_copy(source, target, sems.at[at]), on)
        for at, (source, target, on) in enumerate(copies)
    ]
    for one, on in copies:
        pl.when(on)(one.start)
    view, heads = head_view(q_ref, acc_ref, peak_ref), acc_ref.shape[0]

    def start(h):
        query, acc, peak = view(h)
        local(query, k_ref[...], v_ref[...], acc, peak)

    def read_masked(tile):
        at = row_steps * STEP + tile * TILE
        bias_ref[...] = bias_where(count_along(bias_ref.shape, 1) + at < keys)
        return *tile_of(bank_ref, at, TILE), bias_ref[...]

    def step_start(step):
        return jnp.where(step < row_steps, step, step - row_steps + 2 * half // STEP) * STEP

    def read_fast(step, with_bias):
        if with_bias:
            return read_masked(step)
        for at, (one, on) in enumerate(copies[2:]):
            pl.when(on & (step == row_steps + at))(one.wait)
        return *tile_of(bank_ref, step_start(step), STEP), None

    def read(tile):
        after = jnp.maximum(tile - masked, 0)
        plain = step_start(after // 2) + after % 2 * TILE
        at = jnp.where(tile < masked, row_steps * STEP + tile * TILE, plain)
        limit = jnp.where(tile < masked, keys, bank_ref.shape[0])
        bias_ref[...] = bias_where(count_along(bias_ref.shape, 1) + at < limit)
        return *tile_of(bank_ref, at, TILE), bias_ref[...]

    for h in range(heads):
        start(h)
    for one, on in copies[:2]:
        pl.when(on)(one.wait)
    steps = row_steps + jnp.where(y == 3, 2, jnp.minimum(y, 1))
    absorb(heads, view, masked, steps, read_fast)
    absorb_again(acc_ref, view, start, masked + STEP // TILE * steps, read)


def more_keys(queries, rest_ref, state_in, refs, used, firsts, pieces, steps, then):
    acc_ref, peak_ref, q_ref, bank_ref, carried_ref, bias_ref, sems = refs
    acc_in, peak_in = sums(state_in)
    copies = [(queries, q_ref, True), (peak_in, peak_ref, True)]
    copies += [(ref.at[pl.ds(0, KEEP)], bank_ref.at[pl.ds(0, KEEP)], on) for ref, on in firsts]
    for at, (ref, on) in enumerate(pieces):
        copies.append((ref, bank_ref.at[pl.ds(TILE + at * STEP, STEP)], on))
    copies.append((acc_in, carried_ref, True))
    copies = [
        (pltpu.make_async_copy(source, target, sems.at[at]), on)
        for at, (source, target, on) in enumerate(copies)
    ]

    def under(condition, act):
        if condition is True:
            act()
        else:
            pl.when(condition)(act)

    for one, on in copies:
        under(on, one.start)
    then()
    acc_ref[...] = jnp.zeros(acc_ref.shape, jnp.float32)
    view, masked = head_view(q_ref, acc_ref, peak_ref), None
    if firsts:
        bank_ref[KEEP:TILE] = rest_ref[: TILE - KEEP]
        number = wide(rest_ref[TILE - KEEP : TILE - KEEP + 1, :HEAD].astype(jnp.int32), TILE)
        at = count_along((1, TILE), 1)
        limit = jnp.where(at < KEEP, number, KEEP + used - number)
        bias_ref[0] = jnp.broadcast_to(bias_where(at < limit), bias_ref.shape[1:])
        bias_ref[1] = jnp.zeros(bias_ref.shape[1:], jnp.float32)
        masked = sum(jnp.where(on, 1, 0) for _, on in firsts)

    def start(h):
        acc_ref[h] = carried_ref[h]

    def read(step):
        if masked is None:
            return *tile_of(bank_ref, TILE + step * TILE, TILE), None
        tile = jnp.where(masked > 0, step, step + 1)
        return *tile_of(bank_ref, tile * TILE, TILE), bias_ref[jnp.minimum(tile, 1)]

    here, later = copies[2 : 2 + len(firsts)], copies[2 + len(firsts) : -1]

    def read_fast(step, with_bias):
        if with_bias:
            for one, on in here:
                under(on, one.wait)
            return *tile_of(bank_ref, 0, TILE), bias_ref[0]
        for at, (one, on) in enumerate(later):
            pl.when(on & (step == at))(one.wait)
        return *tile_of(bank_ref, TILE + step * STEP, STEP), None

    for one, _ in copies[:2]:
        one.wait()
    absorb(acc_ref.shape[0], view, masked, steps, read_fast)
    copies[-1][0].wait()
    acc_ref[...] += carried_ref[...]
    tiles = STEP // TILE * steps + (0 if masked is None else masked)
    absorb_again(acc_ref, view, start, tiles, read)


def rest_kernel(
    place_ref, rest_ref, queries, first_ref, below_b, above_a, below2_ref, above2_ref, weight_ref, state_in,
    own_out, far_out, near_out, own_ref, send_ref, w_ref, att_ref, out_sems, *refs,
):
    mine, used = place_ref[0], place_ref[1]
    y = mine // WIDE
    pieces = (below_b, y > 0), (below2_ref, y > 1), (above2_ref, y > 1), (above_a, y == 3)
    firsts = (first_ref, (mine > 0) & (y < 2)), (below2_ref, y == 2), (above_a, y == 3)
    steps = jnp.where(y == 3, 4, jnp.where(y == 2, 3, y))
    weight_copy = pltpu.make_async_copy(weight_ref, w_ref, out_sems.at[3])
    more_keys(
        queries, rest_ref, state_in, refs, used, firsts, pieces, steps, weight_copy.start
    )
    acc_ref = refs[0]
    for h in range(acc_ref.shape[0]):
        att_ref[:, h * HEAD : (h + 1) * HEAD] = (
            acc_ref[h, :, :HEAD] / acc_ref[h, :, HEAD:]
        ).astype(jnp.bfloat16)
    weight_copy.wait()
    chips, _, columns = own_out.shape
    chip, core = place_ref[2], place_ref[3]

    @pl.loop(0, chips)
    def _(step):
        ahead = jnp.where(step == 0, 2, jnp.where(step == 1, 1, jnp.where(step == 2, 3, 0)))
        column = lax.rem(chip + ahead, chips) * 2
        for ref, side in ((own_ref, core), (send_ref, 1 - core)):
            start = pl.multiple_of((column + side) * columns, columns)
            ref[step] = dot(att_ref[...], w_ref[:, pl.ds(start, columns)]).astype(jnp.bfloat16)
        pltpu.make_async_copy(own_ref.at[step], own_out.at[step], out_sems.at[0]).start()

        @pl.when(step == 0)
        def _():
            pltpu.make_async_copy(send_ref.at[0], far_out, out_sems.at[1]).start()

        @pl.when(step > 0)
        def _():
            target = near_out.at[step - 1]
            pltpu.make_async_copy(send_ref.at[step], target, out_sems.at[2]).start()

    pltpu.make_async_copy(own_ref, own_out, out_sems.at[0]).wait()
    pltpu.make_async_copy(send_ref.at[0], far_out, out_sems.at[1]).wait()
    pltpu.make_async_copy(send_ref.at[pl.ds(1, chips - 1)], near_out, out_sems.at[2]).wait()


def pack_row_kernel(place_ref, *refs):
    z = place_ref[0] % WIDE
    at, middle = KEEP, WIDE * KEEP // 2
    for ref in refs[:-2]:
        rows = ref.shape[0]
        start = pl.multiple_of(lax.rem(z * KEEP + at, WIDE * KEEP), KEEP // 2)
        at += rows
        for out_ref, first in zip(refs[-2:], (0, middle)):

            @pl.when((start >= first) & (start < first + middle))
            def _():
                out_ref[pl.ds(pl.multiple_of(start - first, KEEP // 2), rows)] = ref[...]


def pack_row(place, pieces):
    return pl.pallas_call(
        pack_row_kernel,
        out_shape=[jax.ShapeDtypeStruct((WIDE * KEEP // 2, 2 * HEAD), jnp.bfloat16)] * 2,
        in_specs=[SMEM] + [VMEM] * len(pieces),
        out_specs=[VMEM] * 2,
        compiler_params=pltpu.CompilerParams(vmem_limit_bytes=8 * 2**20),
        name="pack_row",
    )(place, *pieces)


def cost(rows, keys):
    return pl.CostEstimate(
        flops=rows * keys * HEAD * 8, bytes_accessed=8 * 2**20, transcendentals=rows * keys
    )


def state_of(length, heads):
    return jax.ShapeDtypeStruct((heads, length, 3 * HEAD), jnp.float32)


def own_row(place, queries, keys, values, *pieces):
    length, width = queries.shape
    whole = lambda x: pl.BlockSpec(x.shape, lambda i: (0,) * len(x.shape))
    state = state_of(length, width // HEAD)
    return pl.pallas_call(
        own_row_kernel,
        grid=(1,),
        out_shape=state,
        in_specs=[SMEM, *[whole(x) for x in (queries, keys, values)], *[ANY] * len(pieces)],
        out_specs=whole(state),
        scratch_shapes=[
            pltpu.VMEM((4 * STEP, 2 * HEAD), jnp.bfloat16),
            pltpu.VMEM((8, TILE), jnp.float32),
            pltpu.SemaphoreType.DMA((4,)),
        ],
        compiler_params=PARAMS,
        cost_estimate=cost(length * width // HEAD, length + 4 * STEP),
        name="own_row",
    )(place, queries, keys, values, *pieces)


def rest_rows(place, queries, rest, banks, weight, state, chips):
    length, width = queries.shape
    heads, keys = width // HEAD, TILE + 4 * STEP
    whole = lambda x: pl.BlockSpec(x.shape, lambda i: (0,) * len(x.shape))
    one = (length, weight.shape[1] // chips // 2)
    shapes = (chips, *one), one, (chips - 1, *one)
    return pl.pallas_call(
        rest_kernel,
        grid=(1,),
        out_shape=[jax.ShapeDtypeStruct(shape, jnp.bfloat16) for shape in shapes],
        in_specs=[SMEM, whole(rest), *[ANY] * (len(banks) + 3)],
        out_specs=[ANY] * 3,
        scratch_shapes=[
            *[pltpu.VMEM((chips, *one), jnp.bfloat16)] * 2,
            pltpu.VMEM(weight.shape, weight.dtype),
            pltpu.VMEM((length, width), jnp.bfloat16),
            pltpu.SemaphoreType.DMA((4,)),
            pltpu.VMEM((heads, length, 2 * HEAD), jnp.float32),
            pltpu.VMEM((heads, length, HEAD), jnp.float32),
            pltpu.VMEM((length, width), jnp.bfloat16),
            pltpu.VMEM((keys, 2 * HEAD), jnp.bfloat16),
            pltpu.VMEM((heads, length, 2 * HEAD), jnp.float32),
            pltpu.VMEM((2, 8, TILE), jnp.float32),
            pltpu.SemaphoreType.DMA((10,)),
        ],
        compiler_params=pltpu.CompilerParams(vmem_limit_bytes=47 * 2**20),
        cost_estimate=cost(length * heads, keys),
        name="rest_rows",
    )(place, rest, queries, *banks, weight, state)


def summed(*refs):
    return sum(ref[...].astype(jnp.float32) for ref in refs)


def cross_kernel(own_ref, other_ref, upper_ref, lower_ref):
    total = summed(own_ref, other_ref).astype(jnp.bfloat16)
    half = upper_ref.shape[0]
    upper_ref[...] = total[:half]
    lower_ref[...] = total[half:]


def add_kernel(*refs):
    terms = refs[:-2]
    middle = len(terms) // 2
    refs[-2][...] = summed(*terms[:middle]).astype(jnp.bfloat16)
    refs[-1][...] = summed(*terms[middle:]).astype(jnp.bfloat16)


def halves_kernel(*refs):
    (*terms, upper_ref, lower_ref), out_ref = refs[:-1], refs[-1]
    half, total = upper_ref.shape[0], summed(*terms)
    out_ref[:half] = (total[:half] + summed(upper_ref)).astype(out_ref.dtype)
    out_ref[half:] = (total[half:] + summed(lower_ref)).astype(out_ref.dtype)


def small_call(kernel, name, terms, shapes, dtype=jnp.bfloat16):
    def spec(term):
        if not isinstance(term, tuple):
            return pl.BlockSpec(term.shape, lambda i: (0, 0))
        x, chunk, half = term
        rows = x.shape[1] // (1 if half is None else 2)
        return pl.BlockSpec((None, rows, x.shape[2]), lambda i: (chunk, half or 0, 0))

    return pl.pallas_call(
        kernel,
        grid=(1,),
        out_shape=[jax.ShapeDtypeStruct(shape, dtype) for shape in shapes],
        in_specs=[spec(term) for term in terms],
        out_specs=[pl.BlockSpec(shape, lambda i: (0, 0)) for shape in shapes],
        compiler_params=pltpu.CompilerParams(vmem_limit_bytes=8 * 2**20),
        name=name,
    )(*[term[0] if isinstance(term, tuple) else term for term in terms])


def on_device(queries, key_rows, value_rows, kept_positions, anchor_length, output_weight):
    mine, head = lax.axis_index("ctx"), lax.axis_index("head")
    length, devices, blocks = queries.shape[0], lax.axis_size("head"), lax.axis_size("ctx")
    chips, chip, core = devices // 2, head // 2, head % 2
    tall = blocks // WIDE
    swap = [(i, i ^ 1) for i in range(devices)]
    up = [(i, (i + 2) % devices) for i in range(devices)]
    down = [(i, (i - 2) % devices) for i in range(devices)]
    along = lambda step: [
        (r * WIDE + c, r * WIDE + (c + step) % WIDE) for r in range(tall) for c in range(WIDE)
    ]
    across = lambda hops: [(a * WIDE + c, b * WIDE + c) for a, b in hops for c in range(WIDE)]
    permute = lambda x, pairs: lax.ppermute(x, "ctx", pairs)

    spots = jnp.stack([chip, core]).astype(jnp.int32)
    place = jnp.concatenate([mine.astype(jnp.int32)[None], anchor_length, spots])
    kept, rest = select(anchor_length, kept_positions, key_rows, value_rows)

    plus, minus = along(1), along(-1)
    half = KEEP // 2
    left, right = [kept], [kept]
    rest = jnp.where(mine == 0, rest, jnp.zeros_like(rest))
    spread = lambda hops: [(r * WIDE + a, r * WIDE + b) for a, b in hops for r in range(tall)]
    upward = [(0, WIDE)], [(0, 3 * WIDE), (WIDE, 2 * WIDE)]
    for step in range(WIDE // 2 - 1):
        left.append(permute(left[-1], plus))
        right.append(permute(right[-1], minus))
        if step < len(upward):
            rest = rest + permute(rest, upward[step])
    opposite = [permute(left[-1][:half], plus), permute(right[-1][half:], minus)]
    ends = pack_row(place, right[1:] + opposite + left[:0:-1] + [kept])

    below_a = permute(ends[0], across([(0, 1), (1, 2), (2, 3)]))
    above_b = permute(ends[1], across([(0, 3), (1, 0)]))
    rest, ends = lax.optimization_barrier((rest, ends))
    rest = rest + permute(rest, spread([(0, 4)]))
    rest = rest + permute(rest, spread([(0, 2), (4, 6)]))
    rest = rest + permute(rest, spread([(0, 1), (2, 3), (4, 5), (6, 7)]))
    first = jnp.where(mine // WIDE == 1, below_a[:KEEP], ends[0][:KEEP])
    rest, first, below_a, above_b, ends = lax.optimization_barrier(
        (rest, first, below_a, above_b, ends)
    )
    below_b = permute(ends[1], across([(0, 1), (1, 2), (2, 3)]))
    above_a = permute(ends[0], across([(0, 3)]))
    below2 = permute(below_a, across([(1, 2), (2, 3)]))
    above2 = permute(above_b, across([(0, 3), (3, 2)]))
    state = own_row(place, queries, key_rows, value_rows, *ends, below_a, above_b)
    banks = (first, below_b, above_a, below2, above2)
    own, far, near = rest_rows(place, queries, rest, banks, output_weight, state, chips)

    far, near = lax.optimization_barrier((lax.ppermute(far, "head", swap), near))
    near = lax.ppermute(near, "head", swap)
    columns = own.shape[2]
    whole, half = (length, columns), (length // 2, columns)
    upper, lower = small_call(cross_kernel, "cross", [(own, 0, None), far], [half, half])
    upper, lower = lax.ppermute(upper, "head", up), lax.ppermute(lower, "head", down)
    terms = [(own, 1, 1), (near, 0, 1), (own, 2, 0), (near, 1, 0)]
    lower_up, upper_down = small_call(add_kernel, "direct", terms, [half, half])
    upper, lower, _, _ = lax.optimization_barrier((upper, lower, lower_up, upper_down))
    lower_up, upper_down = lax.ppermute(lower_up, "head", up), lax.ppermute(upper_down, "head", down)
    terms = [(own, 1, 0), (near, 0, 0), upper, (own, 2, 1), (near, 1, 1), lower]
    upper_up, lower_down = small_call(add_kernel, "turn", terms, [half, half])
    upper_up, lower_down = lax.ppermute(upper_up, "head", up), lax.ppermute(lower_down, "head", down)
    terms = [(own, 3, None), (near, 2, None), upper_down, lower_up]
    (total,) = small_call(halves_kernel, "collect", terms, [whole], jnp.float32)
    return small_call(halves_kernel, "finish", [total, upper_up, lower_down], [whole])[0]


def solution(mesh):
    placed = (
        P("ctx", "head"),
        P("ctx", "head"),
        P("ctx", "head"),
        P("head", "ctx"),
        P("head"),
        P("head", None),
    )
    return jax.shard_map(
        on_device, mesh=mesh, in_specs=placed, out_specs=P("ctx", "head"), check_vma=False
    )
```

```python
import functools

import jax
import jax.numpy as jnp
from jax import lax
from jax.experimental import pallas as pl
from jax.experimental.pallas import tpu as pltpu
from jax.sharding import PartitionSpec as P

HEAD = 128
WIDE = 8
INFO = 16
KEEP = 256
LOG2E = 1.4426950408889634
FACTOR = HEAD**-0.5 * LOG2E
LIMIT = 2.0**100
NEGATIVE = -1e30
NT = (((1,), (1,)), ((), ()))
VMEM = pl.BlockSpec(memory_space=pltpu.VMEM)
SMEM = pl.BlockSpec(memory_space=pltpu.SMEM)
HBM = pl.BlockSpec(memory_space=pltpu.HBM)
ANY = pl.BlockSpec(memory_space=pl.ANY)
TILE = 512
STEP = 1024
PARAMS = pltpu.CompilerParams(vmem_limit_bytes=60 * 2**20)


def dot(a, b):
    return jnp.dot(a, b, preferred_element_type=jnp.float32)


def dot_nt(a, b):
    return lax.dot_general(a, b, NT, preferred_element_type=jnp.float32)


def count_along(shape, dim):
    return lax.broadcasted_iota(jnp.int32, shape, dim)


def ones_where(condition):
    return jnp.where(condition, 1.0, 0.0).astype(jnp.bfloat16)


def select_kernel(used_ref, *refs):
    sources, (kept_rows_ref, rest_ref), targets, sems = refs[:3], refs[3:5], refs[5:8], refs[8]
    copies = [
        pltpu.make_async_copy(source, target, sems.at[at])
        for at, (source, target) in enumerate(zip(sources, targets))
    ]
    for copy in copies:
        copy.start()
    for copy in copies:
        copy.wait()
    kept_ref, key_ref, value_ref = targets
    length, keep = key_ref.shape[0], kept_ref.shape[1]
    hit = ones_where(count_along((length, keep), 0) == kept_ref[...])
    kept = dot_nt(jnp.ones((8, keep), jnp.bfloat16), hit)
    square = (length, length)
    before = ones_where(count_along(square, 0) < count_along(square, 1))
    rank = dot(kept.astype(jnp.bfloat16), before)
    column = count_along((8, length), 1)
    place = jnp.where(kept > 0.5, rank, column.astype(jnp.float32) + keep - rank)
    order = ones_where(count_along(square, 0).astype(jnp.float32) == place[:1])
    for at, ref in enumerate((key_ref, value_ref)):
        columns = slice(at * HEAD, (at + 1) * HEAD)
        rows = dot(order, ref[...]).astype(jnp.bfloat16)
        kept_rows_ref[:, columns] = rows[:keep]
        rest_ref[: length - keep, columns] = rows[keep:]
    in_both = jnp.where((kept > 0.5) & (column < used_ref[0]), 1.0, 0.0)[:1]
    number = jnp.sum(in_both, axis=1, keepdims=True)
    rest_ref[length - keep :] = jnp.broadcast_to(number, (INFO, 2 * HEAD)).astype(jnp.bfloat16)


def select(used, kept, keys, values):
    length = keys.shape[0]
    rows = (KEEP, length - KEEP + INFO)
    return pl.pallas_call(
        select_kernel,
        out_shape=[jax.ShapeDtypeStruct((n, 2 * HEAD), jnp.bfloat16) for n in rows],
        in_specs=[SMEM, HBM, HBM, HBM],
        out_specs=[VMEM] * 2,
        scratch_shapes=[
            *[pltpu.VMEM(x.shape, x.dtype) for x in (kept, keys, values)],
            pltpu.SemaphoreType.DMA((3,)),
        ],
        compiler_params=PARAMS,
        name="select_kept",
    )(used, kept, keys, values)


def wide(column, width):
    return jnp.concatenate([column] * (width // HEAD), axis=1)


def widened(values):
    return jnp.concatenate([values, jnp.ones_like(values)], axis=1)


def scores(query, keys):
    return dot_nt(query, keys) * FACTOR


def local(query, keys, values, acc_ref, peak_ref):
    length = query.shape[0]
    causal = count_along((length, length), 1) <= count_along((length, length), 0)
    raw = jnp.where(causal, scores(query, keys), NEGATIVE)
    peak = jnp.broadcast_to(jnp.max(raw, axis=1, keepdims=True), (length, HEAD))
    peak_ref[...] = peak
    weights = jnp.exp2(raw - wide(peak, length)).astype(jnp.bfloat16)
    acc_ref[...] = dot(weights, widened(values))


def biased(raw, bias):
    if bias is None:
        return raw
    return (raw.reshape(-1, *bias.shape) + bias).reshape(raw.shape)


def fixed(heads, view, keys, values, bias):
    raw = scores(view(0)[0], keys)
    for h in range(heads):
        _, acc_ref, peak_ref = view(h)
        ahead = scores(view(h + 1)[0], keys) if h + 1 < heads else None
        weights = jnp.exp2(biased(raw, bias) - wide(peak_ref[...], keys.shape[0]))
        acc_ref[...] += dot(weights.astype(jnp.bfloat16), values)
        raw = ahead


def moving(query, acc_ref, peak_ref, keys, values, bias):
    raw = biased(scores(query, keys), bias)
    old = peak_ref[...]
    peak = jnp.maximum(old, jnp.max(raw, axis=1, keepdims=True))
    weights = jnp.exp2(raw - wide(peak, keys.shape[0])).astype(jnp.bfloat16)
    peak_ref[...] = peak
    acc_ref[...] = acc_ref[...] * wide(jnp.exp2(old - peak), 2 * HEAD) + dot(weights, values)


def absorb(heads, view, masked, steps, read):
    if masked is not None:

        @pl.loop(0, masked)
        def _(step):
            fixed(heads, view, *read(step, True))

    @pl.loop(0, steps)
    def _(step):
        fixed(heads, view, *read(step, False))


def absorb_again(acc_ref, view, start, tiles, read):
    largest = jnp.max(acc_ref[:, :, HEAD:])

    @pl.when(jnp.logical_not(largest < LIMIT))
    def _():
        @pl.loop(0, acc_ref.shape[0])
        def _(h):
            start(h)

            @pl.loop(0, tiles)
            def _(tile):
                moving(*view(h), *read(tile))


def tile_of(ref, start, size):
    rows = pl.ds(pl.multiple_of(start, TILE), size)
    return ref[rows, :HEAD], widened(ref[rows, HEAD:])


def head_view(q_ref, acc_ref, peak_ref):
    def view(h):
        columns = pl.ds(pl.multiple_of(h * HEAD, HEAD), HEAD)
        return q_ref[:, columns], acc_ref.at[h], peak_ref.at[h]

    return view


def bias_where(allowed):
    return jnp.where(allowed, 0.0, NEGATIVE)


def sums(state_ref):
    return state_ref.at[:, :, pl.ds(0, 2 * HEAD)], state_ref.at[:, :, pl.ds(2 * HEAD, HEAD)]


def own_row_kernel(
    place_ref, q_ref, k_ref, v_ref, row_a, row_b, below_a, above_b, state_ref, bank_ref, bias_ref,
    sems,
):
    y, z = place_ref[0] // WIDE, place_ref[0] % WIDE
    acc_ref, peak_ref = sums(state_ref)
    keys, half = z * KEEP, row_a.shape[0]
    row_steps = keys // STEP
    masked = (keys - row_steps * STEP + TILE - 1) // TILE
    copies = [
        (row_a, bank_ref.at[pl.ds(0, half)], z >= 0),
        (row_b, bank_ref.at[pl.ds(half, half)], z >= 0),
        (below_a, bank_ref.at[pl.ds(2 * half, half)], y > 0),
        (above_b, bank_ref.at[pl.ds(3 * half, half)], y == 3),
    ]
    copies = [
        (pltpu.make_async_copy(source, target, sems.at[at]), on)
        for at, (source, target, on) in enumerate(copies)
    ]
    for one, on in copies:
        pl.when(on)(one.start)
    view, heads = head_view(q_ref, acc_ref, peak_ref), acc_ref.shape[0]

    def start(h):
        query, acc, peak = view(h)
        local(query, k_ref[...], v_ref[...], acc, peak)

    def read_masked(tile):
        at = row_steps * STEP + tile * TILE
        bias_ref[...] = bias_where(count_along(bias_ref.shape, 1) + at < keys)
        return *tile_of(bank_ref, at, TILE), bias_ref[...]

    def step_start(step):
        return jnp.where(step < row_steps, step, step - row_steps + 2 * half // STEP) * STEP

    def read_fast(step, with_bias):
        if with_bias:
            return read_masked(step)
        for at, (one, on) in enumerate(copies[2:]):
            pl.when(on & (step == row_steps + at))(one.wait)
        return *tile_of(bank_ref, step_start(step), STEP), None

    def read(tile):
        after = jnp.maximum(tile - masked, 0)
        plain = step_start(after // 2) + after % 2 * TILE
        at = jnp.where(tile < masked, row_steps * STEP + tile * TILE, plain)
        limit = jnp.where(tile < masked, keys, bank_ref.shape[0])
        bias_ref[...] = bias_where(count_along(bias_ref.shape, 1) + at < limit)
        return *tile_of(bank_ref, at, TILE), bias_ref[...]

    for h in range(heads):
        start(h)
    for one, on in copies[:2]:
        pl.when(on)(one.wait)
    steps = row_steps + jnp.where(y == 3, 2, jnp.minimum(y, 1))
    absorb(heads, view, masked, steps, read_fast)
    absorb_again(acc_ref, view, start, masked + STEP // TILE * steps, read)


def more_keys(queries, rest_ref, state_in, refs, used, firsts, pieces, steps, then):
    acc_ref, peak_ref, q_ref, bank_ref, carried_ref, bias_ref, sems = refs
    acc_in, peak_in = sums(state_in)
    copies = [(queries, q_ref, True), (peak_in, peak_ref, True)]
    copies += [(ref.at[pl.ds(0, KEEP)], bank_ref.at[pl.ds(0, KEEP)], on) for ref, on in firsts]
    for at, (ref, on) in enumerate(pieces):
        copies.append((ref, bank_ref.at[pl.ds(TILE + at * STEP, STEP)], on))
    copies.append((acc_in, carried_ref, True))
    copies = [
        (pltpu.make_async_copy(source, target, sems.at[at]), on)
        for at, (source, target, on) in enumerate(copies)
    ]

    def under(condition, act):
        if condition is True:
            act()
        else:
            pl.when(condition)(act)

    for one, on in copies:
        under(on, one.start)
    then()
    acc_ref[...] = jnp.zeros(acc_ref.shape, jnp.float32)
    view, masked = head_view(q_ref, acc_ref, peak_ref), None
    if firsts:
        bank_ref[KEEP:TILE] = rest_ref[: TILE - KEEP]
        number = wide(rest_ref[TILE - KEEP : TILE - KEEP + 1, :HEAD].astype(jnp.int32), TILE)
        at = count_along((1, TILE), 1)
        limit = jnp.where(at < KEEP, number, KEEP + used - number)
        bias_ref[0] = jnp.broadcast_to(bias_where(at < limit), bias_ref.shape[1:])
        bias_ref[1] = jnp.zeros(bias_ref.shape[1:], jnp.float32)
        masked = sum(jnp.where(on, 1, 0) for _, on in firsts)

    def start(h):
        acc_ref[h] = carried_ref[h]

    def read(step):
        if masked is None:
            return *tile_of(bank_ref, TILE + step * TILE, TILE), None
        tile = jnp.where(masked > 0, step, step + 1)
        return *tile_of(bank_ref, tile * TILE, TILE), bias_ref[jnp.minimum(tile, 1)]

    here, later = copies[2 : 2 + len(firsts)], copies[2 + len(firsts) : -1]

    def read_fast(step, with_bias):
        if with_bias:
            for one, on in here:
                under(on, one.wait)
            return *tile_of(bank_ref, 0, TILE), bias_ref[0]
        for at, (one, on) in enumerate(later):
            pl.when(on & (step == at))(one.wait)
        return *tile_of(bank_ref, TILE + step * STEP, STEP), None

    for one, _ in copies[:2]:
        one.wait()
    absorb(acc_ref.shape[0], view, masked, steps, read_fast)
    copies[-1][0].wait()
    acc_ref[...] += carried_ref[...]
    tiles = STEP // TILE * steps + (0 if masked is None else masked)
    absorb_again(acc_ref, view, start, tiles, read)


def rest_kernel(
    place_ref, rest_ref, queries, first_ref, below_b, above_a, below2_ref, above2_ref, weight_ref, state_in,
    own_out, far_out, near_out, own_ref, send_ref, w_ref, att_ref, out_sems, *refs,
):
    mine, used = place_ref[0], place_ref[1]
    y = mine // WIDE
    pieces = (below_b, y > 0), (below2_ref, y > 1), (above2_ref, y > 1), (above_a, y == 3)
    firsts = (first_ref, (mine > 0) & (y < 2)), (below2_ref, y == 2), (above_a, y == 3)
    steps = jnp.where(y == 3, 4, jnp.where(y == 2, 3, y))
    weight_copy = pltpu.make_async_copy(weight_ref, w_ref, out_sems.at[3])
    more_keys(
        queries, rest_ref, state_in, refs, used, firsts, pieces, steps, weight_copy.start
    )
    acc_ref = refs[0]
    for h in range(acc_ref.shape[0]):
        att_ref[:, h * HEAD : (h + 1) * HEAD] = (
            acc_ref[h, :, :HEAD] / acc_ref[h, :, HEAD:]
        ).astype(jnp.bfloat16)
    weight_copy.wait()
    chips, _, columns = own_out.shape
    chip, core = place_ref[2], place_ref[3]

    @pl.loop(0, chips)
    def _(step):
        ahead = jnp.where(step == 0, 2, jnp.where(step == 1, 1, jnp.where(step == 2, 3, 0)))
        column = lax.rem(chip + ahead, chips) * 2
        for ref, side in ((own_ref, core), (send_ref, 1 - core)):
            start = pl.multiple_of((column + side) * columns, columns)
            ref[step] = dot(att_ref[...], w_ref[:, pl.ds(start, columns)]).astype(jnp.bfloat16)
        pltpu.make_async_copy(own_ref.at[step], own_out.at[step], out_sems.at[0]).start()

        @pl.when(step == 0)
        def _():
            pltpu.make_async_copy(send_ref.at[0], far_out, out_sems.at[1]).start()

        @pl.when(step > 0)
        def _():
            target = near_out.at[step - 1]
            pltpu.make_async_copy(send_ref.at[step], target, out_sems.at[2]).start()

    pltpu.make_async_copy(own_ref, own_out, out_sems.at[0]).wait()
    pltpu.make_async_copy(send_ref.at[0], far_out, out_sems.at[1]).wait()
    pltpu.make_async_copy(send_ref.at[pl.ds(1, chips - 1)], near_out, out_sems.at[2]).wait()


def pack_row_kernel(place_ref, *refs):
    z = place_ref[0] % WIDE
    at, middle = KEEP, WIDE * KEEP // 2
    for ref in refs[:-2]:
        rows = ref.shape[0]
        start = pl.multiple_of(lax.rem(z * KEEP + at, WIDE * KEEP), KEEP // 2)
        at += rows
        for out_ref, first in zip(refs[-2:], (0, middle)):

            @pl.when((start >= first) & (start < first + middle))
            def _():
                out_ref[pl.ds(pl.multiple_of(start - first, KEEP // 2), rows)] = ref[...]


def pack_row(place, pieces):
    return pl.pallas_call(
        pack_row_kernel,
        out_shape=[jax.ShapeDtypeStruct((WIDE * KEEP // 2, 2 * HEAD), jnp.bfloat16)] * 2,
        in_specs=[SMEM] + [VMEM] * len(pieces),
        out_specs=[VMEM] * 2,
        compiler_params=pltpu.CompilerParams(vmem_limit_bytes=8 * 2**20),
        name="pack_row",
    )(place, *pieces)


def cost(rows, keys):
    return pl.CostEstimate(
        flops=rows * keys * HEAD * 8, bytes_accessed=8 * 2**20, transcendentals=rows * keys
    )


def state_of(length, heads):
    return jax.ShapeDtypeStruct((heads, length, 3 * HEAD), jnp.float32)


def own_row(place, queries, keys, values, *pieces):
    length, width = queries.shape
    whole = lambda x: pl.BlockSpec(x.shape, lambda i: (0,) * len(x.shape))
    state = state_of(length, width // HEAD)
    return pl.pallas_call(
        own_row_kernel,
        grid=(1,),
        out_shape=state,
        in_specs=[SMEM, *[whole(x) for x in (queries, keys, values)], *[ANY] * len(pieces)],
        out_specs=whole(state),
        scratch_shapes=[
            pltpu.VMEM((4 * STEP, 2 * HEAD), jnp.bfloat16),
            pltpu.VMEM((8, TILE), jnp.float32),
            pltpu.SemaphoreType.DMA((4,)),
        ],
        compiler_params=PARAMS,
        cost_estimate=cost(length * width // HEAD, length + 4 * STEP),
        name="own_row",
    )(place, queries, keys, values, *pieces)


def rest_rows(place, queries, rest, banks, weight, state, chips):
    length, width = queries.shape
    heads, keys = width // HEAD, TILE + 4 * STEP
    whole = lambda x: pl.BlockSpec(x.shape, lambda i: (0,) * len(x.shape))
    one = (length, weight.shape[1] // chips // 2)
    shapes = (chips, *one), one, (chips - 1, *one)
    return pl.pallas_call(
        rest_kernel,
        grid=(1,),
        out_shape=[jax.ShapeDtypeStruct(shape, jnp.bfloat16) for shape in shapes],
        in_specs=[SMEM, whole(rest), *[ANY] * (len(banks) + 3)],
        out_specs=[ANY] * 3,
        scratch_shapes=[
            *[pltpu.VMEM((chips, *one), jnp.bfloat16)] * 2,
            pltpu.VMEM(weight.shape, weight.dtype),
            pltpu.VMEM((length, width), jnp.bfloat16),
            pltpu.SemaphoreType.DMA((4,)),
            pltpu.VMEM((heads, length, 2 * HEAD), jnp.float32),
            pltpu.VMEM((heads, length, HEAD), jnp.float32),
            pltpu.VMEM((length, width), jnp.bfloat16),
            pltpu.VMEM((keys, 2 * HEAD), jnp.bfloat16),
            pltpu.VMEM((heads, length, 2 * HEAD), jnp.float32),
            pltpu.VMEM((2, 8, TILE), jnp.float32),
            pltpu.SemaphoreType.DMA((10,)),
        ],
        compiler_params=pltpu.CompilerParams(vmem_limit_bytes=47 * 2**20),
        cost_estimate=cost(length * heads, keys),
        name="rest_rows",
    )(place, rest, queries, *banks, weight, state)


def summed(*refs):
    return sum(ref[...].astype(jnp.float32) for ref in refs)


def cross_kernel(own_ref, other_ref, upper_ref, lower_ref):
    total = summed(own_ref, other_ref).astype(jnp.bfloat16)
    half = upper_ref.shape[0]
    upper_ref[...] = total[:half]
    lower_ref[...] = total[half:]


def add_kernel(*refs):
    terms = refs[:-2]
    middle = len(terms) // 2
    refs[-2][...] = summed(*terms[:middle]).astype(jnp.bfloat16)
    refs[-1][...] = summed(*terms[middle:]).astype(jnp.bfloat16)


def halves_kernel(*refs):
    (*terms, upper_ref, lower_ref), out_ref = refs[:-1], refs[-1]
    half, total = upper_ref.shape[0], summed(*terms)
    out_ref[:half] = (total[:half] + summed(upper_ref)).astype(out_ref.dtype)
    out_ref[half:] = (total[half:] + summed(lower_ref)).astype(out_ref.dtype)


def small_call(kernel, name, terms, shapes, dtype=jnp.bfloat16):
    def spec(term):
        if not isinstance(term, tuple):
            return pl.BlockSpec(term.shape, lambda i: (0, 0))
        x, chunk, half = term
        rows = x.shape[1] // (1 if half is None else 2)
        return pl.BlockSpec((None, rows, x.shape[2]), lambda i: (chunk, half or 0, 0))

    return pl.pallas_call(
        kernel,
        grid=(1,),
        out_shape=[jax.ShapeDtypeStruct(shape, dtype) for shape in shapes],
        in_specs=[spec(term) for term in terms],
        out_specs=[pl.BlockSpec(shape, lambda i: (0, 0)) for shape in shapes],
        compiler_params=pltpu.CompilerParams(vmem_limit_bytes=8 * 2**20),
        name=name,
    )(*[term[0] if isinstance(term, tuple) else term for term in terms])


def on_device(queries, key_rows, value_rows, kept_positions, anchor_length, output_weight):
    mine, head = lax.axis_index("ctx"), lax.axis_index("head")
    length, devices, blocks = queries.shape[0], lax.axis_size("head"), lax.axis_size("ctx")
    chips, chip, core = devices // 2, head // 2, head % 2
    tall = blocks // WIDE
    swap = [(i, i ^ 1) for i in range(devices)]
    up = [(i, (i + 2) % devices) for i in range(devices)]
    down = [(i, (i - 2) % devices) for i in range(devices)]
    along = lambda step: [
        (r * WIDE + c, r * WIDE + (c + step) % WIDE) for r in range(tall) for c in range(WIDE)
    ]
    across = lambda hops: [(a * WIDE + c, b * WIDE + c) for a, b in hops for c in range(WIDE)]
    permute = lambda x, pairs: lax.ppermute(x, "ctx", pairs)

    spots = jnp.stack([chip, core]).astype(jnp.int32)
    place = jnp.concatenate([mine.astype(jnp.int32)[None], anchor_length, spots])
    kept, rest = select(anchor_length, kept_positions, key_rows, value_rows)

    plus, minus = along(1), along(-1)
    half = KEEP // 2
    left, right = [kept], [kept]
    rest = jnp.where(mine == 0, rest, jnp.zeros_like(rest))
    spread = lambda hops: [(r * WIDE + a, r * WIDE + b) for a, b in hops for r in range(tall)]
    upward = [(0, WIDE)], [(0, 3 * WIDE), (WIDE, 2 * WIDE)]
    for step in range(WIDE // 2 - 1):
        left.append(permute(left[-1], plus))
        right.append(permute(right[-1], minus))
        if step < len(upward):
            rest = rest + permute(rest, upward[step])
        else:
            left[-1], right[-1], rest = lax.optimization_barrier((left[-1], right[-1], rest))
    opposite = [permute(left[-1][:half], plus), permute(right[-1][half:], minus)]
    ends = pack_row(place, right[1:] + opposite + left[:0:-1] + [kept])

    below_a = permute(ends[0], across([(0, 1), (1, 2), (2, 3)]))
    above_b = permute(ends[1], across([(0, 3), (1, 0)]))
    rest, ends = lax.optimization_barrier((rest, ends))
    rest = rest + permute(rest, spread([(0, 2)]))
    rest = rest + permute(rest, spread([(0, 6), (2, 4)]))
    rest, below_a, above_b, ends = lax.optimization_barrier((rest, below_a, above_b, ends))
    below_b = permute(ends[1], across([(0, 1), (1, 2), (2, 3)]))
    above_a = permute(ends[0], across([(0, 3)]))
    below2 = permute(below_a, across([(1, 2), (2, 3)]))
    above2 = permute(above_b, across([(0, 3), (3, 2)]))
    rest = rest + permute(rest, spread([(0, 1), (2, 3), (4, 5), (6, 7)]))
    state = own_row(place, queries, key_rows, value_rows, *ends, below_a, above_b)
    first = jnp.where(mine // WIDE == 1, below_a[:KEEP], ends[0][:KEEP])
    banks = (first, below_b, above_a, below2, above2)
    own, far, near = rest_rows(place, queries, rest, banks, output_weight, state, chips)

    far, near = lax.optimization_barrier((lax.ppermute(far, "head", swap), near))
    near = lax.ppermute(near, "head", swap)
    columns = own.shape[2]
    whole, half = (length, columns), (length // 2, columns)
    upper, lower = small_call(cross_kernel, "cross", [(own, 0, None), far], [half, half])
    upper, lower = lax.ppermute(upper, "head", up), lax.ppermute(lower, "head", down)
    terms = [(own, 1, 1), (near, 0, 1), (own, 2, 0), (near, 1, 0)]
    lower_up, upper_down = small_call(add_kernel, "direct", terms, [half, half])
    upper, lower, _, _ = lax.optimization_barrier((upper, lower, lower_up, upper_down))
    lower_up, upper_down = lax.ppermute(lower_up, "head", up), lax.ppermute(upper_down, "head", down)
    terms = [(own, 1, 0), (near, 0, 0), upper, (own, 2, 1), (near, 1, 1), lower]
    upper_up, lower_down = small_call(add_kernel, "turn", terms, [half, half])
    upper_up, lower_down = lax.ppermute(upper_up, "head", up), lax.ppermute(lower_down, "head", down)
    terms = [(own, 3, None), (near, 2, None), upper_down, lower_up]
    (total,) = small_call(halves_kernel, "collect", terms, [whole], jnp.float32)
    return small_call(halves_kernel, "finish", [total, upper_up, lower_down], [whole])[0]


def solution(mesh):
    placed = (
        P("ctx", "head"),
        P("ctx", "head"),
        P("ctx", "head"),
        P("head", "ctx"),
        P("head"),
        P("head", None),
    )
    return jax.shard_map(
        on_device, mesh=mesh, in_specs=placed, out_specs=P("ctx", "head"), check_vma=False
    )
```

```python
import functools

import jax
import jax.numpy as jnp
from jax import lax
from jax.experimental import pallas as pl
from jax.experimental.pallas import tpu as pltpu
from jax.sharding import PartitionSpec as P

HEAD = 128
WIDE = 8
INFO = 16
KEEP = 256
LOG2E = 1.4426950408889634
FACTOR = HEAD**-0.5 * LOG2E
LIMIT = 2.0**100
NEGATIVE = -1e30
NT = (((1,), (1,)), ((), ()))
VMEM = pl.BlockSpec(memory_space=pltpu.VMEM)
SMEM = pl.BlockSpec(memory_space=pltpu.SMEM)
HBM = pl.BlockSpec(memory_space=pltpu.HBM)
ANY = pl.BlockSpec(memory_space=pl.ANY)
TILE = 512
STEP = 1024
PARAMS = pltpu.CompilerParams(vmem_limit_bytes=60 * 2**20)


def dot(a, b):
    return jnp.dot(a, b, preferred_element_type=jnp.float32)


def dot_nt(a, b):
    return lax.dot_general(a, b, NT, preferred_element_type=jnp.float32)


def count_along(shape, dim):
    return lax.broadcasted_iota(jnp.int32, shape, dim)


def ones_where(condition):
    return jnp.where(condition, 1.0, 0.0).astype(jnp.bfloat16)


def select_kernel(used_ref, *refs):
    sources, (kept_rows_ref, rest_ref), targets, sems = refs[:3], refs[3:5], refs[5:8], refs[8]
    copies = [
        pltpu.make_async_copy(source, target, sems.at[at])
        for at, (source, target) in enumerate(zip(sources, targets))
    ]
    for copy in copies:
        copy.start()
    for copy in copies:
        copy.wait()
    kept_ref, key_ref, value_ref = targets
    length, keep = key_ref.shape[0], kept_ref.shape[1]
    hit = ones_where(count_along((length, keep), 0) == kept_ref[...])
    kept = dot_nt(jnp.ones((8, keep), jnp.bfloat16), hit)
    square = (length, length)
    before = ones_where(count_along(square, 0) < count_along(square, 1))
    rank = dot(kept.astype(jnp.bfloat16), before)
    column = count_along((8, length), 1)
    place = jnp.where(kept > 0.5, rank, column.astype(jnp.float32) + keep - rank)
    order = ones_where(count_along(square, 0).astype(jnp.float32) == place[:1])
    for at, ref in enumerate((key_ref, value_ref)):
        columns = slice(at * HEAD, (at + 1) * HEAD)
        rows = dot(order, ref[...]).astype(jnp.bfloat16)
        kept_rows_ref[:, columns] = rows[:keep]
        rest_ref[: length - keep, columns] = rows[keep:]
    in_both = jnp.where((kept > 0.5) & (column < used_ref[0]), 1.0, 0.0)[:1]
    number = jnp.sum(in_both, axis=1, keepdims=True)
    rest_ref[length - keep :] = jnp.broadcast_to(number, (INFO, 2 * HEAD)).astype(jnp.bfloat16)


def select(used, kept, keys, values):
    length = keys.shape[0]
    rows = (KEEP, length - KEEP + INFO)
    return pl.pallas_call(
        select_kernel,
        out_shape=[jax.ShapeDtypeStruct((n, 2 * HEAD), jnp.bfloat16) for n in rows],
        in_specs=[SMEM, HBM, HBM, HBM],
        out_specs=[VMEM] * 2,
        scratch_shapes=[
            *[pltpu.VMEM(x.shape, x.dtype) for x in (kept, keys, values)],
            pltpu.SemaphoreType.DMA((3,)),
        ],
        compiler_params=PARAMS,
        name="select_kept",
    )(used, kept, keys, values)


def wide(column, width):
    return jnp.concatenate([column] * (width // HEAD), axis=1)


def widened(values):
    return jnp.concatenate([values, jnp.ones_like(values)], axis=1)


def scores(query, keys):
    return dot_nt(query, keys) * FACTOR


def local(query, keys, values, acc_ref, peak_ref):
    length = query.shape[0]
    causal = count_along((length, length), 1) <= count_along((length, length), 0)
    raw = jnp.where(causal, scores(query, keys), NEGATIVE)
    peak = jnp.broadcast_to(jnp.max(raw, axis=1, keepdims=True), (length, HEAD))
    peak_ref[...] = peak
    weights = jnp.exp2(raw - wide(peak, length)).astype(jnp.bfloat16)
    acc_ref[...] = dot(weights, widened(values))


def biased(raw, bias):
    if bias is None:
        return raw
    return (raw.reshape(-1, *bias.shape) + bias).reshape(raw.shape)


def fixed(heads, view, keys, values, bias):
    raw = scores(view(0)[0], keys)
    for h in range(heads):
        _, acc_ref, peak_ref = view(h)
        ahead = scores(view(h + 1)[0], keys) if h + 1 < heads else None
        weights = jnp.exp2(biased(raw, bias) - wide(peak_ref[...], keys.shape[0]))
        acc_ref[...] += dot(weights.astype(jnp.bfloat16), values)
        raw = ahead


def moving(query, acc_ref, peak_ref, keys, values, bias):
    raw = biased(scores(query, keys), bias)
    old = peak_ref[...]
    peak = jnp.maximum(old, jnp.max(raw, axis=1, keepdims=True))
    weights = jnp.exp2(raw - wide(peak, keys.shape[0])).astype(jnp.bfloat16)
    peak_ref[...] = peak
    acc_ref[...] = acc_ref[...] * wide(jnp.exp2(old - peak), 2 * HEAD) + dot(weights, values)


def absorb(heads, view, masked, steps, read):
    if masked is not None:

        @pl.loop(0, masked)
        def _(step):
            fixed(heads, view, *read(step, True))

    @pl.loop(0, steps)
    def _(step):
        fixed(heads, view, *read(step, False))


def absorb_again(acc_ref, view, start, tiles, read):
    largest = jnp.max(acc_ref[:, :, HEAD:])

    @pl.when(jnp.logical_not(largest < LIMIT))
    def _():
        @pl.loop(0, acc_ref.shape[0])
        def _(h):
            start(h)

            @pl.loop(0, tiles)
            def _(tile):
                moving(*view(h), *read(tile))


def tile_of(ref, start, size):
    rows = pl.ds(pl.multiple_of(start, TILE), size)
    return ref[rows, :HEAD], widened(ref[rows, HEAD:])


def head_view(q_ref, acc_ref, peak_ref):
    def view(h):
        columns = pl.ds(pl.multiple_of(h * HEAD, HEAD), HEAD)
        return q_ref[:, columns], acc_ref.at[h], peak_ref.at[h]

    return view


def bias_where(allowed):
    return jnp.where(allowed, 0.0, NEGATIVE)


def sums(state_ref):
    return state_ref.at[:, :, pl.ds(0, 2 * HEAD)], state_ref.at[:, :, pl.ds(2 * HEAD, HEAD)]


def own_row_kernel(
    place_ref, q_ref, k_ref, v_ref, row_a, row_b, one_a, other_b, state_ref, bank_ref, bias_ref,
    sems,
):
    y, z, core = place_ref[0] // WIDE, place_ref[0] % WIDE, place_ref[3]
    acc_ref, peak_ref = sums(state_ref)
    keys, half = z * KEEP, row_a.shape[0]
    row_steps = keys // STEP
    masked = (keys - row_steps * STEP + TILE - 1) // TILE
    copies = [
        (row_a, bank_ref.at[pl.ds(0, half)], z >= 0),
        (row_b, bank_ref.at[pl.ds(half, half)], z >= 0),
        (one_a, bank_ref.at[pl.ds(2 * half, half)], (core == 0) & (y > 0)),
        (other_b, bank_ref.at[pl.ds(2 * half, half)], (core == 1) & (y > 0)),
        (one_a, bank_ref.at[pl.ds(3 * half, half)], (core == 1) & (y == 3)),
        (other_b, bank_ref.at[pl.ds(3 * half, half)], (core == 0) & (y == 3)),
    ]
    copies = [
        (pltpu.make_async_copy(source, target, sems.at[at]), on)
        for at, (source, target, on) in enumerate(copies)
    ]
    for one, on in copies:
        pl.when(on)(one.start)
    view, heads = head_view(q_ref, acc_ref, peak_ref), acc_ref.shape[0]

    def start(h):
        query, acc, peak = view(h)
        local(query, k_ref[...], v_ref[...], acc, peak)

    def read_masked(tile):
        at = row_steps * STEP + tile * TILE
        bias_ref[...] = bias_where(count_along(bias_ref.shape, 1) + at < keys)
        return *tile_of(bank_ref, at, TILE), bias_ref[...]

    def step_start(step):
        return jnp.where(step < row_steps, step, step - row_steps + 2 * half // STEP) * STEP

    def read_fast(step, with_bias):
        if with_bias:
            return read_masked(step)
        for at, (one, on) in enumerate(copies[2:]):
            pl.when(on & (step == row_steps + at // 2))(one.wait)
        return *tile_of(bank_ref, step_start(step), STEP), None

    def read(tile):
        after = jnp.maximum(tile - masked, 0)
        plain = step_start(after // 2) + after % 2 * TILE
        at = jnp.where(tile < masked, row_steps * STEP + tile * TILE, plain)
        limit = jnp.where(tile < masked, keys, bank_ref.shape[0])
        bias_ref[...] = bias_where(count_along(bias_ref.shape, 1) + at < limit)
        return *tile_of(bank_ref, at, TILE), bias_ref[...]

    for h in range(heads):
        start(h)
    for one, on in copies[:2]:
        pl.when(on)(one.wait)
    steps = row_steps + jnp.where(y == 3, 2, jnp.minimum(y, 1))
    absorb(heads, view, masked, steps, read_fast)
    absorb_again(acc_ref, view, start, masked + STEP // TILE * steps, read)


def more_keys(queries, rest_ref, state_in, refs, used, firsts, pieces, steps, then):
    acc_ref, peak_ref, q_ref, bank_ref, carried_ref, bias_ref, sems = refs
    acc_in, peak_in = sums(state_in)
    copies = [(queries, q_ref, True), (peak_in, peak_ref, True)]
    copies += [(ref.at[pl.ds(0, KEEP)], bank_ref.at[pl.ds(0, KEEP)], on) for ref, on in firsts]
    for ref, on, at in pieces:
        copies.append((ref, bank_ref.at[pl.ds(TILE + at * STEP, STEP)], on))
    copies.append((acc_in, carried_ref, True))
    copies = [
        (pltpu.make_async_copy(source, target, sems.at[at]), on)
        for at, (source, target, on) in enumerate(copies)
    ]

    def under(condition, act):
        if condition is True:
            act()
        else:
            pl.when(condition)(act)

    for one, on in copies:
        under(on, one.start)
    then()
    acc_ref[...] = jnp.zeros(acc_ref.shape, jnp.float32)
    view, masked = head_view(q_ref, acc_ref, peak_ref), None
    if firsts:
        bank_ref[KEEP:TILE] = rest_ref[: TILE - KEEP]
        number = wide(rest_ref[TILE - KEEP : TILE - KEEP + 1, :HEAD].astype(jnp.int32), TILE)
        at = count_along((1, TILE), 1)
        limit = jnp.where(at < KEEP, number, KEEP + used - number)
        bias_ref[0] = jnp.broadcast_to(bias_where(at < limit), bias_ref.shape[1:])
        bias_ref[1] = jnp.zeros(bias_ref.shape[1:], jnp.float32)
        masked = sum(jnp.where(on, 1, 0) for _, on in firsts)

    def start(h):
        acc_ref[h] = carried_ref[h]

    def read(step):
        if masked is None:
            return *tile_of(bank_ref, TILE + step * TILE, TILE), None
        tile = jnp.where(masked > 0, step, step + 1)
        return *tile_of(bank_ref, tile * TILE, TILE), bias_ref[jnp.minimum(tile, 1)]

    here, later = copies[2 : 2 + len(firsts)], copies[2 + len(firsts) : -1]

    def read_fast(step, with_bias):
        if with_bias:
            for one, on in here:
                under(on, one.wait)
            return *tile_of(bank_ref, 0, TILE), bias_ref[0]
        for (one, on), (_, _, at) in zip(later, pieces):
            pl.when(on & (step == at))(one.wait)
        return *tile_of(bank_ref, TILE + step * STEP, STEP), None

    for one, _ in copies[:2]:
        one.wait()
    absorb(acc_ref.shape[0], view, masked, steps, read_fast)
    copies[-1][0].wait()
    acc_ref[...] += carried_ref[...]
    tiles = STEP // TILE * steps + (0 if masked is None else masked)
    absorb_again(acc_ref, view, start, tiles, read)


def rest_kernel(
    place_ref, rest_ref, queries, first_ref, one_b, other_a, two_a, two_b, weight_ref, state_in,
    own_out, far_out, near_out, own_ref, send_ref, w_ref, att_ref, out_sems, *refs,
):
    mine, used = place_ref[0], place_ref[1]
    y = mine // WIDE
    core = place_ref[3]
    last = (core == 1) & (y == 1) | (core == 0) & (y == 3)
    pieces = (
        (one_b, (core == 0) & (y > 0), 0),
        (other_a, (core == 1) & (y > 0), 0),
        (two_a, y > 1, 1),
        (two_b, y > 1, 2),
        (one_b, (core == 1) & (y == 3), 3),
        (other_a, (core == 0) & (y == 3), 3),
    )
    firsts = (first_ref, (mine > 0) & (y != 2) & ~last), (two_a, y == 2), (other_a, last)
    steps = jnp.where(y == 3, 4, jnp.where(y == 2, 3, y))
    weight_copy = pltpu.make_async_copy(weight_ref, w_ref, out_sems.at[3])
    more_keys(
        queries, rest_ref, state_in, refs, used, firsts, pieces, steps, weight_copy.start
    )
    acc_ref = refs[0]
    for h in range(acc_ref.shape[0]):
        att_ref[:, h * HEAD : (h + 1) * HEAD] = (
            acc_ref[h, :, :HEAD] / acc_ref[h, :, HEAD:]
        ).astype(jnp.bfloat16)
    weight_copy.wait()
    chips, _, columns = own_out.shape
    chip, core = place_ref[2], place_ref[3]

    @pl.loop(0, chips)
    def _(step):
        ahead = jnp.where(step == 0, 2, jnp.where(step == 1, 1, jnp.where(step == 2, 3, 0)))
        column = lax.rem(chip + ahead, chips) * 2
        for ref, side in ((own_ref, core), (send_ref, 1 - core)):
            start = pl.multiple_of((column + side) * columns, columns)
            ref[step] = dot(att_ref[...], w_ref[:, pl.ds(start, columns)]).astype(jnp.bfloat16)
        pltpu.make_async_copy(own_ref.at[step], own_out.at[step], out_sems.at[0]).start()

        @pl.when(step == 0)
        def _():
            pltpu.make_async_copy(send_ref.at[0], far_out, out_sems.at[1]).start()

        @pl.when(step > 0)
        def _():
            target = near_out.at[step - 1]
            pltpu.make_async_copy(send_ref.at[step], target, out_sems.at[2]).start()

    pltpu.make_async_copy(own_ref, own_out, out_sems.at[0]).wait()
    pltpu.make_async_copy(send_ref.at[0], far_out, out_sems.at[1]).wait()
    pltpu.make_async_copy(send_ref.at[pl.ds(1, chips - 1)], near_out, out_sems.at[2]).wait()


def pack_row_kernel(moves, place_ref, *refs):
    z, way = place_ref[0] % WIDE, 1 - 2 * place_ref[3]
    middle = WIDE * KEEP // 2
    for ref, (blocks, row) in zip(refs[:-2], moves):
        start = lax.rem(z + way * blocks + WIDE, WIDE) * KEEP + row
        for out_ref, first in zip(refs[-2:], (0, middle)):

            @pl.when((start >= first) & (start < first + middle))
            def _():
                at = pl.multiple_of(start - first, KEEP // 2)
                out_ref[pl.ds(at, ref.shape[0])] = ref[...]


def pack_row(place, pieces, moves):
    return pl.pallas_call(
        functools.partial(pack_row_kernel, moves),
        out_shape=[jax.ShapeDtypeStruct((WIDE * KEEP // 2, 2 * HEAD), jnp.bfloat16)] * 2,
        in_specs=[SMEM] + [VMEM] * len(pieces),
        out_specs=[VMEM] * 2,
        compiler_params=pltpu.CompilerParams(vmem_limit_bytes=8 * 2**20),
        name="pack_row",
    )(place, *pieces)


def cost(rows, keys):
    return pl.CostEstimate(
        flops=rows * keys * HEAD * 8, bytes_accessed=8 * 2**20, transcendentals=rows * keys
    )


def state_of(length, heads):
    return jax.ShapeDtypeStruct((heads, length, 3 * HEAD), jnp.float32)


def own_row(place, queries, keys, values, *pieces):
    length, width = queries.shape
    whole = lambda x: pl.BlockSpec(x.shape, lambda i: (0,) * len(x.shape))
    state = state_of(length, width // HEAD)
    return pl.pallas_call(
        own_row_kernel,
        grid=(1,),
        out_shape=state,
        in_specs=[SMEM, *[whole(x) for x in (queries, keys, values)], *[ANY] * len(pieces)],
        out_specs=whole(state),
        scratch_shapes=[
            pltpu.VMEM((4 * STEP, 2 * HEAD), jnp.bfloat16),
            pltpu.VMEM((8, TILE), jnp.float32),
            pltpu.SemaphoreType.DMA((6,)),
        ],
        compiler_params=PARAMS,
        cost_estimate=cost(length * width // HEAD, length + 4 * STEP),
        name="own_row",
    )(place, queries, keys, values, *pieces)


def rest_rows(place, queries, rest, banks, weight, state, chips):
    length, width = queries.shape
    heads, keys = width // HEAD, TILE + 4 * STEP
    whole = lambda x: pl.BlockSpec(x.shape, lambda i: (0,) * len(x.shape))
    one = (length, weight.shape[1] // chips // 2)
    shapes = (chips, *one), one, (chips - 1, *one)
    return pl.pallas_call(
        rest_kernel,
        grid=(1,),
        out_shape=[jax.ShapeDtypeStruct(shape, jnp.bfloat16) for shape in shapes],
        in_specs=[SMEM, whole(rest), *[ANY] * (len(banks) + 3)],
        out_specs=[ANY] * 3,
        scratch_shapes=[
            *[pltpu.VMEM((chips, *one), jnp.bfloat16)] * 2,
            pltpu.VMEM(weight.shape, weight.dtype),
            pltpu.VMEM((length, width), jnp.bfloat16),
            pltpu.SemaphoreType.DMA((4,)),
            pltpu.VMEM((heads, length, 2 * HEAD), jnp.float32),
            pltpu.VMEM((heads, length, HEAD), jnp.float32),
            pltpu.VMEM((length, width), jnp.bfloat16),
            pltpu.VMEM((keys, 2 * HEAD), jnp.bfloat16),
            pltpu.VMEM((heads, length, 2 * HEAD), jnp.float32),
            pltpu.VMEM((2, 8, TILE), jnp.float32),
            pltpu.SemaphoreType.DMA((12,)),
        ],
        compiler_params=pltpu.CompilerParams(vmem_limit_bytes=47 * 2**20),
        cost_estimate=cost(length * heads, keys),
        name="rest_rows",
    )(place, rest, queries, *banks, weight, state)


def summed(*refs):
    return sum(ref[...].astype(jnp.float32) for ref in refs)


def cross_kernel(own_ref, other_ref, upper_ref, lower_ref):
    total = summed(own_ref, other_ref).astype(jnp.bfloat16)
    half = upper_ref.shape[0]
    upper_ref[...] = total[:half]
    lower_ref[...] = total[half:]


def add_kernel(*refs):
    terms = refs[:-2]
    middle = len(terms) // 2
    refs[-2][...] = summed(*terms[:middle]).astype(jnp.bfloat16)
    refs[-1][...] = summed(*terms[middle:]).astype(jnp.bfloat16)


def halves_kernel(*refs):
    (*terms, upper_ref, lower_ref), out_ref = refs[:-1], refs[-1]
    half, total = upper_ref.shape[0], summed(*terms)
    out_ref[:half] = (total[:half] + summed(upper_ref)).astype(out_ref.dtype)
    out_ref[half:] = (total[half:] + summed(lower_ref)).astype(out_ref.dtype)


def small_call(kernel, name, terms, shapes, dtype=jnp.bfloat16):
    def spec(term):
        if not isinstance(term, tuple):
            return pl.BlockSpec(term.shape, lambda i: (0, 0))
        x, chunk, half = term
        rows = x.shape[1] // (1 if half is None else 2)
        return pl.BlockSpec((None, rows, x.shape[2]), lambda i: (chunk, half or 0, 0))

    return pl.pallas_call(
        kernel,
        grid=(1,),
        out_shape=[jax.ShapeDtypeStruct(shape, dtype) for shape in shapes],
        in_specs=[spec(term) for term in terms],
        out_specs=[pl.BlockSpec(shape, lambda i: (0, 0)) for shape in shapes],
        compiler_params=pltpu.CompilerParams(vmem_limit_bytes=8 * 2**20),
        name=name,
    )(*[term[0] if isinstance(term, tuple) else term for term in terms])


def on_device(queries, key_rows, value_rows, kept_positions, anchor_length, output_weight):
    mine, head = lax.axis_index("ctx"), lax.axis_index("head")
    length, devices, blocks = queries.shape[0], lax.axis_size("head"), lax.axis_size("ctx")
    chips, chip, core = devices // 2, head // 2, head % 2
    tall = blocks // WIDE
    swap = [(i, i ^ 1) for i in range(devices)]
    up = [(i, (i + 2) % devices) for i in range(devices)]
    down = [(i, (i - 2) % devices) for i in range(devices)]
    along = lambda step: [
        (r * WIDE + c, r * WIDE + (c + step) % WIDE) for r in range(tall) for c in range(WIDE)
    ]
    across = lambda hops: [(a * WIDE + c, b * WIDE + c) for a, b in hops for c in range(WIDE)]
    permute = lambda x, pairs: lax.ppermute(x, "ctx", pairs)

    def both(x, *ways):
        pairs = [
            (a * devices + h, b * devices + h)
            for one, way in enumerate(ways)
            for a, b in way
            for h in range(one, devices, 2)
        ]
        return lax.ppermute(x, ("ctx", "head"), pairs)

    spots = jnp.stack([chip, core]).astype(jnp.int32)
    place = jnp.concatenate([mine.astype(jnp.int32)[None], anchor_length, spots])
    kept, rest = select(anchor_length, kept_positions, key_rows, value_rows)

    plus, minus = along(1), along(-1)
    half = KEEP // 2
    left, right = [kept], [kept]
    rest = jnp.where(mine == 0, rest, jnp.zeros_like(rest))
    spread = lambda hops: [(r * WIDE + a, r * WIDE + b) for a, b in hops for r in range(tall)]
    upward = [(0, WIDE)], [(0, 3 * WIDE), (WIDE, 2 * WIDE)]
    for step in range(WIDE // 2 - 1):
        left.append(both(left[-1], plus, minus))
        right.append(both(right[-1], minus, plus))
        if step < len(upward):
            rest = rest + permute(rest, upward[step])
        else:
            left[-1], right[-1], rest = lax.optimization_barrier((left[-1], right[-1], rest))
    left.append(both(left[-1][:half], plus, minus))
    right.append(both(right[-1][half:], minus, plus))
    moves = [(-at, 0) for at in range(5)] + [(1, 0), (2, 0), (3, 0), (4, half)]
    ends = pack_row(place, left + right[1:], moves)

    to_above, to_below = across([(0, 1), (1, 2), (2, 3)]), across([(0, 3), (1, 0)])
    one_a = both(ends[0], to_above, to_below)
    other_b = both(ends[1], to_below, to_above)
    rest, ends = lax.optimization_barrier((rest, ends))
    rest = rest + permute(rest, spread([(0, 2)]))
    rest = rest + permute(rest, spread([(0, 6), (2, 4)]))
    rest, one_a, other_b, ends = lax.optimization_barrier((rest, one_a, other_b, ends))
    one_b = both(ends[1], to_above, across([(0, 3)]))
    other_a = both(ends[0], across([(0, 3)]), to_above)
    on_above, on_below = across([(1, 2), (2, 3)]), across([(0, 3), (3, 2)])
    two_a = both(one_a, on_above, on_below)
    two_b = both(other_b, on_below, on_above)
    rest = rest + permute(rest, spread([(0, 1), (2, 3), (4, 5), (6, 7)]))
    state = own_row(place, queries, key_rows, value_rows, *ends, one_a, other_b)
    y = mine // WIDE
    came = (y == 1) & (core == 0) | (y == 3) & (core == 1)
    first = jnp.where(came, one_a[:KEEP], ends[0][:KEEP])
    banks = (first, one_b, other_a, two_a, two_b)
    own, far, near = rest_rows(place, queries, rest, banks, output_weight, state, chips)

    far, near = lax.optimization_barrier((lax.ppermute(far, "head", swap), near))
    near = lax.ppermute(near, "head", swap)
    columns = own.shape[2]
    whole, half = (length, columns), (length // 2, columns)
    upper, lower = small_call(cross_kernel, "cross", [(own, 0, None), far], [half, half])
    upper, lower = lax.ppermute(upper, "head", up), lax.ppermute(lower, "head", down)
    terms = [(own, 1, 1), (near, 0, 1), (own, 2, 0), (near, 1, 0)]
    lower_up, upper_down = small_call(add_kernel, "direct", terms, [half, half])
    upper, lower, _, _ = lax.optimization_barrier((upper, lower, lower_up, upper_down))
    lower_up, upper_down = lax.ppermute(lower_up, "head", up), lax.ppermute(upper_down, "head", down)
    terms = [(own, 1, 0), (near, 0, 0), upper, (own, 2, 1), (near, 1, 1), lower]
    upper_up, lower_down = small_call(add_kernel, "turn", terms, [half, half])
    upper_up, lower_down = lax.ppermute(upper_up, "head", up), lax.ppermute(lower_down, "head", down)
    terms = [(own, 3, None), (near, 2, None), upper_down, lower_up]
    (total,) = small_call(halves_kernel, "collect", terms, [whole], jnp.float32)
    return small_call(halves_kernel, "finish", [total, upper_up, lower_down], [whole])[0]


def solution(mesh):
    placed = (
        P("ctx", "head"),
        P("ctx", "head"),
        P("ctx", "head"),
        P("head", "ctx"),
        P("head"),
        P("head", None),
    )
    return jax.shard_map(
        on_device, mesh=mesh, in_specs=placed, out_specs=P("ctx", "head"), check_vma=False
    )
```

```python
import functools

import jax
import jax.numpy as jnp
from jax import lax
from jax.experimental import pallas as pl
from jax.experimental.pallas import tpu as pltpu
from jax.sharding import PartitionSpec as P

HEAD = 128
WIDE = 8
INFO = 16
KEEP = 256
LOG2E = 1.4426950408889634
FACTOR = HEAD**-0.5 * LOG2E
LIMIT = 2.0**100
NEGATIVE = -1e30
NT = (((1,), (1,)), ((), ()))
VMEM = pl.BlockSpec(memory_space=pltpu.VMEM)
SMEM = pl.BlockSpec(memory_space=pltpu.SMEM)
HBM = pl.BlockSpec(memory_space=pltpu.HBM)
ANY = pl.BlockSpec(memory_space=pl.ANY)
TILE = 512
STEP = 1024
PARAMS = pltpu.CompilerParams(vmem_limit_bytes=60 * 2**20)


def dot(a, b):
    return jnp.dot(a, b, preferred_element_type=jnp.float32)


def dot_nt(a, b):
    return lax.dot_general(a, b, NT, preferred_element_type=jnp.float32)


def count_along(shape, dim):
    return lax.broadcasted_iota(jnp.int32, shape, dim)


def ones_where(condition):
    return jnp.where(condition, 1.0, 0.0).astype(jnp.bfloat16)


def select_kernel(used_ref, *refs):
    sources, (kept_rows_ref, rest_ref), targets, sems = refs[:3], refs[3:5], refs[5:8], refs[8]
    copies = [
        pltpu.make_async_copy(source, target, sems.at[at])
        for at, (source, target) in enumerate(zip(sources, targets))
    ]
    for copy in copies:
        copy.start()
    for copy in copies:
        copy.wait()
    kept_ref, key_ref, value_ref = targets
    length, keep = key_ref.shape[0], kept_ref.shape[1]
    hit = ones_where(count_along((length, keep), 0) == kept_ref[...])
    kept = dot_nt(jnp.ones((8, keep), jnp.bfloat16), hit)
    square = (length, length)
    before = ones_where(count_along(square, 0) < count_along(square, 1))
    rank = dot(kept.astype(jnp.bfloat16), before)
    column = count_along((8, length), 1)
    place = jnp.where(kept > 0.5, rank, column.astype(jnp.float32) + keep - rank)
    order = ones_where(count_along(square, 0).astype(jnp.float32) == place[:1])
    for at, ref in enumerate((key_ref, value_ref)):
        columns = slice(at * HEAD, (at + 1) * HEAD)
        rows = dot(order, ref[...]).astype(jnp.bfloat16)
        kept_rows_ref[:, columns] = rows[:keep]
        rest_ref[: length - keep, columns] = rows[keep:]
    in_both = jnp.where((kept > 0.5) & (column < used_ref[0]), 1.0, 0.0)[:1]
    number = jnp.sum(in_both, axis=1, keepdims=True)
    rest_ref[length - keep :] = jnp.broadcast_to(number, (INFO, 2 * HEAD)).astype(jnp.bfloat16)


def select(used, kept, keys, values):
    length = keys.shape[0]
    rows = (KEEP, length - KEEP + INFO)
    return pl.pallas_call(
        select_kernel,
        out_shape=[jax.ShapeDtypeStruct((n, 2 * HEAD), jnp.bfloat16) for n in rows],
        in_specs=[SMEM, HBM, HBM, HBM],
        out_specs=[VMEM] * 2,
        scratch_shapes=[
            *[pltpu.VMEM(x.shape, x.dtype) for x in (kept, keys, values)],
            pltpu.SemaphoreType.DMA((3,)),
        ],
        compiler_params=PARAMS,
        name="select_kept",
    )(used, kept, keys, values)


def wide(column, width):
    return jnp.concatenate([column] * (width // HEAD), axis=1)


def widened(values):
    return jnp.concatenate([values, jnp.ones_like(values)], axis=1)


def scores(query, keys):
    return dot_nt(query, keys) * FACTOR


def local(query, keys, values, acc_ref, peak_ref):
    length = query.shape[0]
    causal = count_along((length, length), 1) <= count_along((length, length), 0)
    raw = jnp.where(causal, scores(query, keys), NEGATIVE)
    peak = jnp.broadcast_to(jnp.max(raw, axis=1, keepdims=True), (length, HEAD))
    peak_ref[...] = peak
    weights = jnp.exp2(raw - wide(peak, length)).astype(jnp.bfloat16)
    acc_ref[...] = dot(weights, widened(values))


def biased(raw, bias):
    if bias is None:
        return raw
    return (raw.reshape(-1, *bias.shape) + bias).reshape(raw.shape)


def fixed(heads, view, keys, values, bias):
    raw = scores(view(0)[0], keys)
    for h in range(heads):
        _, acc_ref, peak_ref = view(h)
        ahead = scores(view(h + 1)[0], keys) if h + 1 < heads else None
        weights = jnp.exp2(biased(raw, bias) - wide(peak_ref[...], keys.shape[0]))
        acc_ref[...] += dot(weights.astype(jnp.bfloat16), values)
        raw = ahead


def moving(query, acc_ref, peak_ref, keys, values, bias):
    raw = biased(scores(query, keys), bias)
    old = peak_ref[...]
    peak = jnp.maximum(old, jnp.max(raw, axis=1, keepdims=True))
    weights = jnp.exp2(raw - wide(peak, keys.shape[0])).astype(jnp.bfloat16)
    peak_ref[...] = peak
    acc_ref[...] = acc_ref[...] * wide(jnp.exp2(old - peak), 2 * HEAD) + dot(weights, values)


def absorb(heads, view, masked, steps, read):
    if masked is not None:

        @pl.loop(0, masked)
        def _(step):
            fixed(heads, view, *read(step, True))

    @pl.loop(0, steps)
    def _(step):
        fixed(heads, view, *read(step, False))


def absorb_again(acc_ref, view, start, tiles, read):
    largest = jnp.max(acc_ref[:, :, HEAD:])

    @pl.when(jnp.logical_not(largest < LIMIT))
    def _():
        @pl.loop(0, acc_ref.shape[0])
        def _(h):
            start(h)

            @pl.loop(0, tiles)
            def _(tile):
                moving(*view(h), *read(tile))


def tile_of(ref, start, size):
    rows = pl.ds(pl.multiple_of(start, TILE), size)
    return ref[rows, :HEAD], widened(ref[rows, HEAD:])


def head_view(q_ref, acc_ref, peak_ref):
    def view(h):
        columns = pl.ds(pl.multiple_of(h * HEAD, HEAD), HEAD)
        return q_ref[:, columns], acc_ref.at[h], peak_ref.at[h]

    return view


def bias_where(allowed):
    return jnp.where(allowed, 0.0, NEGATIVE)


def sums(state_ref):
    return state_ref.at[:, :, pl.ds(0, 2 * HEAD)], state_ref.at[:, :, pl.ds(2 * HEAD, HEAD)]


def own_row_kernel(
    place_ref, q_ref, k_ref, v_ref, row_a, row_b, below_a, above_b, state_ref, bank_ref, bias_ref,
    sems,
):
    y, z = place_ref[0] // WIDE, place_ref[0] % WIDE
    acc_ref, peak_ref = sums(state_ref)
    keys, half = z * KEEP, row_a.shape[0]
    row_steps = keys // STEP
    masked = (keys - row_steps * STEP + TILE - 1) // TILE
    copies = [
        (row_a, bank_ref.at[pl.ds(0, half)], z >= 0),
        (row_b, bank_ref.at[pl.ds(half, half)], z >= 0),
        (below_a, bank_ref.at[pl.ds(2 * half, half)], y > 0),
        (above_b, bank_ref.at[pl.ds(3 * half, half)], y == 3),
    ]
    copies = [
        (pltpu.make_async_copy(source, target, sems.at[at]), on)
        for at, (source, target, on) in enumerate(copies)
    ]
    for one, on in copies:
        pl.when(on)(one.start)
    view, heads = head_view(q_ref, acc_ref, peak_ref), acc_ref.shape[0]

    def start(h):
        query, acc, peak = view(h)
        local(query, k_ref[...], v_ref[...], acc, peak)

    def read_masked(tile):
        at = row_steps * STEP + tile * TILE
        bias_ref[...] = bias_where(count_along(bias_ref.shape, 1) + at < keys)
        return *tile_of(bank_ref, at, TILE), bias_ref[...]

    def step_start(step):
        return jnp.where(step < row_steps, step, step - row_steps + 2 * half // STEP) * STEP

    def read_fast(step, with_bias):
        if with_bias:
            return read_masked(step)
        for at, (one, on) in enumerate(copies[2:]):
            pl.when(on & (step == row_steps + at))(one.wait)
        return *tile_of(bank_ref, step_start(step), STEP), None

    def read(tile):
        after = jnp.maximum(tile - masked, 0)
        plain = step_start(after // 2) + after % 2 * TILE
        at = jnp.where(tile < masked, row_steps * STEP + tile * TILE, plain)
        limit = jnp.where(tile < masked, keys, bank_ref.shape[0])
        bias_ref[...] = bias_where(count_along(bias_ref.shape, 1) + at < limit)
        return *tile_of(bank_ref, at, TILE), bias_ref[...]

    for h in range(heads):
        start(h)
    for one, on in copies[:2]:
        pl.when(on)(one.wait)
    steps = row_steps + jnp.where(y == 3, 2, jnp.minimum(y, 1))
    absorb(heads, view, masked, steps, read_fast)
    absorb_again(acc_ref, view, start, masked + STEP // TILE * steps, read)


def more_keys(queries, rest_ref, state_in, refs, used, firsts, pieces, steps, then):
    acc_ref, peak_ref, q_ref, bank_ref, carried_ref, bias_ref, sems = refs
    acc_in, peak_in = sums(state_in)
    copies = [(queries, q_ref, True), (peak_in, peak_ref, True)]
    copies += [(ref.at[pl.ds(0, KEEP)], bank_ref.at[pl.ds(0, KEEP)], on) for ref, on in firsts]
    for at, (ref, on) in enumerate(pieces):
        copies.append((ref, bank_ref.at[pl.ds(TILE + at * STEP, STEP)], on))
    copies.append((acc_in, carried_ref, True))
    copies = [
        (pltpu.make_async_copy(source, target, sems.at[at]), on)
        for at, (source, target, on) in enumerate(copies)
    ]

    def under(condition, act):
        if condition is True:
            act()
        else:
            pl.when(condition)(act)

    for one, on in copies:
        under(on, one.start)
    then()
    acc_ref[...] = jnp.zeros(acc_ref.shape, jnp.float32)
    view, masked = head_view(q_ref, acc_ref, peak_ref), None
    if firsts:
        bank_ref[KEEP:TILE] = rest_ref[: TILE - KEEP]
        number = wide(rest_ref[TILE - KEEP : TILE - KEEP + 1, :HEAD].astype(jnp.int32), TILE)
        at = count_along((1, TILE), 1)
        limit = jnp.where(at < KEEP, number, KEEP + used - number)
        bias_ref[0] = jnp.broadcast_to(bias_where(at < limit), bias_ref.shape[1:])
        bias_ref[1] = jnp.zeros(bias_ref.shape[1:], jnp.float32)
        masked = sum(jnp.where(on, 1, 0) for _, on in firsts)

    def start(h):
        acc_ref[h] = carried_ref[h]

    def read(step):
        if masked is None:
            return *tile_of(bank_ref, TILE + step * TILE, TILE), None
        tile = jnp.where(masked > 0, step, step + 1)
        return *tile_of(bank_ref, tile * TILE, TILE), bias_ref[jnp.minimum(tile, 1)]

    here, later = copies[2 : 2 + len(firsts)], copies[2 + len(firsts) : -1]

    def read_fast(step, with_bias):
        if with_bias:
            for one, on in here:
                under(on, one.wait)
            return *tile_of(bank_ref, 0, TILE), bias_ref[0]
        for at, (one, on) in enumerate(later):
            pl.when(on & (step == at))(one.wait)
        return *tile_of(bank_ref, TILE + step * STEP, STEP), None

    for one, _ in copies[:2]:
        one.wait()
    absorb(acc_ref.shape[0], view, masked, steps, read_fast)
    copies[-1][0].wait()
    acc_ref[...] += carried_ref[...]
    tiles = STEP // TILE * steps + (0 if masked is None else masked)
    absorb_again(acc_ref, view, start, tiles, read)


def rest_kernel(
    place_ref, rest_ref, queries, first_ref, below_b, above_a, below2_ref, above2_ref, weight_ref, state_in,
    own_out, far_out, near_out, own_ref, send_ref, w_ref, att_ref, out_sems, *refs,
):
    mine, used = place_ref[0], place_ref[1]
    y = mine // WIDE
    pieces = (below_b, y > 0), (below2_ref, y > 1), (above2_ref, y > 1), (above_a, y == 3)
    firsts = (first_ref, (mine > 0) & (y < 2)), (below2_ref, y == 2), (above_a, y == 3)
    steps = jnp.where(y == 3, 4, jnp.where(y == 2, 3, y))
    weight_copy = pltpu.make_async_copy(weight_ref, w_ref, out_sems.at[3])
    more_keys(
        queries, rest_ref, state_in, refs, used, firsts, pieces, steps, weight_copy.start
    )
    acc_ref = refs[0]
    for h in range(acc_ref.shape[0]):
        att_ref[:, h * HEAD : (h + 1) * HEAD] = (
            acc_ref[h, :, :HEAD] / acc_ref[h, :, HEAD:]
        ).astype(jnp.bfloat16)
    weight_copy.wait()
    chips, _, columns = own_out.shape
    chip, core = place_ref[2], place_ref[3]

    @pl.loop(0, chips)
    def _(step):
        ahead = jnp.where(step == 0, 2, jnp.where(step == 1, 1, jnp.where(step == 2, 3, 0)))
        column = lax.rem(chip + ahead, chips) * 2
        for ref, side in ((own_ref, core), (send_ref, 1 - core)):
            start = pl.multiple_of((column + side) * columns, columns)
            ref[step] = dot(att_ref[...], w_ref[:, pl.ds(start, columns)]).astype(jnp.bfloat16)
        pltpu.make_async_copy(own_ref.at[step], own_out.at[step], out_sems.at[0]).start()

        @pl.when(step == 0)
        def _():
            pltpu.make_async_copy(send_ref.at[0], far_out, out_sems.at[1]).start()

        @pl.when(step > 0)
        def _():
            target = near_out.at[step - 1]
            pltpu.make_async_copy(send_ref.at[step], target, out_sems.at[2]).start()

    pltpu.make_async_copy(own_ref, own_out, out_sems.at[0]).wait()
    pltpu.make_async_copy(send_ref.at[0], far_out, out_sems.at[1]).wait()
    pltpu.make_async_copy(send_ref.at[pl.ds(1, chips - 1)], near_out, out_sems.at[2]).wait()


def pack_row_kernel(place_ref, *refs):
    z = place_ref[0] % WIDE
    at, middle = KEEP, WIDE * KEEP // 2
    for ref in refs[:-2]:
        rows = ref.shape[0]
        start = pl.multiple_of(lax.rem(z * KEEP + at, WIDE * KEEP), KEEP // 2)
        at += rows
        for out_ref, first in zip(refs[-2:], (0, middle)):

            @pl.when((start >= first) & (start < first + middle))
            def _():
                out_ref[pl.ds(pl.multiple_of(start - first, KEEP // 2), rows)] = ref[...]


def pack_row(place, pieces):
    return pl.pallas_call(
        pack_row_kernel,
        out_shape=[jax.ShapeDtypeStruct((WIDE * KEEP // 2, 2 * HEAD), jnp.bfloat16)] * 2,
        in_specs=[SMEM] + [VMEM] * len(pieces),
        out_specs=[VMEM] * 2,
        compiler_params=pltpu.CompilerParams(vmem_limit_bytes=8 * 2**20),
        name="pack_row",
    )(place, *pieces)


def cost(rows, keys):
    return pl.CostEstimate(
        flops=rows * keys * HEAD * 8, bytes_accessed=8 * 2**20, transcendentals=rows * keys
    )


def state_of(length, heads):
    return jax.ShapeDtypeStruct((heads, length, 3 * HEAD), jnp.float32)


def own_row(place, queries, keys, values, *pieces):
    length, width = queries.shape
    whole = lambda x: pl.BlockSpec(x.shape, lambda i: (0,) * len(x.shape))
    state = state_of(length, width // HEAD)
    return pl.pallas_call(
        own_row_kernel,
        grid=(1,),
        out_shape=state,
        in_specs=[SMEM, *[whole(x) for x in (queries, keys, values)], *[ANY] * len(pieces)],
        out_specs=whole(state),
        scratch_shapes=[
            pltpu.VMEM((4 * STEP, 2 * HEAD), jnp.bfloat16),
            pltpu.VMEM((8, TILE), jnp.float32),
            pltpu.SemaphoreType.DMA((4,)),
        ],
        compiler_params=PARAMS,
        cost_estimate=cost(length * width // HEAD, length + 4 * STEP),
        name="own_row",
    )(place, queries, keys, values, *pieces)


def rest_rows(place, queries, rest, banks, weight, state, chips):
    length, width = queries.shape
    heads, keys = width // HEAD, TILE + 4 * STEP
    whole = lambda x: pl.BlockSpec(x.shape, lambda i: (0,) * len(x.shape))
    one = (length, weight.shape[1] // chips // 2)
    shapes = (chips, *one), one, (chips - 1, *one)
    return pl.pallas_call(
        rest_kernel,
        grid=(1,),
        out_shape=[jax.ShapeDtypeStruct(shape, jnp.bfloat16) for shape in shapes],
        in_specs=[SMEM, whole(rest), *[ANY] * (len(banks) + 3)],
        out_specs=[ANY] * 3,
        scratch_shapes=[
            *[pltpu.VMEM((chips, *one), jnp.bfloat16)] * 2,
            pltpu.VMEM(weight.shape, weight.dtype),
            pltpu.VMEM((length, width), jnp.bfloat16),
            pltpu.SemaphoreType.DMA((4,)),
            pltpu.VMEM((heads, length, 2 * HEAD), jnp.float32),
            pltpu.VMEM((heads, length, HEAD), jnp.float32),
            pltpu.VMEM((length, width), jnp.bfloat16),
            pltpu.VMEM((keys, 2 * HEAD), jnp.bfloat16),
            pltpu.VMEM((heads, length, 2 * HEAD), jnp.float32),
            pltpu.VMEM((2, 8, TILE), jnp.float32),
            pltpu.SemaphoreType.DMA((10,)),
        ],
        compiler_params=pltpu.CompilerParams(vmem_limit_bytes=47 * 2**20),
        cost_estimate=cost(length * heads, keys),
        name="rest_rows",
    )(place, rest, queries, *banks, weight, state)


def summed(*refs):
    return sum(ref[...].astype(jnp.float32) for ref in refs)


def cross_kernel(own_ref, other_ref, upper_ref, lower_ref):
    total = summed(own_ref, other_ref).astype(jnp.bfloat16)
    half = upper_ref.shape[0]
    upper_ref[...] = total[:half]
    lower_ref[...] = total[half:]


def add_kernel(*refs):
    terms = refs[:-2]
    middle = len(terms) // 2
    refs[-2][...] = summed(*terms[:middle]).astype(jnp.bfloat16)
    refs[-1][...] = summed(*terms[middle:]).astype(jnp.bfloat16)


def halves_kernel(*refs):
    (*terms, upper_ref, lower_ref), out_ref = refs[:-1], refs[-1]
    half, total = upper_ref.shape[0], summed(*terms)
    out_ref[:half] = (total[:half] + summed(upper_ref)).astype(out_ref.dtype)
    out_ref[half:] = (total[half:] + summed(lower_ref)).astype(out_ref.dtype)


def small_call(kernel, name, terms, shapes, dtype=jnp.bfloat16):
    def spec(term):
        if not isinstance(term, tuple):
            return pl.BlockSpec(term.shape, lambda i: (0, 0))
        x, chunk, half = term
        rows = x.shape[1] // (1 if half is None else 2)
        return pl.BlockSpec((None, rows, x.shape[2]), lambda i: (chunk, half or 0, 0))

    return pl.pallas_call(
        kernel,
        grid=(1,),
        out_shape=[jax.ShapeDtypeStruct(shape, dtype) for shape in shapes],
        in_specs=[spec(term) for term in terms],
        out_specs=[pl.BlockSpec(shape, lambda i: (0, 0)) for shape in shapes],
        compiler_params=pltpu.CompilerParams(vmem_limit_bytes=8 * 2**20),
        name=name,
    )(*[term[0] if isinstance(term, tuple) else term for term in terms])


def on_device(queries, key_rows, value_rows, kept_positions, anchor_length, output_weight):
    mine, head = lax.axis_index("ctx"), lax.axis_index("head")
    length, devices, blocks = queries.shape[0], lax.axis_size("head"), lax.axis_size("ctx")
    chips, chip, core = devices // 2, head // 2, head % 2
    tall = blocks // WIDE
    swap = [(i, i ^ 1) for i in range(devices)]
    up = [(i, (i + 2) % devices) for i in range(devices)]
    down = [(i, (i - 2) % devices) for i in range(devices)]
    along = lambda step: [
        (r * WIDE + c, r * WIDE + (c + step) % WIDE) for r in range(tall) for c in range(WIDE)
    ]
    across = lambda hops: [(a * WIDE + c, b * WIDE + c) for a, b in hops for c in range(WIDE)]
    permute = lambda x, pairs: lax.ppermute(x, "ctx", pairs)

    spots = jnp.stack([chip, core]).astype(jnp.int32)
    place = jnp.concatenate([mine.astype(jnp.int32)[None], anchor_length, spots])
    kept, rest = select(anchor_length, kept_positions, key_rows, value_rows)

    plus, minus = along(1), along(-1)
    half = KEEP // 2
    left, right = [kept], [kept]
    rest = jnp.where(mine == 0, rest, jnp.zeros_like(rest))
    spread = lambda hops: [(r * WIDE + a, r * WIDE + b) for a, b in hops for r in range(tall)]
    upward = [(0, WIDE)], [(0, 3 * WIDE), (WIDE, 2 * WIDE)]
    for step in range(WIDE // 2 - 1):
        left.append(permute(left[-1], plus))
        right.append(permute(right[-1], minus))
        if step < len(upward):
            rest = rest + permute(rest, upward[step])
    opposite = [permute(left[-1][:half], plus), permute(right[-1][half:], minus)]
    ends = pack_row(place, right[1:] + opposite + left[:0:-1] + [kept])

    rest, ends = lax.optimization_barrier((rest, ends))
    below_a = permute(ends[0], across([(0, 1), (1, 2), (2, 3)]))
    above_b = permute(ends[1], across([(0, 3), (1, 0)]))
    rest = rest + permute(rest, spread([(0, 2)]))
    rest = rest + permute(rest, spread([(0, 6), (2, 4)]))
    rest, below_a, above_b, ends = lax.optimization_barrier((rest, below_a, above_b, ends))
    below_b = permute(ends[1], across([(0, 1), (1, 2), (2, 3)]))
    above_a = permute(ends[0], across([(0, 3)]))
    below2 = permute(below_a, across([(1, 2), (2, 3)]))
    above2 = permute(above_b, across([(0, 3), (3, 2)]))
    rest = rest + permute(rest, spread([(0, 1), (2, 3), (4, 5), (6, 7)]))
    state = own_row(place, queries, key_rows, value_rows, *ends, below_a, above_b)
    first = jnp.where(mine // WIDE == 1, below_a[:KEEP], ends[0][:KEEP])
    banks = (first, below_b, above_a, below2, above2)
    own, far, near = rest_rows(place, queries, rest, banks, output_weight, state, chips)

    far, near = lax.optimization_barrier((lax.ppermute(far, "head", swap), near))
    near = lax.ppermute(near, "head", swap)
    columns = own.shape[2]
    whole, half = (length, columns), (length // 2, columns)
    upper, lower = small_call(cross_kernel, "cross", [(own, 0, None), far], [half, half])
    upper, lower = lax.ppermute(upper, "head", up), lax.ppermute(lower, "head", down)
    terms = [(own, 1, 1), (near, 0, 1), (own, 2, 0), (near, 1, 0)]
    lower_up, upper_down = small_call(add_kernel, "direct", terms, [half, half])
    upper, lower, _, _ = lax.optimization_barrier((upper, lower, lower_up, upper_down))
    lower_up, upper_down = lax.ppermute(lower_up, "head", up), lax.ppermute(upper_down, "head", down)
    terms = [(own, 1, 0), (near, 0, 0), upper, (own, 2, 1), (near, 1, 1), lower]
    upper_up, lower_down = small_call(add_kernel, "turn", terms, [half, half])
    upper_up, lower_down = lax.ppermute(upper_up, "head", up), lax.ppermute(lower_down, "head", down)
    terms = [(own, 3, None), (near, 2, None), upper_down, lower_up]
    (total,) = small_call(halves_kernel, "collect", terms, [whole], jnp.float32)
    return small_call(halves_kernel, "finish", [total, upper_up, lower_down], [whole])[0]


def solution(mesh):
    placed = (
        P("ctx", "head"),
        P("ctx", "head"),
        P("ctx", "head"),
        P("head", "ctx"),
        P("head"),
        P("head", None),
    )
    return jax.shard_map(
        on_device, mesh=mesh, in_specs=placed, out_specs=P("ctx", "head"), check_vma=False
    )
```

```python
import functools

import jax
import jax.numpy as jnp
from jax import lax
from jax.experimental import pallas as pl
from jax.experimental.pallas import tpu as pltpu
from jax.sharding import PartitionSpec as P

HEAD = 128
WIDE = 8
INFO = 16
KEEP = 256
LOG2E = 1.4426950408889634
FACTOR = HEAD**-0.5 * LOG2E
LIMIT = 2.0**100
NEGATIVE = -1e30
NT = (((1,), (1,)), ((), ()))
VMEM = pl.BlockSpec(memory_space=pltpu.VMEM)
SMEM = pl.BlockSpec(memory_space=pltpu.SMEM)
HBM = pl.BlockSpec(memory_space=pltpu.HBM)
ANY = pl.BlockSpec(memory_space=pl.ANY)
TILE = 512
STEP = 1024
PARAMS = pltpu.CompilerParams(vmem_limit_bytes=60 * 2**20)


def dot(a, b):
    return jnp.dot(a, b, preferred_element_type=jnp.float32)


def dot_nt(a, b):
    return lax.dot_general(a, b, NT, preferred_element_type=jnp.float32)


def count_along(shape, dim):
    return lax.broadcasted_iota(jnp.int32, shape, dim)


def ones_where(condition):
    return jnp.where(condition, 1.0, 0.0).astype(jnp.bfloat16)


def select_kernel(used_ref, *refs):
    sources, (kept_rows_ref, rest_ref), targets, sems = refs[:3], refs[3:5], refs[5:8], refs[8]
    copies = [
        pltpu.make_async_copy(source, target, sems.at[at])
        for at, (source, target) in enumerate(zip(sources, targets))
    ]
    for copy in copies:
        copy.start()
    for copy in copies:
        copy.wait()
    kept_ref, key_ref, value_ref = targets
    length, keep = key_ref.shape[0], kept_ref.shape[1]
    hit = ones_where(count_along((length, keep), 0) == kept_ref[...])
    kept = dot_nt(jnp.ones((8, keep), jnp.bfloat16), hit)
    square = (length, length)
    before = ones_where(count_along(square, 0) < count_along(square, 1))
    rank = dot(kept.astype(jnp.bfloat16), before)
    column = count_along((8, length), 1)
    place = jnp.where(kept > 0.5, rank, column.astype(jnp.float32) + keep - rank)
    order = ones_where(count_along(square, 0).astype(jnp.float32) == place[:1])
    for at, ref in enumerate((key_ref, value_ref)):
        columns = slice(at * HEAD, (at + 1) * HEAD)
        rows = dot(order, ref[...]).astype(jnp.bfloat16)
        kept_rows_ref[:, columns] = rows[:keep]
        rest_ref[: length - keep, columns] = rows[keep:]
    in_both = jnp.where((kept > 0.5) & (column < used_ref[0]), 1.0, 0.0)[:1]
    number = jnp.sum(in_both, axis=1, keepdims=True)
    rest_ref[length - keep :] = jnp.broadcast_to(number, (INFO, 2 * HEAD)).astype(jnp.bfloat16)


def select(used, kept, keys, values):
    length = keys.shape[0]
    rows = (KEEP, length - KEEP + INFO)
    return pl.pallas_call(
        select_kernel,
        out_shape=[jax.ShapeDtypeStruct((n, 2 * HEAD), jnp.bfloat16) for n in rows],
        in_specs=[SMEM, HBM, HBM, HBM],
        out_specs=[VMEM] * 2,
        scratch_shapes=[
            *[pltpu.VMEM(x.shape, x.dtype) for x in (kept, keys, values)],
            pltpu.SemaphoreType.DMA((3,)),
        ],
        compiler_params=PARAMS,
        name="select_kept",
    )(used, kept, keys, values)


def wide(column, width):
    return jnp.concatenate([column] * (width // HEAD), axis=1)


def widened(values):
    return jnp.concatenate([values, jnp.ones_like(values)], axis=1)


def scores(query, keys):
    return dot_nt(query, keys) * FACTOR


def local(query, keys, values, acc_ref, peak_ref):
    length = query.shape[0]
    causal = count_along((length, length), 1) <= count_along((length, length), 0)
    raw = jnp.where(causal, scores(query, keys), NEGATIVE)
    peak = jnp.broadcast_to(jnp.max(raw, axis=1, keepdims=True), (length, HEAD))
    peak_ref[...] = peak
    weights = jnp.exp2(raw - wide(peak, length)).astype(jnp.bfloat16)
    acc_ref[...] = dot(weights, widened(values))


def biased(raw, bias):
    if bias is None:
        return raw
    return (raw.reshape(-1, *bias.shape) + bias).reshape(raw.shape)


def fixed(heads, view, keys, values, bias):
    raw = scores(view(0)[0], keys)
    for h in range(heads):
        _, acc_ref, peak_ref = view(h)
        ahead = scores(view(h + 1)[0], keys) if h + 1 < heads else None
        weights = jnp.exp2(biased(raw, bias) - wide(peak_ref[...], keys.shape[0]))
        acc_ref[...] += dot(weights.astype(jnp.bfloat16), values)
        raw = ahead


def moving(query, acc_ref, peak_ref, keys, values, bias):
    raw = biased(scores(query, keys), bias)
    old = peak_ref[...]
    peak = jnp.maximum(old, jnp.max(raw, axis=1, keepdims=True))
    weights = jnp.exp2(raw - wide(peak, keys.shape[0])).astype(jnp.bfloat16)
    peak_ref[...] = peak
    acc_ref[...] = acc_ref[...] * wide(jnp.exp2(old - peak), 2 * HEAD) + dot(weights, values)


def absorb(heads, view, masked, steps, read):
    if masked is not None:

        @pl.loop(0, masked)
        def _(step):
            fixed(heads, view, *read(step, True))

    @pl.loop(0, steps)
    def _(step):
        fixed(heads, view, *read(step, False))


def absorb_again(acc_ref, view, start, tiles, read):
    largest = jnp.max(acc_ref[:, :, HEAD:])

    @pl.when(jnp.logical_not(largest < LIMIT))
    def _():
        @pl.loop(0, acc_ref.shape[0])
        def _(h):
            start(h)

            @pl.loop(0, tiles)
            def _(tile):
                moving(*view(h), *read(tile))


def tile_of(ref, start, size):
    rows = pl.ds(pl.multiple_of(start, TILE), size)
    return ref[rows, :HEAD], widened(ref[rows, HEAD:])


def head_view(q_ref, acc_ref, peak_ref):
    def view(h):
        columns = pl.ds(pl.multiple_of(h * HEAD, HEAD), HEAD)
        return q_ref[:, columns], acc_ref.at[h], peak_ref.at[h]

    return view


def bias_where(allowed):
    return jnp.where(allowed, 0.0, NEGATIVE)


def sums(state_ref):
    return state_ref.at[:, :, pl.ds(0, 2 * HEAD)], state_ref.at[:, :, pl.ds(2 * HEAD, HEAD)]


def own_row_kernel(
    place_ref, q_ref, k_ref, v_ref, row_a, row_b, below_a, above_b, state_ref, bank_ref, bias_ref,
    sems,
):
    y, z = place_ref[0] // WIDE, place_ref[0] % WIDE
    acc_ref, peak_ref = sums(state_ref)
    keys, half = z * KEEP, row_a.shape[0]
    row_steps = keys // STEP
    masked = (keys - row_steps * STEP + TILE - 1) // TILE
    copies = [
        (row_a, bank_ref.at[pl.ds(0, half)], z >= 0),
        (row_b, bank_ref.at[pl.ds(half, half)], z >= 0),
        (below_a, bank_ref.at[pl.ds(2 * half, half)], y > 0),
        (above_b, bank_ref.at[pl.ds(3 * half, half)], y == 3),
    ]
    copies = [
        (pltpu.make_async_copy(source, target, sems.at[at]), on)
        for at, (source, target, on) in enumerate(copies)
    ]
    for one, on in copies:
        pl.when(on)(one.start)
    view, heads = head_view(q_ref, acc_ref, peak_ref), acc_ref.shape[0]

    def start(h):
        query, acc, peak = view(h)
        local(query, k_ref[...], v_ref[...], acc, peak)

    def read_masked(tile):
        at = row_steps * STEP + tile * TILE
        bias_ref[...] = bias_where(count_along(bias_ref.shape, 1) + at < keys)
        return *tile_of(bank_ref, at, TILE), bias_ref[...]

    def step_start(step):
        return jnp.where(step < row_steps, step, step - row_steps + 2 * half // STEP) * STEP

    def read_fast(step, with_bias):
        if with_bias:
            return read_masked(step)
        for at, (one, on) in enumerate(copies[2:]):
            pl.when(on & (step == row_steps + at))(one.wait)
        return *tile_of(bank_ref, step_start(step), STEP), None

    def read(tile):
        after = jnp.maximum(tile - masked, 0)
        plain = step_start(after // 2) + after % 2 * TILE
        at = jnp.where(tile < masked, row_steps * STEP + tile * TILE, plain)
        limit = jnp.where(tile < masked, keys, bank_ref.shape[0])
        bias_ref[...] = bias_where(count_along(bias_ref.shape, 1) + at < limit)
        return *tile_of(bank_ref, at, TILE), bias_ref[...]

    for h in range(heads):
        start(h)
    for one, on in copies[:2]:
        pl.when(on)(one.wait)
    steps = row_steps + jnp.where(y == 3, 2, jnp.minimum(y, 1))
    absorb(heads, view, masked, steps, read_fast)
    absorb_again(acc_ref, view, start, masked + STEP // TILE * steps, read)


def more_keys(queries, rest_ref, state_in, refs, used, firsts, pieces, steps, then):
    acc_ref, peak_ref, q_ref, bank_ref, carried_ref, bias_ref, sems = refs
    acc_in, peak_in = sums(state_in)
    copies = [(queries, q_ref, True), (peak_in, peak_ref, True)]
    copies += [(ref.at[pl.ds(0, KEEP)], bank_ref.at[pl.ds(0, KEEP)], on) for ref, on in firsts]
    for at, (ref, on) in enumerate(pieces):
        copies.append((ref, bank_ref.at[pl.ds(TILE + at * STEP, STEP)], on))
    copies.append((acc_in, carried_ref, True))
    copies = [
        (pltpu.make_async_copy(source, target, sems.at[at]), on)
        for at, (source, target, on) in enumerate(copies)
    ]

    def under(condition, act):
        if condition is True:
            act()
        else:
            pl.when(condition)(act)

    for one, on in copies:
        under(on, one.start)
    then()
    acc_ref[...] = jnp.zeros(acc_ref.shape, jnp.float32)
    view, masked = head_view(q_ref, acc_ref, peak_ref), None
    if firsts:
        bank_ref[KEEP:TILE] = rest_ref[: TILE - KEEP]
        number = wide(rest_ref[TILE - KEEP : TILE - KEEP + 1, :HEAD].astype(jnp.int32), TILE)
        at = count_along((1, TILE), 1)
        limit = jnp.where(at < KEEP, number, KEEP + used - number)
        bias_ref[0] = jnp.broadcast_to(bias_where(at < limit), bias_ref.shape[1:])
        bias_ref[1] = jnp.zeros(bias_ref.shape[1:], jnp.float32)
        masked = sum(jnp.where(on, 1, 0) for _, on in firsts)

    def start(h):
        acc_ref[h] = carried_ref[h]

    def read(step):
        if masked is None:
            return *tile_of(bank_ref, TILE + step * TILE, TILE), None
        tile = jnp.where(masked > 0, step, step + 1)
        return *tile_of(bank_ref, tile * TILE, TILE), bias_ref[jnp.minimum(tile, 1)]

    here, later = copies[2 : 2 + len(firsts)], copies[2 + len(firsts) : -1]

    def read_fast(step, with_bias):
        if with_bias:
            for one, on in here:
                under(on, one.wait)
            return *tile_of(bank_ref, 0, TILE), bias_ref[0]
        for at, (one, on) in enumerate(later):
            pl.when(on & (step == at))(one.wait)
        return *tile_of(bank_ref, TILE + step * STEP, STEP), None

    for one, _ in copies[:2]:
        one.wait()
    absorb(acc_ref.shape[0], view, masked, steps, read_fast)
    copies[-1][0].wait()
    acc_ref[...] += carried_ref[...]
    tiles = STEP // TILE * steps + (0 if masked is None else masked)
    absorb_again(acc_ref, view, start, tiles, read)


def rest_kernel(
    place_ref, rest_ref, queries, first_ref, below_b, above_a, below2_ref, above2_ref, weight_ref, state_in,
    own_out, far_out, near_out, own_ref, send_ref, w_ref, att_ref, out_sems, *refs,
):
    mine, used = place_ref[0], place_ref[1]
    y = mine // WIDE
    pieces = (below_b, y > 0), (below2_ref, y > 1), (above2_ref, y > 1), (above_a, y == 3)
    firsts = (first_ref, (mine > 0) & (y < 2)), (below2_ref, y == 2), (above_a, y == 3)
    steps = jnp.where(y == 3, 4, jnp.where(y == 2, 3, y))
    weight_copy = pltpu.make_async_copy(weight_ref, w_ref, out_sems.at[3])
    more_keys(
        queries, rest_ref, state_in, refs, used, firsts, pieces, steps, weight_copy.start
    )
    acc_ref = refs[0]
    for h in range(acc_ref.shape[0]):
        att_ref[:, h * HEAD : (h + 1) * HEAD] = (
            acc_ref[h, :, :HEAD] / acc_ref[h, :, HEAD:]
        ).astype(jnp.bfloat16)
    weight_copy.wait()
    chips, _, columns = own_out.shape
    chip, core = place_ref[2], place_ref[3]

    @pl.loop(0, chips)
    def _(step):
        ahead = jnp.where(step == 0, 2, jnp.where(step == 1, 1, jnp.where(step == 2, 3, 0)))
        column = lax.rem(chip + ahead, chips) * 2
        for ref, side in ((own_ref, core), (send_ref, 1 - core)):
            start = pl.multiple_of((column + side) * columns, columns)
            ref[step] = dot(att_ref[...], w_ref[:, pl.ds(start, columns)]).astype(jnp.bfloat16)
        pltpu.make_async_copy(own_ref.at[step], own_out.at[step], out_sems.at[0]).start()

        @pl.when(step == 0)
        def _():
            pltpu.make_async_copy(send_ref.at[0], far_out, out_sems.at[1]).start()

        @pl.when(step > 0)
        def _():
            target = near_out.at[step - 1]
            pltpu.make_async_copy(send_ref.at[step], target, out_sems.at[2]).start()

    pltpu.make_async_copy(own_ref, own_out, out_sems.at[0]).wait()
    pltpu.make_async_copy(send_ref.at[0], far_out, out_sems.at[1]).wait()
    pltpu.make_async_copy(send_ref.at[pl.ds(1, chips - 1)], near_out, out_sems.at[2]).wait()


def pack_row_kernel(place_ref, *refs):
    z = place_ref[0] % WIDE
    at, middle = KEEP, WIDE * KEEP // 2
    for ref in refs[:-2]:
        rows = ref.shape[0]
        start = pl.multiple_of(lax.rem(z * KEEP + at, WIDE * KEEP), KEEP // 2)
        at += rows
        for out_ref, first in zip(refs[-2:], (0, middle)):

            @pl.when((start >= first) & (start < first + middle))
            def _():
                out_ref[pl.ds(pl.multiple_of(start - first, KEEP // 2), rows)] = ref[...]


def pack_row(place, pieces):
    return pl.pallas_call(
        pack_row_kernel,
        out_shape=[jax.ShapeDtypeStruct((WIDE * KEEP // 2, 2 * HEAD), jnp.bfloat16)] * 2,
        in_specs=[SMEM] + [VMEM] * len(pieces),
        out_specs=[VMEM] * 2,
        compiler_params=pltpu.CompilerParams(vmem_limit_bytes=8 * 2**20),
        name="pack_row",
    )(place, *pieces)


def cost(rows, keys):
    return pl.CostEstimate(
        flops=rows * keys * HEAD * 8, bytes_accessed=8 * 2**20, transcendentals=rows * keys
    )


def state_of(length, heads):
    return jax.ShapeDtypeStruct((heads, length, 3 * HEAD), jnp.float32)


def own_row(place, queries, keys, values, *pieces):
    length, width = queries.shape
    whole = lambda x: pl.BlockSpec(x.shape, lambda i: (0,) * len(x.shape))
    state = state_of(length, width // HEAD)
    return pl.pallas_call(
        own_row_kernel,
        grid=(1,),
        out_shape=state,
        in_specs=[SMEM, *[whole(x) for x in (queries, keys, values)], *[ANY] * len(pieces)],
        out_specs=whole(state),
        scratch_shapes=[
            pltpu.VMEM((4 * STEP, 2 * HEAD), jnp.bfloat16),
            pltpu.VMEM((8, TILE), jnp.float32),
            pltpu.SemaphoreType.DMA((4,)),
        ],
        compiler_params=PARAMS,
        cost_estimate=cost(length * width // HEAD, length + 4 * STEP),
        name="own_row",
    )(place, queries, keys, values, *pieces)


def rest_rows(place, queries, rest, banks, weight, state, chips):
    length, width = queries.shape
    heads, keys = width // HEAD, TILE + 4 * STEP
    whole = lambda x: pl.BlockSpec(x.shape, lambda i: (0,) * len(x.shape))
    one = (length, weight.shape[1] // chips // 2)
    shapes = (chips, *one), one, (chips - 1, *one)
    return pl.pallas_call(
        rest_kernel,
        grid=(1,),
        out_shape=[jax.ShapeDtypeStruct(shape, jnp.bfloat16) for shape in shapes],
        in_specs=[SMEM, whole(rest), *[ANY] * (len(banks) + 3)],
        out_specs=[ANY] * 3,
        scratch_shapes=[
            *[pltpu.VMEM((chips, *one), jnp.bfloat16)] * 2,
            pltpu.VMEM(weight.shape, weight.dtype),
            pltpu.VMEM((length, width), jnp.bfloat16),
            pltpu.SemaphoreType.DMA((4,)),
            pltpu.VMEM((heads, length, 2 * HEAD), jnp.float32),
            pltpu.VMEM((heads, length, HEAD), jnp.float32),
            pltpu.VMEM((length, width), jnp.bfloat16),
            pltpu.VMEM((keys, 2 * HEAD), jnp.bfloat16),
            pltpu.VMEM((heads, length, 2 * HEAD), jnp.float32),
            pltpu.VMEM((2, 8, TILE), jnp.float32),
            pltpu.SemaphoreType.DMA((10,)),
        ],
        compiler_params=pltpu.CompilerParams(vmem_limit_bytes=47 * 2**20),
        cost_estimate=cost(length * heads, keys),
        name="rest_rows",
    )(place, rest, queries, *banks, weight, state)


def summed(*refs):
    return sum(ref[...].astype(jnp.float32) for ref in refs)


def cross_kernel(own_ref, other_ref, upper_ref, lower_ref):
    total = summed(own_ref, other_ref).astype(jnp.bfloat16)
    half = upper_ref.shape[0]
    upper_ref[...] = total[:half]
    lower_ref[...] = total[half:]


def add_kernel(*refs):
    terms = refs[:-2]
    middle = len(terms) // 2
    refs[-2][...] = summed(*terms[:middle]).astype(jnp.bfloat16)
    refs[-1][...] = summed(*terms[middle:]).astype(jnp.bfloat16)


def halves_kernel(*refs):
    (*terms, upper_ref, lower_ref), out_ref = refs[:-1], refs[-1]
    half, total = upper_ref.shape[0], summed(*terms)
    out_ref[:half] = (total[:half] + summed(upper_ref)).astype(out_ref.dtype)
    out_ref[half:] = (total[half:] + summed(lower_ref)).astype(out_ref.dtype)


def small_call(kernel, name, terms, shapes, dtype=jnp.bfloat16):
    def spec(term):
        if not isinstance(term, tuple):
            return pl.BlockSpec(term.shape, lambda i: (0, 0))
        x, chunk, half = term
        rows = x.shape[1] // (1 if half is None else 2)
        return pl.BlockSpec((None, rows, x.shape[2]), lambda i: (chunk, half or 0, 0))

    return pl.pallas_call(
        kernel,
        grid=(1,),
        out_shape=[jax.ShapeDtypeStruct(shape, dtype) for shape in shapes],
        in_specs=[spec(term) for term in terms],
        out_specs=[pl.BlockSpec(shape, lambda i: (0, 0)) for shape in shapes],
        compiler_params=pltpu.CompilerParams(vmem_limit_bytes=8 * 2**20),
        name=name,
    )(*[term[0] if isinstance(term, tuple) else term for term in terms])


def on_device(queries, key_rows, value_rows, kept_positions, anchor_length, output_weight):
    mine, head = lax.axis_index("ctx"), lax.axis_index("head")
    length, devices, blocks = queries.shape[0], lax.axis_size("head"), lax.axis_size("ctx")
    chips, chip, core = devices // 2, head // 2, head % 2
    tall = blocks // WIDE
    swap = [(i, i ^ 1) for i in range(devices)]
    up = [(i, (i + 2) % devices) for i in range(devices)]
    down = [(i, (i - 2) % devices) for i in range(devices)]
    along = lambda step: [
        (r * WIDE + c, r * WIDE + (c + step) % WIDE) for r in range(tall) for c in range(WIDE)
    ]
    across = lambda hops: [(a * WIDE + c, b * WIDE + c) for a, b in hops for c in range(WIDE)]
    permute = lambda x, pairs: lax.ppermute(x, "ctx", pairs)

    spots = jnp.stack([chip, core]).astype(jnp.int32)
    place = jnp.concatenate([mine.astype(jnp.int32)[None], anchor_length, spots])
    kept, rest = select(anchor_length, kept_positions, key_rows, value_rows)

    plus, minus = along(1), along(-1)
    half = KEEP // 2
    left, right = [kept], [kept]
    rest = jnp.where(mine == 0, rest, jnp.zeros_like(rest))
    spread = lambda hops: [(r * WIDE + a, r * WIDE + b) for a, b in hops for r in range(tall)]
    upward = [(0, WIDE)], [(0, 3 * WIDE), (WIDE, 2 * WIDE)]
    for step in range(WIDE // 2 - 1):
        left.append(permute(left[-1], plus))
        right.append(permute(right[-1], minus))
        if step < len(upward):
            rest = rest + permute(rest, upward[step])
    opposite = [permute(left[-1][:half], plus), permute(right[-1][half:], minus)]
    ends = pack_row(place, right[1:] + opposite + left[:0:-1] + [kept])

    rest = rest + permute(rest, spread([(0, 2)]))
    rest, ends = lax.optimization_barrier((rest, ends))
    below_a = permute(ends[0], across([(0, 1), (1, 2), (2, 3)]))
    above_b = permute(ends[1], across([(0, 3), (1, 0)]))
    rest = rest + permute(rest, spread([(0, 6), (2, 4)]))
    rest, below_a, above_b, ends = lax.optimization_barrier((rest, below_a, above_b, ends))
    below_b = permute(ends[1], across([(0, 1), (1, 2), (2, 3)]))
    above_a = permute(ends[0], across([(0, 3)]))
    below2 = permute(below_a, across([(1, 2), (2, 3)]))
    above2 = permute(above_b, across([(0, 3), (3, 2)]))
    rest = rest + permute(rest, spread([(0, 1), (2, 3), (4, 5), (6, 7)]))
    state = own_row(place, queries, key_rows, value_rows, *ends, below_a, above_b)
    first = jnp.where(mine // WIDE == 1, below_a[:KEEP], ends[0][:KEEP])
    banks = (first, below_b, above_a, below2, above2)
    own, far, near = rest_rows(place, queries, rest, banks, output_weight, state, chips)

    far, near = lax.optimization_barrier((lax.ppermute(far, "head", swap), near))
    near = lax.ppermute(near, "head", swap)
    columns = own.shape[2]
    whole, half = (length, columns), (length // 2, columns)
    upper, lower = small_call(cross_kernel, "cross", [(own, 0, None), far], [half, half])
    upper, lower = lax.ppermute(upper, "head", up), lax.ppermute(lower, "head", down)
    terms = [(own, 1, 1), (near, 0, 1), (own, 2, 0), (near, 1, 0)]
    lower_up, upper_down = small_call(add_kernel, "direct", terms, [half, half])
    upper, lower, _, _ = lax.optimization_barrier((upper, lower, lower_up, upper_down))
    lower_up, upper_down = lax.ppermute(lower_up, "head", up), lax.ppermute(upper_down, "head", down)
    terms = [(own, 1, 0), (near, 0, 0), upper, (own, 2, 1), (near, 1, 1), lower]
    upper_up, lower_down = small_call(add_kernel, "turn", terms, [half, half])
    upper_up, lower_down = lax.ppermute(upper_up, "head", up), lax.ppermute(lower_down, "head", down)
    terms = [(own, 3, None), (near, 2, None), upper_down, lower_up]
    (total,) = small_call(halves_kernel, "collect", terms, [whole], jnp.float32)
    return small_call(halves_kernel, "finish", [total, upper_up, lower_down], [whole])[0]


def solution(mesh):
    placed = (
        P("ctx", "head"),
        P("ctx", "head"),
        P("ctx", "head"),
        P("head", "ctx"),
        P("head"),
        P("head", None),
    )
    return jax.shard_map(
        on_device, mesh=mesh, in_specs=placed, out_specs=P("ctx", "head"), check_vma=False
    )
```
